32 devices in a mesh: dp: 4 (over z), tm: 8 (over y, x, core).
Axes of the slice: x: 2, y: 2, z: 4, core: 2. Of those that a mesh axis runs over, the one named last changes fastest.
Arguments:
- frames_in: bfloat16 [4, 24, 8, 8, 320], P('dp', 'tm'), may hold values from -6 to 6
- cotangent: bfloat16 [4, 24, 8, 8, 320], P('dp', 'tm'), may hold values from -6 to 6
- counts: int32 [4, 8], P('dp'), may hold values from 1 to 3, 16 in all within a row
- norm_gain: float32 [320], replicated, may hold values from 0.5 to 1.5
- norm_shift: float32 [320], replicated, may hold values from -3 to 3
- spatial_weight: bfloat16 [2880, 320], replicated, may hold values from -0.109375 to 0.109375
- temporal_weight: bfloat16 [960, 320], replicated, may hold values from -0.1875 to 0.1875
Outputs:
- input_grad: bfloat16 [4, 24, 8, 8, 320], P('dp', 'tm')
- temporal_grad: float32 [960, 320], replicated
The draws below stay inside these ranges and needn't reach their ends.
Inputs may be any that keep to these rules, and one draw needn't show every extreme that they name: `counts`: each row sums to 16; in every row some index of tm holds exactly 3 frames.
All inputs are finite; a program needn't handle non-finite values.
Results may differ from the reference program's by a relative error of at most 0.006.
Values may be sent and summed in bfloat16 or wider, within the bound.
A program may use at most 64 MiB of HBM per device.

```python
import math
import jax
import jax.numpy as jnp
import numpy as np
from jax import lax

C = 320
GROUPS = 32
CAP = 3
WW = 8
HH = 8
FRAMES = 16
SLOTS = 24
VIDEOS = 4
N_TM = 8


def spiked(array, own_key, source, target, parts, factor):
    owner, partner = [(jnp.arange(array.shape[axis_at]) // (array.shape[axis_at] // parts)).reshape([-1 if axis == axis_at else 1 for axis in range(array.ndim)]) for axis_at in (source, target)]
    chosen = jax.random.permutation(own_key, parts)[partner]
    strong = (owner == chosen) | (owner == (partner + parts // 2) % parts)
    return jnp.where(strong, factor * array, array)


def block_levels(own_key, shape, cuts, least, top_value):
    def one(axis_at, shards_of):
        steps = jax.random.uniform(jax.random.fold_in(jax.random.fold_in(own_key, 6), axis_at), (shards_of,), jnp.float32, least / len(cuts), top_value / len(cuts))
        return jnp.repeat(jnp.exp(steps), shape[axis_at] // shards_of).reshape((-1,) + (1,) * (len(shape) - axis_at - 1))

    level = one(*cuts[0])
    for cut in cuts[1:]:
        level = level * one(*cut)
    return level


def profile(amount, total, reach, lean):
    weights = [(1 << 20) // math.isqrt(standing ** lean) + 1 for standing in range(2, amount + 1)]
    spare, given = total - reach - (amount - 1), [1] * (amount - 1)
    while spare > 0:
        free = [i for i in range(amount - 1) if given[i] < reach]
        mass, left = sum([weights[i] for i in free]), spare
        for i in free:
            extra = min(reach - given[i], max(1, left * weights[i] // mass), spare)
            given[i] = given[i] + extra
            spare = spare - extra
    return np.array([reach] + given)


def uneven_parts(rng, count, total, most, skew):
    if count == 2:
        one = jax.random.randint(rng, (), max(1, total - most), min(most, total - 1) + 1)
        return jnp.stack([one, total - one])
    sizes = jnp.asarray(profile(count, total, most, skew), jnp.int32)
    couples = (count - 1) // 2
    donor, receiver = sizes[1:1 + 2 * couples:2], sizes[2:2 + 2 * couples:2]
    slack = jnp.minimum(donor - 1, most - receiver)
    shifted = jax.random.randint(jax.random.fold_in(rng, 1), (couples,), 0, 1 << 20) % (slack + 1)
    sizes = sizes.at[1:1 + 2 * couples:2].set(donor - shifted).at[2:2 + 2 * couples:2].set(receiver + shifted)
    return sizes[jax.random.permutation(jax.random.fold_in(rng, 2), count)]


def gaussian(key, shape, scale, bound, split=(), held_as=jnp.bfloat16):
    values = scale * jax.random.normal(key, shape, jnp.float32)
    if split:
        values = values * block_levels(key, shape, split, -0.22, 0.18)
    return jnp.clip(values, -bound, bound).astype(held_as)


def noise_with(own_key, extent, scale, most, split, heavy, kind=jnp.bfloat16):
    values = scale * jax.random.normal(own_key, extent, jnp.float32)
    if split:
        values = values * block_levels(own_key, extent, split, -0.22, 0.18)
    return jnp.clip(spiked(values, jax.random.fold_in(own_key, 3), *heavy), -most, most).astype(kind)


def setup_inputs(seed: int = 0) -> dict:
    streams_of = jax.random.split(jax.random.key(seed), 8)
    return {
        "frames_in": gaussian(streams_of[0], (VIDEOS, SLOTS, HH, WW, C), 1.0, 6.0, ((0, 4), (1, 8))),
        "cotangent": noise_with(streams_of[1], (VIDEOS, SLOTS, HH, WW, C), 1.0, 6.0, ((0, 4), (1, 8)), (1, 4, 8, 2.0)),
        "counts": jax.vmap(lambda own: uneven_parts(own, N_TM, FRAMES, CAP, 0))(jax.random.split(streams_of[2], VIDEOS)).reshape((VIDEOS, N_TM)).astype(jnp.int32),
        "norm_gain": jnp.clip(1.0 + 0.1 * jax.random.normal(streams_of[3], (C,), jnp.float32), 0.5, 1.5),
        "norm_shift": gaussian(streams_of[4], (C,), 0.5, 3.0, (), jnp.float32),
        "spatial_weight": gaussian(streams_of[5], (9 * C, C), (9 * C) ** -0.5, 0.109375),
        "temporal_weight": gaussian(streams_of[6], (3 * C, C), (3 * C) ** -0.5, 0.1875),
    }


def norm_act(values, gain, shift, groups):
    nframes, height, width, channels = values.shape
    per_group = channels // groups
    entries = height * width * per_group

    def group_mean(totals):
        summed = totals.reshape(nframes, groups, per_group).sum(axis=2) / entries
        return jnp.repeat(summed, per_group, axis=1).reshape(nframes, 1, 1, channels)
    centre = group_mean(values.sum(axis=(1, 2)))
    centred = values - centre
    spread = group_mean((centred * centred).sum(axis=(1, 2)))
    normed = centred * lax.rsqrt(spread + 1e-05) * gain + shift
    return jax.nn.silu(normed)

def patches(field):
    height, width = (field.shape[1], field.shape[2])
    padded = jnp.pad(field, ((0, 0), (1, 1), (1, 1), (0, 0)))
    pieces = [padded[:, row_off:row_off + height, col_off:col_off + width, :] for row_off in range(3) for col_off in range(3)]
    return jnp.concatenate(pieces, axis=3)

def spatial_conv(field, weight):
    stacked = patches(field)
    leading = stacked.shape[:3]
    product = jnp.dot(stacked.reshape(-1, stacked.shape[3]), weight, preferred_element_type=jnp.float32)
    return product.reshape(leading + (weight.shape[1],))

def spatial_conv_t(field, weight):
    channels = weight.shape[1]
    flipped = weight.reshape(9, -1, channels)[::-1].transpose(0, 2, 1).reshape(-1, weight.shape[0] // 9)
    return spatial_conv(field, flipped)

def silu_grad(values):
    sigma = jax.nn.sigmoid(values)
    return sigma * (1.0 + values * (1.0 - sigma))

def temporal_core(y_ext, g_ext, weight):
    nframes = y_ext.shape[0] - 2
    channels = weight.shape[1]
    units = jax.nn.silu(y_ext.astype(jnp.float32)).astype(jnp.bfloat16)
    g_mid = g_ext[1:-1].reshape(-1, channels)
    grads = []
    back_sum = jnp.zeros((g_mid.shape[0], channels), jnp.float32)
    for tap_k in range(3):
        taken = units[tap_k:tap_k + nframes].reshape(-1, channels)
        grads.append(lax.dot_general(taken, g_mid, (((0,), (0,)), ((), ())), preferred_element_type=jnp.float32))
        tap_weight = weight[tap_k * channels:(tap_k + 1) * channels]
        source = g_ext[2 - tap_k:2 - tap_k + nframes].reshape(-1, channels)
        back_sum = back_sum + lax.dot_general(source, tap_weight, (((1,), (1,)), ((), ())), preferred_element_type=jnp.float32)
    middle = y_ext[1:-1]
    back_t = (silu_grad(middle.astype(jnp.float32)) * back_sum.reshape(middle.shape)).astype(jnp.bfloat16)
    return (back_t, jnp.concatenate(grads, axis=0))

def frame_slots(counts_row, nframes, cap):
    ndevices = counts_row.shape[0]
    ends = jnp.cumsum(counts_row).astype(jnp.int32)
    starts = ends - counts_row
    frame_ids = jnp.arange(nframes, dtype=jnp.int32)
    owner = lax.optimization_barrier(jnp.sum((ends[None, :] <= frame_ids[:, None]).astype(jnp.int32), axis=1))
    device_ids = jnp.arange(ndevices, dtype=jnp.int32)
    first = lax.optimization_barrier(jnp.sum(jnp.where(device_ids[None, :] == owner[:, None], starts[None, :], 0), axis=1))
    return (owner * cap + frame_ids - first).astype(jnp.int32)

def slot_frames(counts_row, cap):
    ndevices = counts_row.shape[0]
    ends = jnp.cumsum(counts_row).astype(jnp.int32)
    starts = ends - counts_row
    slot_ids = jnp.arange(ndevices * cap, dtype=jnp.int32)
    device = slot_ids // cap
    inner = slot_ids % cap
    device_ids = jnp.arange(ndevices, dtype=jnp.int32)
    onehot = device[:, None] == device_ids[None, :]
    held = lax.optimization_barrier(jnp.sum(jnp.where(onehot, counts_row[None, :], 0), axis=1))
    first = lax.optimization_barrier(jnp.sum(jnp.where(onehot, starts[None, :], 0), axis=1))
    live = inner < held
    return (jnp.where(live, first + inner, 0).astype(jnp.int32), live)

def reference(frames_in, cotangent, counts, norm_gain, norm_shift, spatial_weight, temporal_weight):

    def one_video(members):
        slot_inputs, slot_cotan, counts_row = members
        pick = frame_slots(counts_row, FRAMES, CAP)
        inputs = jnp.take(slot_inputs, pick, axis=0)
        cotan = jnp.take(slot_cotan, pick, axis=0)

        def activate(values):
            return norm_act(values, norm_gain, norm_shift, GROUPS)
        inputs_f = inputs.astype(jnp.float32)
        act_f, act_back = jax.vjp(activate, inputs_f)
        acts = act_f.astype(jnp.bfloat16)
        mixed = spatial_conv(acts, spatial_weight)
        y_out = (inputs_f + mixed).astype(jnp.bfloat16)
        pad_spec = ((1, 1), (0, 0), (0, 0), (0, 0))
        back_t, grad_part = temporal_core(jnp.pad(y_out, pad_spec), jnp.pad(cotan, pad_spec), temporal_weight)
        d_out = (cotan.astype(jnp.float32) + back_t.astype(jnp.float32)).astype(jnp.bfloat16)
        d_act = spatial_conv_t(d_out, spatial_weight)
        d_in = (d_out.astype(jnp.float32) + act_back(d_act)[0]).astype(jnp.bfloat16)
        back_idx, live = slot_frames(counts_row, CAP)
        d_slots = jnp.where(live[:, None, None, None], jnp.take(d_in, back_idx, axis=0), jnp.zeros((), jnp.bfloat16))
        return (d_slots.astype(jnp.bfloat16), grad_part)
    input_grad, grads = lax.map(one_video, (frames_in, cotangent, counts))
    scale = 1.0 / math.sqrt(VIDEOS * FRAMES * HH * WW)
    temporal_grad = lax.optimization_barrier(jnp.sum(grads, axis=0)) * scale
    return (input_grad, temporal_grad)
```

```python
import math

import jax
import jax.numpy as jnp
from jax import lax
from jax.experimental import pallas as pl
from jax.experimental.pallas import tpu as pltpu
from jax.sharding import PartitionSpec as P

GROUPS = 32


def norm_act(values, gain, shift, groups):
    nframes, height, width, channels = values.shape
    per_group = channels // groups
    entries = height * width * per_group

    def group_mean(totals):
        summed = totals.reshape(nframes, groups, per_group).sum(axis=2) / entries
        return jnp.repeat(summed, per_group, axis=1).reshape(nframes, 1, 1, channels)

    centre = group_mean(values.sum(axis=(1, 2)))
    centred = values - centre
    spread = group_mean((centred * centred).sum(axis=(1, 2)))
    normed = centred * lax.rsqrt(spread + 1e-05) * gain + shift
    return jax.nn.silu(normed)


def patches(field):
    height, width = (field.shape[1], field.shape[2])
    padded = jnp.pad(field, ((0, 0), (1, 1), (1, 1), (0, 0)))
    pieces = [
        padded[:, row_off : row_off + height, col_off : col_off + width, :]
        for row_off in range(3)
        for col_off in range(3)
    ]
    return jnp.concatenate(pieces, axis=3)


def spatial_conv(field, weight):
    stacked = patches(field)
    leading = stacked.shape[:3]
    product = jnp.dot(
        stacked.reshape(-1, stacked.shape[3]), weight, preferred_element_type=jnp.float32
    )
    return product.reshape(leading + (weight.shape[1],))


def spatial_conv_t(field, weight):
    channels = weight.shape[1]
    flipped = (
        weight.reshape(9, -1, channels)[::-1].transpose(0, 2, 1).reshape(-1, weight.shape[0] // 9)
    )
    return spatial_conv(field, flipped)


def silu_grad(values):
    sigma = jax.nn.sigmoid(values)
    return sigma * (1.0 + values * (1.0 - sigma))


def temporal_core(y_ext, g_ext, weight):
    nframes = y_ext.shape[0] - 2
    channels = weight.shape[1]
    units = jax.nn.silu(y_ext.astype(jnp.float32)).astype(jnp.bfloat16)
    g_middle = g_ext[1:-1]
    g_mid = g_middle.reshape(-1, channels)
    grads = []
    back_sum = jnp.zeros((g_mid.shape[0], channels), jnp.float32)
    for tap_k in range(3):
        taken = units[tap_k : tap_k + nframes].reshape(-1, channels)
        grads.append(
            lax.dot_general(
                taken, g_mid, (((0,), (0,)), ((), ())), preferred_element_type=jnp.float32
            )
        )
        tap_weight = weight[tap_k * channels : (tap_k + 1) * channels]
        source = g_ext[2 - tap_k : 2 - tap_k + nframes].reshape(-1, channels)
        back_sum = back_sum + lax.dot_general(
            source, tap_weight, (((1,), (1,)), ((), ())), preferred_element_type=jnp.float32
        )
    middle = y_ext[1:-1]
    back_t = (silu_grad(middle.astype(jnp.float32)) * back_sum.reshape(middle.shape)).astype(
        jnp.bfloat16
    )
    return (back_t, jnp.concatenate(grads, axis=0))


def frame_slots(counts_row, nframes, cap):
    ndevices = counts_row.shape[0]
    ends = jnp.cumsum(counts_row)
    starts = ends - counts_row
    frame_ids = jnp.arange(nframes, dtype=jnp.int32)
    owner = jnp.sum((ends[None, :] <= frame_ids[:, None]).astype(jnp.int32), axis=1)
    device_ids = jnp.arange(ndevices, dtype=jnp.int32)
    first = jnp.sum(jnp.where(device_ids[None, :] == owner[:, None], starts[None, :], 0), axis=1)
    return owner * cap + frame_ids - first


def slot_frames(counts_row, cap):
    ndevices = counts_row.shape[0]
    ends = jnp.cumsum(counts_row)
    starts = ends - counts_row
    slot_ids = jnp.arange(ndevices * cap, dtype=jnp.int32)
    device = slot_ids // cap
    inner = slot_ids % cap
    device_ids = jnp.arange(ndevices, dtype=jnp.int32)
    onehot = device[:, None] == device_ids[None, :]
    held = jnp.sum(jnp.where(onehot, counts_row[None, :], 0), axis=1)
    first = jnp.sum(jnp.where(onehot, starts[None, :], 0), axis=1)
    live = inner < held
    return (jnp.where(live, first + inner, 0), live)


def shards(frames_in, cotangent, counts, norm_gain, norm_shift, spatial_weight, temporal_weight):
    inputs = frames_in[0]
    cotan = cotangent[0]
    counts_row = counts[0]
    cap = inputs.shape[0]
    tm_size = lax.axis_size("tm")
    own_count = jnp.sum(
        jnp.where(jnp.arange(tm_size, dtype=jnp.int32) == lax.axis_index("tm"), counts_row, 0)
    )
    live_slots = (jnp.arange(cap, dtype=jnp.int32) < own_count)[:, None, None, None]

    def activate(values):
        return norm_act(values, norm_gain, norm_shift, GROUPS)

    inputs_f = inputs.astype(jnp.float32)
    act_f, act_back = jax.vjp(activate, inputs_f)
    acts = act_f.astype(jnp.bfloat16)
    mixed = spatial_conv(acts, spatial_weight)
    y_out = (inputs_f + mixed).astype(jnp.bfloat16)
    y_rows, g_rows = (
        lax.all_to_all(y_out, "tm", split_axis=1, concat_axis=0, tiled=True),
        lax.all_to_all(cotan, "tm", split_axis=1, concat_axis=0, tiled=True),
    )
    pick = frame_slots(counts_row, 2 * tm_size, cap)
    pad_spec = ((1, 1), (0, 0), (0, 0), (0, 0))
    y_ext = jnp.pad(jnp.take(y_rows, pick, axis=0), pad_spec)
    g_ext = jnp.pad(jnp.take(g_rows, pick, axis=0), pad_spec)
    back_rows, grad_part = temporal_core(y_ext, g_ext, temporal_weight)
    back_idx, live = slot_frames(counts_row, cap)
    back_slots = jnp.where(
        live[:, None, None, None],
        jnp.take(back_rows, back_idx, axis=0),
        jnp.zeros((), jnp.bfloat16),
    )
    back_t = lax.all_to_all(back_slots, "tm", split_axis=0, concat_axis=1, tiled=True)
    d_out = (cotan.astype(jnp.float32) + back_t.astype(jnp.float32)).astype(jnp.bfloat16)
    d_act = spatial_conv_t(d_out, spatial_weight)
    d_in = d_out.astype(jnp.float32) + act_back(d_act)[0]
    d_in = jnp.where(live_slots, d_in, 0.0).astype(jnp.bfloat16)
    height, width = (inputs.shape[1], inputs.shape[2])
    scale = 1.0 / math.sqrt(lax.axis_size("dp") * 2 * tm_size * height * width)
    summed = lax.psum(grad_part, ("dp", "tm"))
    return (d_in[None], summed * scale)


CAP = 3
SIDE = 8
CH = 320
PIX = SIDE * SIDE
ROWS = CAP * PIX
LANE = 128
UNITS = 8
BLOCK = 80
CHUNKS = 32
F32 = jnp.float32
BF16 = jnp.bfloat16


def dot(a, b, ca, cb):
    return lax.dot_general(a, b, (((ca,), (cb,)), ((), ())), preferred_element_type=F32)


def group_matrix():
    def ids(axis):
        index = lax.broadcasted_iota(jnp.int32, (CH, CH), axis).astype(F32)
        return jnp.floor((index + 0.5) * (GROUPS / CH))

    return (ids(0) == ids(1)).astype(BF16)


def group_means(totals, members):
    rows = jnp.concatenate(totals, axis=0)
    high = rows.astype(BF16)
    rest = rows - high.astype(F32)
    mid = rest.astype(BF16)
    low = (rest - mid.astype(F32)).astype(BF16)
    summed = dot(high, members, 1, 0) + dot(mid, members, 1, 0) + dot(low, members, 1, 0)
    return summed * (1.0 / (PIX * (CH // GROUPS)))


def frame_of(value, frame):
    return value[frame * PIX : (frame + 1) * PIX]


def column_sum(value):
    return jnp.sum(value, axis=0, keepdims=True)


def sigmoid(value):
    return 1.0 / (1.0 + jnp.exp(-value))


def stage_shifts(value, line, padded):
    column = lax.broadcasted_iota(jnp.int32, (ROWS, CH), 0) % SIDE
    line[8 : 8 + ROWS, :] = value
    left = jnp.where(column == 0, 0.0, line[7 : 7 + ROWS, :])
    right = jnp.where(column == SIDE - 1, 0.0, line[9 : 9 + ROWS, :])
    for j, moved in enumerate((left, value, right)):
        padded[j, :, 1 : 1 + SIDE] = moved.reshape(CAP, SIDE, SIDE, CH)


def shifted(padded, j, i):
    return padded[j, :, i : i + SIDE].reshape(ROWS, CH).astype(BF16)


def fused_kernel(
    counts, x_ref, g_ref, gain_ref, shift_ref, ws_hbm, wt_hbm, out_ref, grad_ref,
    ws, wt, line, padded, edge, halo, part, part16, from_core, quad16, from_plane, own16, from_z, full,
    weight_sem, halo_send, halo_recv, core_sem, plane_send, plane_recv, z_send, z_recv,
    gather_send, gather_z, gather_plane, gather_core,
):
    dp = lax.axis_index("dp")
    tm = lax.axis_index("tm")
    yy, xx, core = tm // 4, (tm // 2) % 2, tm % 2
    chip = tm // 2

    def at(z, chip_id, core_id):
        return (z, chip_id * 2 + core_id)

    plane = [yy * 2 + (1 - xx), (1 - yy) * 2 + xx, (1 - yy) * 2 + (1 - xx)]
    z_to = [lax.rem(dp + d, 4) for d in (1, 2, 3)]
    z_from = [lax.rem(dp + 4 - d, 4) for d in (1, 2, 3)]
    before, after = lax.rem(tm + 7, 8), lax.rem(tm + 1, 8)
    partner = at(dp, chip, 1 - core)
    peers = [(dp, before), (dp, after)] + [at(dp, p, core) for p in plane] + [at(z, chip, core) for z in z_to]

    def remote(src, dst, send_sem, recv_sem, device):
        copy = pltpu.make_async_remote_copy(
            src_ref=src, dst_ref=dst, send_sem=send_sem, recv_sem=recv_sem,
            device_id=device, device_id_type=pl.DeviceIdType.MESH,
        )
        return copy

    barrier = pltpu.get_barrier_semaphore()
    for peer in peers:
        pl.semaphore_signal(barrier, inc=1, device_id=peer, device_id_type=pl.DeviceIdType.MESH)
    load_s = pltpu.make_async_copy(ws_hbm, ws, weight_sem.at[0])
    load_t = pltpu.make_async_copy(wt_hbm, wt, weight_sem.at[1])
    load_s.start()
    load_t.start()

    count = counts[0, tm]
    g16 = g_ref[...]
    g = g16.astype(F32)
    g_frames = [frame_of(g, s) for s in range(CAP)]
    last = jnp.where(count == 3, g_frames[2], jnp.where(count == 2, g_frames[1], g_frames[0]))
    edge[0] = g_frames[0].astype(BF16)
    edge[1] = last.astype(BF16)
    pl.semaphore_wait(barrier, len(peers))
    halo_copies = [
        remote(edge.at[0], halo.at[1], halo_send.at[0], halo_recv.at[1], (dp, before)),
        remote(edge.at[1], halo.at[0], halo_send.at[1], halo_recv.at[0], (dp, after)),
    ]
    for copy in halo_copies:
        copy.start()

    members = group_matrix()
    gain, shift = gain_ref[...], shift_ref[...]
    x = x_ref[...].astype(F32)
    x_frames = [frame_of(x, s) for s in range(CAP)]
    means = group_means([column_sum(v) for v in x_frames], members)
    centred = [v - means[s : s + 1] for s, v in enumerate(x_frames)]
    spread = group_means([column_sum(v * v) for v in centred], members)
    inverse = lax.rsqrt(spread + 1e-05)
    xhat = jnp.concatenate([v * inverse[s : s + 1] for s, v in enumerate(centred)], axis=0)
    normed = xhat * gain + shift
    sig_n = sigmoid(normed)
    padded[...] = jnp.zeros_like(padded)
    stage_shifts(normed * sig_n, line, padded)

    load_s.wait()
    mixed = jnp.zeros((ROWS, CH), F32)
    for tap in range(9):
        mixed = mixed + dot(shifted(padded, tap % 3, tap // 3), ws[:, tap * CH : (tap + 1) * CH], 1, 1)
    y = (x + mixed).astype(BF16).astype(F32)
    sig_y = sigmoid(y)
    slot = lax.broadcasted_iota(jnp.int32, (ROWS, CH), 0) // PIX
    live = slot < count
    u = jnp.where(live, y * sig_y, 0.0).astype(BF16)

    for copy in halo_copies:
        copy.wait()
    prev_edge = jnp.where(tm == 0, 0.0, halo[0].astype(F32))
    next_edge = jnp.where(tm == 7, 0.0, halo[1].astype(F32))
    g_prev = jnp.concatenate([prev_edge, g_frames[0], g_frames[1]], axis=0).astype(BF16)
    g_next = jnp.concatenate(
        [
            jnp.where(count == 1, next_edge, g_frames[1]),
            jnp.where(count == 2, next_edge, g_frames[2]),
            next_edge,
        ],
        axis=0,
    ).astype(BF16)
    taps = (g_next, g16, g_prev)

    none = jnp.zeros((ROWS, 64), BF16)
    u_low = jnp.concatenate([u, none], axis=1)
    u_high = jnp.concatenate([none, u], axis=1)
    t0 = dot(taps[0], u_low, 0, 0)
    t1 = dot(taps[1], u_high, 0, 0)
    t2 = dot(taps[2], u_low, 0, 0)
    units = [
        t0[:, 0:128], t0[:, 128:256], t0[:, 256:384] + t1[:, 0:128], t1[:, 128:256], t1[:, 256:384],
        t2[:, 0:128], t2[:, 128:256], t2[:, 256:384],
    ]
    for r in range(4):
        for l in range(UNITS):
            piece = units[l][r * BLOCK : (r + 1) * BLOCK]
            part[r * UNITS + l] = piece
            part16[r * UNITS + l] = piece.astype(BF16)

    core_copy = remote(part16.at[pl.ds((1 - core) * 16, 16)], from_core, core_sem.at[0], core_sem.at[1], partner)
    core_copy.start()

    load_t.wait()
    du = jnp.zeros((ROWS, CH), F32)
    for k in range(3):
        du = du + dot(taps[k], wt[:, k * CH : (k + 1) * CH], 1, 0)
    back_t = (sig_y * (1.0 + y * (1.0 - sig_y)) * du).astype(BF16).astype(F32)
    dy = jnp.where(live, (g + back_t).astype(BF16).astype(F32), 0.0)

    core_copy.wait()
    quad = part[pl.ds(core * 16, 16)] + from_core[...].astype(F32)
    part[pl.ds(core * 16, 16)] = quad
    quad16[...] = quad.astype(BF16)
    plane_copies = [
        remote(quad16.at[pl.ds(p * 4, 4)], from_plane.at[d], plane_send.at[d], plane_recv.at[d], at(dp, p, core))
        for d, p in enumerate(plane)
    ]
    for copy in plane_copies:
        copy.start()

    stage_shifts(dy, line, padded)
    da = jnp.zeros((ROWS, CH), F32)
    for tap in range(9):
        da = da + dot(shifted(padded, 2 - tap % 3, 2 - tap // 3), ws[:, tap * CH : (tap + 1) * CH], 1, 0)

    for copy in plane_copies:
        copy.wait()
    first = core * 16 + chip * 4
    four = part[pl.ds(first, 4)] + from_plane[0].astype(F32) + from_plane[1].astype(F32) + from_plane[2].astype(F32)
    part[pl.ds(first, 4)] = four
    own16[...] = four.astype(BF16)
    z_copies = [
        remote(own16.at[z], from_z.at[d], z_send.at[d], z_recv.at[d], at(z, chip, core))
        for d, z in enumerate(z_to)
    ]
    for copy in z_copies:
        copy.start()

    dhat = da * (sig_n * (1.0 + normed * (1.0 - sig_n))) * gain
    dhat_frames = [frame_of(dhat, s) for s in range(CAP)]
    xhat_frames = [frame_of(xhat, s) for s in range(CAP)]
    mean_d = group_means([column_sum(v) for v in dhat_frames], members)
    mean_dx = group_means([column_sum(v * w) for v, w in zip(dhat_frames, xhat_frames)], members)
    dx = jnp.concatenate(
        [
            inverse[s : s + 1] * (dhat_frames[s] - mean_d[s : s + 1] - xhat_frames[s] * mean_dx[s : s + 1])
            for s in range(CAP)
        ],
        axis=0,
    )
    out_ref[...] = jnp.where(live, dy + dx, 0.0).astype(BF16)

    for copy in z_copies:
        copy.wait()
    mine = first + dp
    total = part[mine] + from_z[0].astype(F32) + from_z[1].astype(F32) + from_z[2].astype(F32)
    full[mine] = total.astype(BF16)

    sent = []

    def pass_on(chunk, sem_id, device, recv_sem):
        copy = remote(full.at[chunk], full.at[chunk], gather_send.at[sem_id], recv_sem, device)
        copy.start()
        sent.append(copy)

    for d, z in enumerate(z_to):
        pass_on(mine, d, at(z, chip, core), gather_z.at[d])
    for d, p in enumerate(plane):
        pass_on(mine, 3 + d, at(dp, p, core), gather_plane.at[d])
    pass_on(mine, 6, partner, gather_core.at[0])
    for k, z in enumerate(z_from):
        chunk = first + z
        remote(full.at[chunk], full.at[chunk], gather_send.at[0], gather_z.at[k], partner).wait_recv()
        for d, p in enumerate(plane):
            pass_on(chunk, 7 + k * 4 + d, at(dp, p, core), gather_plane.at[(k + 1) * 3 + d])
        pass_on(chunk, 7 + k * 4 + 3, partner, gather_core.at[k + 1])
    sem_id = 19
    for k, z in enumerate([dp] + z_from):
        for d, p in enumerate(plane):
            chunk = core * 16 + p * 4 + z
            remote(full.at[chunk], full.at[chunk], gather_send.at[0], gather_plane.at[k * 3 + d], partner).wait_recv()
            pass_on(chunk, sem_id, partner, gather_core.at[4 + k * 3 + d])
            sem_id = sem_id + 1
    others = [chip] + plane
    for k, z in enumerate([dp] + z_from):
        for d, p in enumerate(others):
            chunk = (1 - core) * 16 + p * 4 + z
            slot_id = k if d == 0 else 4 + k * 3 + d - 1
            remote(full.at[chunk], full.at[chunk], gather_send.at[0], gather_core.at[slot_id], partner).wait_recv()
    for copy in sent:
        copy.wait_send()

    scale = 1.0 / math.sqrt(4 * 2 * 8 * PIX)
    for r in range(4):
        for l in range(UNITS):
            width = min(LANE, 3 * CH - l * LANE)
            value = full[r * UNITS + l].astype(F32) * scale
            grad_ref[r * BLOCK : (r + 1) * BLOCK, l * LANE : l * LANE + width] = value[:, :width]


def fused_shards(frames_in, cotangent, counts, norm_gain, norm_shift, spatial_weight, temporal_weight):
    vmem = pl.BlockSpec(memory_space=pltpu.VMEM)
    hbm = pl.BlockSpec(memory_space=pl.ANY)
    dma = pltpu.SemaphoreType.DMA
    out, grad = pl.pallas_call(
        fused_kernel,
        out_shape=(
            jax.ShapeDtypeStruct((ROWS, CH), BF16),
            jax.ShapeDtypeStruct((CH, 3 * CH), F32),
        ),
        in_specs=[pl.BlockSpec(memory_space=pltpu.SMEM), vmem, vmem, vmem, vmem, hbm, hbm],
        out_specs=(vmem, vmem),
        scratch_shapes=[
            pltpu.VMEM((CH, 9 * CH), BF16),
            pltpu.VMEM((CH, 3 * CH), BF16),
            pltpu.VMEM((ROWS + 16, CH), F32),
            pltpu.VMEM((3, CAP, SIDE + 2, SIDE, CH), F32),
            pltpu.VMEM((2, PIX, CH), BF16),
            pltpu.VMEM((2, PIX, CH), BF16),
            pltpu.VMEM((CHUNKS, BLOCK, LANE), F32),
            pltpu.VMEM((CHUNKS, BLOCK, LANE), BF16),
            pltpu.VMEM((16, BLOCK, LANE), BF16),
            pltpu.VMEM((16, BLOCK, LANE), BF16),
            pltpu.VMEM((3, 4, BLOCK, LANE), BF16),
            pltpu.VMEM((4, BLOCK, LANE), BF16),
            pltpu.VMEM((3, BLOCK, LANE), BF16),
            pltpu.VMEM((CHUNKS, BLOCK, LANE), BF16),
            dma((2,)), dma((2,)), dma((2,)), dma((2,)), dma((3,)), dma((3,)), dma((3,)), dma((3,)),
            dma((31,)), dma((3,)), dma((12,)), dma((16,)),
        ],
        compiler_params=pltpu.CompilerParams(
            collective_id=0, has_side_effects=True, vmem_limit_bytes=40 * 1024 * 1024
        ),
    )(
        counts,
        frames_in.reshape(ROWS, CH),
        cotangent.reshape(ROWS, CH),
        norm_gain.reshape(1, CH),
        norm_shift.reshape(1, CH),
        spatial_weight.T,
        temporal_weight.T,
    )
    return out.reshape(frames_in.shape), grad.T


def solution(mesh):
    fused = mesh.shape["dp"] == 4 and mesh.shape["tm"] == 8

    def block(frames_in, *rest):
        if fused and frames_in.shape == (1, CAP, SIDE, SIDE, CH):
            return fused_shards(frames_in, *rest)
        return shards(frames_in, *rest)

    return jax.shard_map(
        block,
        mesh=mesh,
        in_specs=(
            P("dp", "tm", None, None, None),
            P("dp", "tm", None, None, None),
            P("dp", None),
            P(),
            P(),
            P(),
            P(),
        ),
        out_specs=(P("dp", "tm", None, None, None), P()),
        check_vma=False,
    )
```

```python
import math

import jax
import jax.numpy as jnp
from jax import lax
from jax.experimental import pallas as pl
from jax.experimental.pallas import tpu as pltpu
from jax.sharding import PartitionSpec as P

GROUPS = 32


def norm_act(values, gain, shift, groups):
    nframes, height, width, channels = values.shape
    per_group = channels // groups
    entries = height * width * per_group

    def group_mean(totals):
        summed = totals.reshape(nframes, groups, per_group).sum(axis=2) / entries
        return jnp.repeat(summed, per_group, axis=1).reshape(nframes, 1, 1, channels)

    centre = group_mean(values.sum(axis=(1, 2)))
    centred = values - centre
    spread = group_mean((centred * centred).sum(axis=(1, 2)))
    normed = centred * lax.rsqrt(spread + 1e-05) * gain + shift
    return jax.nn.silu(normed)


def patches(field):
    height, width = (field.shape[1], field.shape[2])
    padded = jnp.pad(field, ((0, 0), (1, 1), (1, 1), (0, 0)))
    pieces = [
        padded[:, row_off : row_off + height, col_off : col_off + width, :]
        for row_off in range(3)
        for col_off in range(3)
    ]
    return jnp.concatenate(pieces, axis=3)


def spatial_conv(field, weight):
    stacked = patches(field)
    leading = stacked.shape[:3]
    product = jnp.dot(
        stacked.reshape(-1, stacked.shape[3]), weight, preferred_element_type=jnp.float32
    )
    return product.reshape(leading + (weight.shape[1],))


def spatial_conv_t(field, weight):
    channels = weight.shape[1]
    flipped = (
        weight.reshape(9, -1, channels)[::-1].transpose(0, 2, 1).reshape(-1, weight.shape[0] // 9)
    )
    return spatial_conv(field, flipped)


def silu_grad(values):
    sigma = jax.nn.sigmoid(values)
    return sigma * (1.0 + values * (1.0 - sigma))


def temporal_core(y_ext, g_ext, weight):
    nframes = y_ext.shape[0] - 2
    channels = weight.shape[1]
    units = jax.nn.silu(y_ext.astype(jnp.float32)).astype(jnp.bfloat16)
    g_middle = g_ext[1:-1]
    g_mid = g_middle.reshape(-1, channels)
    grads = []
    back_sum = jnp.zeros((g_mid.shape[0], channels), jnp.float32)
    for tap_k in range(3):
        taken = units[tap_k : tap_k + nframes].reshape(-1, channels)
        grads.append(
            lax.dot_general(
                taken, g_mid, (((0,), (0,)), ((), ())), preferred_element_type=jnp.float32
            )
        )
        tap_weight = weight[tap_k * channels : (tap_k + 1) * channels]
        source = g_ext[2 - tap_k : 2 - tap_k + nframes].reshape(-1, channels)
        back_sum = back_sum + lax.dot_general(
            source, tap_weight, (((1,), (1,)), ((), ())), preferred_element_type=jnp.float32
        )
    middle = y_ext[1:-1]
    back_t = (silu_grad(middle.astype(jnp.float32)) * back_sum.reshape(middle.shape)).astype(
        jnp.bfloat16
    )
    return (back_t, jnp.concatenate(grads, axis=0))


def frame_slots(counts_row, nframes, cap):
    ndevices = counts_row.shape[0]
    ends = jnp.cumsum(counts_row)
    starts = ends - counts_row
    frame_ids = jnp.arange(nframes, dtype=jnp.int32)
    owner = jnp.sum((ends[None, :] <= frame_ids[:, None]).astype(jnp.int32), axis=1)
    device_ids = jnp.arange(ndevices, dtype=jnp.int32)
    first = jnp.sum(jnp.where(device_ids[None, :] == owner[:, None], starts[None, :], 0), axis=1)
    return owner * cap + frame_ids - first


def slot_frames(counts_row, cap):
    ndevices = counts_row.shape[0]
    ends = jnp.cumsum(counts_row)
    starts = ends - counts_row
    slot_ids = jnp.arange(ndevices * cap, dtype=jnp.int32)
    device = slot_ids // cap
    inner = slot_ids % cap
    device_ids = jnp.arange(ndevices, dtype=jnp.int32)
    onehot = device[:, None] == device_ids[None, :]
    held = jnp.sum(jnp.where(onehot, counts_row[None, :], 0), axis=1)
    first = jnp.sum(jnp.where(onehot, starts[None, :], 0), axis=1)
    live = inner < held
    return (jnp.where(live, first + inner, 0), live)


def shards(frames_in, cotangent, counts, norm_gain, norm_shift, spatial_weight, temporal_weight):
    inputs = frames_in[0]
    cotan = cotangent[0]
    counts_row = counts[0]
    cap = inputs.shape[0]
    tm_size = lax.axis_size("tm")
    own_count = jnp.sum(
        jnp.where(jnp.arange(tm_size, dtype=jnp.int32) == lax.axis_index("tm"), counts_row, 0)
    )
    live_slots = (jnp.arange(cap, dtype=jnp.int32) < own_count)[:, None, None, None]

    def activate(values):
        return norm_act(values, norm_gain, norm_shift, GROUPS)

    inputs_f = inputs.astype(jnp.float32)
    act_f, act_back = jax.vjp(activate, inputs_f)
    acts = act_f.astype(jnp.bfloat16)
    mixed = spatial_conv(acts, spatial_weight)
    y_out = (inputs_f + mixed).astype(jnp.bfloat16)
    y_rows, g_rows = (
        lax.all_to_all(y_out, "tm", split_axis=1, concat_axis=0, tiled=True),
        lax.all_to_all(cotan, "tm", split_axis=1, concat_axis=0, tiled=True),
    )
    pick = frame_slots(counts_row, 2 * tm_size, cap)
    pad_spec = ((1, 1), (0, 0), (0, 0), (0, 0))
    y_ext = jnp.pad(jnp.take(y_rows, pick, axis=0), pad_spec)
    g_ext = jnp.pad(jnp.take(g_rows, pick, axis=0), pad_spec)
    back_rows, grad_part = temporal_core(y_ext, g_ext, temporal_weight)
    back_idx, live = slot_frames(counts_row, cap)
    back_slots = jnp.where(
        live[:, None, None, None],
        jnp.take(back_rows, back_idx, axis=0),
        jnp.zeros((), jnp.bfloat16),
    )
    back_t = lax.all_to_all(back_slots, "tm", split_axis=0, concat_axis=1, tiled=True)
    d_out = (cotan.astype(jnp.float32) + back_t.astype(jnp.float32)).astype(jnp.bfloat16)
    d_act = spatial_conv_t(d_out, spatial_weight)
    d_in = d_out.astype(jnp.float32) + act_back(d_act)[0]
    d_in = jnp.where(live_slots, d_in, 0.0).astype(jnp.bfloat16)
    height, width = (inputs.shape[1], inputs.shape[2])
    scale = 1.0 / math.sqrt(lax.axis_size("dp") * 2 * tm_size * height * width)
    summed = lax.psum(grad_part, ("dp", "tm"))
    return (d_in[None], summed * scale)


CAP = 3
SIDE = 8
CH = 320
PIX = SIDE * SIDE
ROWS = CAP * PIX
LANE = 128
UNITS = 8
BLOCK = 80
CHUNKS = 32
F32 = jnp.float32
BF16 = jnp.bfloat16


def dot(a, b, ca, cb):
    return lax.dot_general(a, b, (((ca,), (cb,)), ((), ())), preferred_element_type=F32)


def group_matrix():
    def ids(axis):
        index = lax.broadcasted_iota(jnp.int32, (CH, CH), axis).astype(F32)
        return jnp.floor((index + 0.5) * (GROUPS / CH))

    return (ids(0) == ids(1)).astype(BF16)


def group_means(totals, members):
    rows = jnp.concatenate(totals, axis=0)
    high = rows.astype(BF16)
    rest = rows - high.astype(F32)
    mid = rest.astype(BF16)
    low = (rest - mid.astype(F32)).astype(BF16)
    summed = dot(high, members, 1, 0) + dot(mid, members, 1, 0) + dot(low, members, 1, 0)
    return summed * (1.0 / (PIX * (CH // GROUPS)))


def frame_of(value, frame):
    return value[frame * PIX : (frame + 1) * PIX]


def column_sum(value):
    return jnp.sum(value, axis=0, keepdims=True)


def sigmoid(value):
    return 1.0 / (1.0 + jnp.exp(-value))


def stage_shifts(value, line, padded):
    column = lax.broadcasted_iota(jnp.int32, (ROWS, CH), 0) % SIDE
    line[8 : 8 + ROWS, :] = value
    left = jnp.where(column == 0, 0.0, line[7 : 7 + ROWS, :])
    right = jnp.where(column == SIDE - 1, 0.0, line[9 : 9 + ROWS, :])
    for j, moved in enumerate((left, value, right)):
        padded[j, :, 1 : 1 + SIDE] = moved.reshape(CAP, SIDE, SIDE, CH)


def shifted(padded, j, i):
    return padded[j, :, i : i + SIDE].reshape(ROWS, CH).astype(BF16)


def fused_kernel(
    counts_hbm, x_hbm, g_hbm, gain_hbm, shift_hbm, ws_hbm, wt_hbm, out_ref, grad_ref,
    counts, x_ref, g_ref, gain_ref, shift_ref, ws, wt, line, padded, edge, halo, part, part16, from_core, quad16, from_plane, own, own16, from_z, full,
    weight_sem, halo_send, halo_recv, core_send, core_recv, plane_send, plane_recv, z_send, z_recv,
    gather_send, gather_z, gather_plane, gather_core,
):
    dp = lax.axis_index("dp")
    tm = lax.axis_index("tm")
    yy, xx, core = tm // 4, (tm // 2) % 2, tm % 2
    chip = tm // 2

    def at(z, chip_id, core_id):
        return (z, chip_id * 2 + core_id)

    plane = [yy * 2 + (1 - xx), (1 - yy) * 2 + xx, (1 - yy) * 2 + (1 - xx)]
    z_to = [lax.rem(dp + d, 4) for d in (1, 2, 3)]
    z_from = [lax.rem(dp + 4 - d, 4) for d in (1, 2, 3)]
    before, after = lax.rem(tm + 7, 8), lax.rem(tm + 1, 8)
    partner = at(dp, chip, 1 - core)
    peers = [(dp, before), (dp, after)] + [at(dp, p, core) for p in plane] + [at(z, chip, core) for z in z_to]

    def remote(src, dst, send_sem, recv_sem, device):
        copy = pltpu.make_async_remote_copy(
            src_ref=src, dst_ref=dst, send_sem=send_sem, recv_sem=recv_sem,
            device_id=device, device_id_type=pl.DeviceIdType.MESH,
        )
        return copy

    barrier = pltpu.get_barrier_semaphore()
    for peer in peers:
        pl.semaphore_signal(barrier, inc=1, device_id=peer, device_id_type=pl.DeviceIdType.MESH)
    places = [
        (g_hbm, g_ref), (counts_hbm, counts), (x_hbm, x_ref), (gain_hbm, gain_ref), (shift_hbm, shift_ref),
        (ws_hbm, ws), (wt_hbm, wt),
    ]
    loads = [pltpu.make_async_copy(src, dst, weight_sem.at[i]) for i, (src, dst) in enumerate(places)]
    for load in loads:
        load.start()
    members = group_matrix()
    for load in loads[:2]:
        load.wait()

    count = counts[0, tm]
    g = g_ref[...].astype(F32)
    g_frames = [frame_of(g, s) for s in range(CAP)]
    last = jnp.where(count == 3, g_frames[2], jnp.where(count == 2, g_frames[1], g_frames[0]))
    edge[0] = g_frames[0].astype(BF16)
    edge[1] = last.astype(BF16)
    halo_copies = [
        remote(edge.at[0], halo.at[1], halo_send.at[0], halo_recv.at[1], (dp, before)),
        remote(edge.at[1], halo.at[0], halo_send.at[1], halo_recv.at[0], (dp, after)),
    ]
    for load in loads[2:5]:
        load.wait()

    gain, shift = gain_ref[...].reshape(1, CH), shift_ref[...].reshape(1, CH)
    x = x_ref[...].astype(F32)
    x_frames = [frame_of(x, s) for s in range(CAP)]
    means = group_means([column_sum(v) for v in x_frames], members)
    centred = [v - means[s : s + 1] for s, v in enumerate(x_frames)]
    spread = group_means([column_sum(v * v) for v in centred], members)
    inverse = lax.rsqrt(spread + 1e-05)
    xhat = jnp.concatenate([v * inverse[s : s + 1] for s, v in enumerate(centred)], axis=0)
    normed = xhat * gain + shift
    sig_n = sigmoid(normed)
    padded[...] = jnp.zeros_like(padded)
    stage_shifts(normed * sig_n, line, padded)

    pl.semaphore_wait(barrier, len(peers))
    for copy in halo_copies:
        copy.start()
    loads[5].wait()
    mixed = jnp.zeros((ROWS, CH), F32)
    for tap in range(9):
        mixed = mixed + dot(shifted(padded, tap % 3, tap // 3), ws[:, tap * CH : (tap + 1) * CH], 1, 1)
    y = (x + mixed).astype(BF16).astype(F32)
    sig_y = sigmoid(y)
    slot = lax.broadcasted_iota(jnp.int32, (ROWS, CH), 0) // PIX
    live = slot < count
    u = jnp.where(live, y * sig_y, 0.0).astype(BF16)

    for copy in halo_copies:
        copy.wait()
    prev_edge = jnp.where(tm == 0, 0.0, halo[0].astype(F32))
    next_edge = jnp.where(tm == 7, 0.0, halo[1].astype(F32))
    g_ext = jnp.concatenate(
        [
            prev_edge,
            g_frames[0],
            jnp.where(count == 1, next_edge, g_frames[1]),
            jnp.where(count == 2, next_edge, g_frames[2]),
            next_edge,
        ],
        axis=0,
    )

    g_turned = g_ext.T.astype(BF16)
    g_ext = g_ext.astype(BF16)
    none = jnp.zeros((ROWS, 64), BF16)
    u_low = jnp.concatenate([u, none], axis=1)
    u_high = jnp.concatenate([none, u], axis=1)

    def below(value, frames):
        zero = jnp.zeros((PIX, value.shape[1]), BF16)
        return jnp.concatenate([zero] * frames + [value] + [zero] * (2 - frames), axis=0)

    t0 = dot(g_turned, below(u_low, 2), 1, 0)
    t1 = dot(g_turned, below(u_high, 1), 1, 0)
    t2 = dot(g_turned, below(u_low, 0), 1, 0)
    units = [
        t0[:, 0:128], t0[:, 128:256], t0[:, 256:384] + t1[:, 0:128], t1[:, 128:256], t1[:, 256:384],
        t2[:, 0:128], t2[:, 128:256], t2[:, 256:384],
    ]
    for r in range(4):
        for l in range(UNITS):
            piece = units[l][r * BLOCK : (r + 1) * BLOCK]
            part[r * UNITS + l] = piece
            part16[r * UNITS + l] = piece.astype(BF16)

    groups = plane + [chip]
    core_copies = [
        remote(
            part16.at[pl.ds((1 - core) * 16 + p * 4, 4)], from_core.at[pl.ds(p * 4, 4)],
            core_send.at[j], core_recv.at[j], partner,
        )
        for j, p in enumerate(groups)
    ]
    for copy in core_copies:
        copy.start()

    loads[6].wait()
    du = jnp.zeros((ROWS, CH), F32)
    for k in range(3):
        du = du + dot(g_ext[(2 - k) * PIX : (2 - k) * PIX + ROWS], wt[:, k * CH : (k + 1) * CH], 1, 0)
    back_t = (sig_y * (1.0 + y * (1.0 - sig_y)) * du).astype(BF16).astype(F32)
    dy = jnp.where(live, (g + back_t).astype(BF16).astype(F32), 0.0)

    z_order = z_to + [dp]
    plane_copies = []
    for j, p in enumerate(groups):
        core_copies[j].wait()
        quad = part[pl.ds(core * 16 + p * 4, 4)] + from_core[pl.ds(p * 4, 4)].astype(F32)
        if j == 3:
            own[...] = quad
            continue
        quad16[j] = quad.astype(BF16)
        for k, z in enumerate(z_order):
            i = j * 4 + k
            copy = remote(quad16.at[j, z], from_plane.at[j, k], plane_send.at[i], plane_recv.at[i], at(dp, p, core))
            copy.start()
            plane_copies.append(copy)

    stage_shifts(dy, line, padded)
    da = jnp.zeros((ROWS, CH), F32)
    for tap in range(9):
        da = da + dot(shifted(padded, 2 - tap % 3, 2 - tap // 3), ws[:, tap * CH : (tap + 1) * CH], 1, 0)

    z_copies = []
    for k, z in enumerate(z_order):
        for j in range(3):
            plane_copies[j * 4 + k].wait()
        four = own[z] + from_plane[0, k].astype(F32) + from_plane[1, k].astype(F32) + from_plane[2, k].astype(F32)
        if k == 3:
            total = four
            continue
        own16[k] = four.astype(BF16)
        copy = remote(own16.at[k], from_z.at[k], z_send.at[k], z_recv.at[k], at(z, chip, core))
        copy.start()
        z_copies.append(copy)

    dhat = da * (sig_n * (1.0 + normed * (1.0 - sig_n))) * gain
    dhat_frames = [frame_of(dhat, s) for s in range(CAP)]
    xhat_frames = [frame_of(xhat, s) for s in range(CAP)]
    mean_d = group_means([column_sum(v) for v in dhat_frames], members)
    mean_dx = group_means([column_sum(v * w) for v, w in zip(dhat_frames, xhat_frames)], members)
    dx = jnp.concatenate(
        [
            inverse[s : s + 1] * (dhat_frames[s] - mean_d[s : s + 1] - xhat_frames[s] * mean_dx[s : s + 1])
            for s in range(CAP)
        ],
        axis=0,
    )
    out_ref[...] = jnp.where(live, dy + dx, 0.0).astype(BF16)

    for copy in z_copies:
        copy.wait()
    first = core * 16 + chip * 4
    mine = first + dp
    total = total + from_z[0].astype(F32) + from_z[1].astype(F32) + from_z[2].astype(F32)
    full[mine] = total.astype(BF16)

    sent = []

    def pass_on(chunk, sem_id, device, recv_sem):
        copy = remote(full.at[chunk], full.at[chunk], gather_send.at[sem_id], recv_sem, device)
        copy.start()
        sent.append(copy)

    for d, z in enumerate(z_to):
        pass_on(mine, d, at(z, chip, core), gather_z.at[d])
    for d, p in enumerate(plane):
        pass_on(mine, 3 + d, at(dp, p, core), gather_plane.at[d])
    pass_on(mine, 6, partner, gather_core.at[0])
    for k, z in enumerate(z_from):
        chunk = first + z
        remote(full.at[chunk], full.at[chunk], gather_send.at[0], gather_z.at[k], partner).wait_recv()
        for d, p in enumerate(plane):
            pass_on(chunk, 7 + k * 4 + d, at(dp, p, core), gather_plane.at[(k + 1) * 3 + d])
        pass_on(chunk, 7 + k * 4 + 3, partner, gather_core.at[k + 1])
    sem_id = 19
    for k, z in enumerate([dp] + z_from):
        for d, p in enumerate(plane):
            chunk = core * 16 + p * 4 + z
            remote(full.at[chunk], full.at[chunk], gather_send.at[0], gather_plane.at[k * 3 + d], partner).wait_recv()
            pass_on(chunk, sem_id, partner, gather_core.at[4 + k * 3 + d])
            sem_id = sem_id + 1
    others = [chip] + plane
    for k, z in enumerate([dp] + z_from):
        for d, p in enumerate(others):
            chunk = (1 - core) * 16 + p * 4 + z
            slot_id = k if d == 0 else 4 + k * 3 + d - 1
            remote(full.at[chunk], full.at[chunk], gather_send.at[0], gather_core.at[slot_id], partner).wait_recv()
    for copy in sent:
        copy.wait_send()

    scale = 1.0 / math.sqrt(4 * 2 * 8 * PIX)
    for r in range(4):
        for l in range(UNITS):
            width = min(LANE, 3 * CH - l * LANE)
            value = full[r * UNITS + l].astype(F32) * scale
            grad_ref[r * BLOCK : (r + 1) * BLOCK, l * LANE : l * LANE + width] = value[:, :width]


def fused_shards(frames_in, cotangent, counts, norm_gain, norm_shift, spatial_weight, temporal_weight):
    vmem = pl.BlockSpec(memory_space=pltpu.VMEM)
    hbm = pl.BlockSpec(memory_space=pltpu.HBM)
    dma = pltpu.SemaphoreType.DMA
    out, grad = pl.pallas_call(
        fused_kernel,
        out_shape=(
            jax.ShapeDtypeStruct((ROWS, CH), BF16),
            jax.ShapeDtypeStruct((CH, 3 * CH), F32),
        ),
        in_specs=[hbm] * 7,
        out_specs=(vmem, vmem),
        scratch_shapes=[
            pltpu.SMEM((1, 8), jnp.int32),
            pltpu.VMEM((ROWS, CH), BF16),
            pltpu.VMEM((ROWS, CH), BF16),
            pltpu.VMEM((CH,), F32),
            pltpu.VMEM((CH,), F32),
            pltpu.VMEM((CH, 9 * CH), BF16),
            pltpu.VMEM((CH, 3 * CH), BF16),
            pltpu.VMEM((ROWS + 16, CH), F32),
            pltpu.VMEM((3, CAP, SIDE + 2, SIDE, CH), F32),
            pltpu.VMEM((2, PIX, CH), BF16),
            pltpu.VMEM((2, PIX, CH), BF16),
            pltpu.VMEM((CHUNKS, BLOCK, LANE), F32),
            pltpu.VMEM((CHUNKS, BLOCK, LANE), BF16),
            pltpu.VMEM((16, BLOCK, LANE), BF16),
            pltpu.VMEM((3, 4, BLOCK, LANE), BF16),
            pltpu.VMEM((3, 4, BLOCK, LANE), BF16),
            pltpu.VMEM((4, BLOCK, LANE), F32),
            pltpu.VMEM((3, BLOCK, LANE), BF16),
            pltpu.VMEM((3, BLOCK, LANE), BF16),
            pltpu.VMEM((CHUNKS, BLOCK, LANE), BF16),
            dma((7,)), dma((2,)), dma((2,)), dma((4,)), dma((4,)), dma((12,)), dma((12,)), dma((3,)), dma((3,)),
            dma((31,)), dma((3,)), dma((12,)), dma((16,)),
        ],
        compiler_params=pltpu.CompilerParams(
            collective_id=0, has_side_effects=True, vmem_limit_bytes=60 * 1024 * 1024
        ),
    )(
        counts,
        frames_in.reshape(ROWS, CH),
        cotangent.reshape(ROWS, CH),
        norm_gain,
        norm_shift,
        spatial_weight.T,
        temporal_weight.T,
    )
    return out.reshape(frames_in.shape), grad.T


def solution(mesh):
    fused = mesh.shape["dp"] == 4 and mesh.shape["tm"] == 8

    def block(frames_in, *rest):
        if fused and frames_in.shape == (1, CAP, SIDE, SIDE, CH):
            return fused_shards(frames_in, *rest)
        return shards(frames_in, *rest)

    return jax.shard_map(
        block,
        mesh=mesh,
        in_specs=(
            P("dp", "tm", None, None, None),
            P("dp", "tm", None, None, None),
            P("dp", None),
            P(),
            P(),
            P(),
            P(),
        ),
        out_specs=(P("dp", "tm", None, None, None), P()),
        check_vma=False,
    )
```

```python
import math

import jax
import jax.numpy as jnp
from jax import lax
from jax.experimental import pallas as pl
from jax.experimental.pallas import tpu as pltpu
from jax.sharding import PartitionSpec as P

GROUPS = 32


def norm_act(values, gain, shift, groups):
    nframes, height, width, channels = values.shape
    per_group = channels // groups
    entries = height * width * per_group

    def group_mean(totals):
        summed = totals.reshape(nframes, groups, per_group).sum(axis=2) / entries
        return jnp.repeat(summed, per_group, axis=1).reshape(nframes, 1, 1, channels)

    centre = group_mean(values.sum(axis=(1, 2)))
    centred = values - centre
    spread = group_mean((centred * centred).sum(axis=(1, 2)))
    normed = centred * lax.rsqrt(spread + 1e-05) * gain + shift
    return jax.nn.silu(normed)


def patches(field):
    height, width = (field.shape[1], field.shape[2])
    padded = jnp.pad(field, ((0, 0), (1, 1), (1, 1), (0, 0)))
    pieces = [
        padded[:, row_off : row_off + height, col_off : col_off + width, :]
        for row_off in range(3)
        for col_off in range(3)
    ]
    return jnp.concatenate(pieces, axis=3)


def spatial_conv(field, weight):
    stacked = patches(field)
    leading = stacked.shape[:3]
    product = jnp.dot(
        stacked.reshape(-1, stacked.shape[3]), weight, preferred_element_type=jnp.float32
    )
    return product.reshape(leading + (weight.shape[1],))


def spatial_conv_t(field, weight):
    channels = weight.shape[1]
    flipped = (
        weight.reshape(9, -1, channels)[::-1].transpose(0, 2, 1).reshape(-1, weight.shape[0] // 9)
    )
    return spatial_conv(field, flipped)


def silu_grad(values):
    sigma = jax.nn.sigmoid(values)
    return sigma * (1.0 + values * (1.0 - sigma))


def temporal_core(y_ext, g_ext, weight):
    nframes = y_ext.shape[0] - 2
    channels = weight.shape[1]
    units = jax.nn.silu(y_ext.astype(jnp.float32)).astype(jnp.bfloat16)
    g_middle = g_ext[1:-1]
    g_mid = g_middle.reshape(-1, channels)
    grads = []
    back_sum = jnp.zeros((g_mid.shape[0], channels), jnp.float32)
    for tap_k in range(3):
        taken = units[tap_k : tap_k + nframes].reshape(-1, channels)
        grads.append(
            lax.dot_general(
                taken, g_mid, (((0,), (0,)), ((), ())), preferred_element_type=jnp.float32
            )
        )
        tap_weight = weight[tap_k * channels : (tap_k + 1) * channels]
        source = g_ext[2 - tap_k : 2 - tap_k + nframes].reshape(-1, channels)
        back_sum = back_sum + lax.dot_general(
            source, tap_weight, (((1,), (1,)), ((), ())), preferred_element_type=jnp.float32
        )
    middle = y_ext[1:-1]
    back_t = (silu_grad(middle.astype(jnp.float32)) * back_sum.reshape(middle.shape)).astype(
        jnp.bfloat16
    )
    return (back_t, jnp.concatenate(grads, axis=0))


def frame_slots(counts_row, nframes, cap):
    ndevices = counts_row.shape[0]
    ends = jnp.cumsum(counts_row)
    starts = ends - counts_row
    frame_ids = jnp.arange(nframes, dtype=jnp.int32)
    owner = jnp.sum((ends[None, :] <= frame_ids[:, None]).astype(jnp.int32), axis=1)
    device_ids = jnp.arange(ndevices, dtype=jnp.int32)
    first = jnp.sum(jnp.where(device_ids[None, :] == owner[:, None], starts[None, :], 0), axis=1)
    return owner * cap + frame_ids - first


def slot_frames(counts_row, cap):
    ndevices = counts_row.shape[0]
    ends = jnp.cumsum(counts_row)
    starts = ends - counts_row
    slot_ids = jnp.arange(ndevices * cap, dtype=jnp.int32)
    device = slot_ids // cap
    inner = slot_ids % cap
    device_ids = jnp.arange(ndevices, dtype=jnp.int32)
    onehot = device[:, None] == device_ids[None, :]
    held = jnp.sum(jnp.where(onehot, counts_row[None, :], 0), axis=1)
    first = jnp.sum(jnp.where(onehot, starts[None, :], 0), axis=1)
    live = inner < held
    return (jnp.where(live, first + inner, 0), live)


def shards(frames_in, cotangent, counts, norm_gain, norm_shift, spatial_weight, temporal_weight):
    inputs = frames_in[0]
    cotan = cotangent[0]
    counts_row = counts[0]
    cap = inputs.shape[0]
    tm_size = lax.axis_size("tm")
    own_count = jnp.sum(
        jnp.where(jnp.arange(tm_size, dtype=jnp.int32) == lax.axis_index("tm"), counts_row, 0)
    )
    live_slots = (jnp.arange(cap, dtype=jnp.int32) < own_count)[:, None, None, None]

    def activate(values):
        return norm_act(values, norm_gain, norm_shift, GROUPS)

    inputs_f = inputs.astype(jnp.float32)
    act_f, act_back = jax.vjp(activate, inputs_f)
    acts = act_f.astype(jnp.bfloat16)
    mixed = spatial_conv(acts, spatial_weight)
    y_out = (inputs_f + mixed).astype(jnp.bfloat16)
    y_rows, g_rows = (
        lax.all_to_all(y_out, "tm", split_axis=1, concat_axis=0, tiled=True),
        lax.all_to_all(cotan, "tm", split_axis=1, concat_axis=0, tiled=True),
    )
    pick = frame_slots(counts_row, 2 * tm_size, cap)
    pad_spec = ((1, 1), (0, 0), (0, 0), (0, 0))
    y_ext = jnp.pad(jnp.take(y_rows, pick, axis=0), pad_spec)
    g_ext = jnp.pad(jnp.take(g_rows, pick, axis=0), pad_spec)
    back_rows, grad_part = temporal_core(y_ext, g_ext, temporal_weight)
    back_idx, live = slot_frames(counts_row, cap)
    back_slots = jnp.where(
        live[:, None, None, None],
        jnp.take(back_rows, back_idx, axis=0),
        jnp.zeros((), jnp.bfloat16),
    )
    back_t = lax.all_to_all(back_slots, "tm", split_axis=0, concat_axis=1, tiled=True)
    d_out = (cotan.astype(jnp.float32) + back_t.astype(jnp.float32)).astype(jnp.bfloat16)
    d_act = spatial_conv_t(d_out, spatial_weight)
    d_in = d_out.astype(jnp.float32) + act_back(d_act)[0]
    d_in = jnp.where(live_slots, d_in, 0.0).astype(jnp.bfloat16)
    height, width = (inputs.shape[1], inputs.shape[2])
    scale = 1.0 / math.sqrt(lax.axis_size("dp") * 2 * tm_size * height * width)
    summed = lax.psum(grad_part, ("dp", "tm"))
    return (d_in[None], summed * scale)


CAP = 3
SIDE = 8
CH = 320
PIX = SIDE * SIDE
ROWS = CAP * PIX
LANE = 128
UNITS = 8
BLOCK = 80
CHUNKS = 32
F32 = jnp.float32
BF16 = jnp.bfloat16


def dot(a, b, ca, cb):
    return lax.dot_general(a, b, (((ca,), (cb,)), ((), ())), preferred_element_type=F32)


def group_matrix():
    def ids(axis):
        index = lax.broadcasted_iota(jnp.int32, (CH, CH), axis).astype(F32)
        return jnp.floor((index + 0.5) * (GROUPS / CH))

    return (ids(0) == ids(1)).astype(BF16)


def group_means(totals, members):
    rows = jnp.concatenate(totals, axis=0)
    high = rows.astype(BF16)
    rest = rows - high.astype(F32)
    mid = rest.astype(BF16)
    low = (rest - mid.astype(F32)).astype(BF16)
    summed = dot(high, members, 1, 0) + dot(mid, members, 1, 0) + dot(low, members, 1, 0)
    return summed * (1.0 / (PIX * (CH // GROUPS)))


def frame_of(value, frame):
    return value[frame * PIX : (frame + 1) * PIX]


def column_sum(value):
    return jnp.sum(value, axis=0, keepdims=True)


def sigmoid(value):
    return 1.0 / (1.0 + jnp.exp(-value))


def stage_shifts(value, line, padded):
    column = lax.broadcasted_iota(jnp.int32, (ROWS, CH), 0) % SIDE
    line[8 : 8 + ROWS, :] = value
    left = jnp.where(column == 0, 0.0, line[7 : 7 + ROWS, :])
    right = jnp.where(column == SIDE - 1, 0.0, line[9 : 9 + ROWS, :])
    for j, moved in enumerate((left, value, right)):
        padded[j, :, 1 : 1 + SIDE] = moved.reshape(CAP, SIDE, SIDE, CH)


def turned_patches(value):
    wide = jnp.concatenate([value, jnp.zeros((64, CH), F32)], axis=0).T
    pixel = lax.broadcasted_iota(jnp.int32, wide.shape, 1)
    row, column = (pixel // SIDE) % SIDE, pixel % SIDE
    pieces = []
    for i in (-1, 0, 1):
        for j in (-1, 0, 1):
            move = (-(i * SIDE + j)) % wide.shape[1]
            moved = pltpu.roll(wide, move, 1) if move else wide
            inside = (row + i >= 0) & (row + i < SIDE) & (column + j >= 0) & (column + j < SIDE)
            pieces.append(jnp.where(inside, moved, 0.0).astype(BF16))
    return jnp.concatenate(pieces, axis=0)


def shifted(padded, j, i):
    return padded[j, :, i : i + SIDE].reshape(ROWS, CH).astype(BF16)


def fused_kernel(
    counts_hbm, x_hbm, g_hbm, gain_hbm, shift_hbm, ws_hbm, wt_hbm, out_ref, grad_ref,
    counts, x_ref, g_ref, gain_ref, shift_ref, ws, wt, line, padded, edge, halo, part, part16, from_core, quad16, from_plane, own, own16, from_z, full,
    weight_sem, halo_send, halo_recv, core_send, core_recv, plane_send, plane_recv, z_send, z_recv,
    gather_send, gather_z, gather_plane, gather_core,
):
    dp = lax.axis_index("dp")
    tm = lax.axis_index("tm")
    yy, xx, core = tm // 4, (tm // 2) % 2, tm % 2
    chip = tm // 2

    def at(z, chip_id, core_id):
        return (z, chip_id * 2 + core_id)

    plane = [yy * 2 + (1 - xx), (1 - yy) * 2 + xx, (1 - yy) * 2 + (1 - xx)]
    near = [dp + 1 - 2 * (dp % 2), 2 - dp // 2, 3 - 3 * (dp // 2)]
    far = near[::-1]
    before, after = lax.rem(tm + 7, 8), lax.rem(tm + 1, 8)
    partner = at(dp, chip, 1 - core)
    peers = [(dp, before), (dp, after)] + [at(dp, p, core) for p in plane] + [at(z, chip, core) for z in near]

    def remote(src, dst, send_sem, recv_sem, device):
        copy = pltpu.make_async_remote_copy(
            src_ref=src, dst_ref=dst, send_sem=send_sem, recv_sem=recv_sem,
            device_id=device, device_id_type=pl.DeviceIdType.MESH,
        )
        return copy

    barrier = pltpu.get_barrier_semaphore()
    for peer in peers:
        pl.semaphore_signal(barrier, inc=1, device_id=peer, device_id_type=pl.DeviceIdType.MESH)
    places = [
        (g_hbm, g_ref), (counts_hbm, counts), (x_hbm, x_ref), (gain_hbm, gain_ref), (shift_hbm, shift_ref),
        (ws_hbm, ws), (wt_hbm, wt),
    ]
    loads = [pltpu.make_async_copy(src, dst, weight_sem.at[i]) for i, (src, dst) in enumerate(places)]
    for load in loads:
        load.start()
    members = group_matrix()
    for load in loads[:2]:
        load.wait()

    count = counts[0, tm]
    g = g_ref[...].astype(F32)
    g_frames = [frame_of(g, s) for s in range(CAP)]
    last = jnp.where(count == 3, g_frames[2], jnp.where(count == 2, g_frames[1], g_frames[0]))
    edge[0] = g_frames[0].astype(BF16)
    edge[1] = last.astype(BF16)
    halo_copies = [
        remote(edge.at[0], halo.at[1], halo_send.at[0], halo_recv.at[1], (dp, before)),
        remote(edge.at[1], halo.at[0], halo_send.at[1], halo_recv.at[0], (dp, after)),
    ]
    for load in loads[2:5]:
        load.wait()

    gain, shift = gain_ref[...].reshape(1, CH), shift_ref[...].reshape(1, CH)
    x = x_ref[...].astype(F32)
    x_frames = [frame_of(x, s) for s in range(CAP)]
    means = group_means([column_sum(v) for v in x_frames], members)
    centred = [v - means[s : s + 1] for s, v in enumerate(x_frames)]
    spread = group_means([column_sum(v * v) for v in centred], members)
    inverse = lax.rsqrt(spread + 1e-05)
    xhat = jnp.concatenate([v * inverse[s : s + 1] for s, v in enumerate(centred)], axis=0)
    normed = xhat * gain + shift
    sig_n = sigmoid(normed)
    padded[...] = jnp.zeros_like(padded)
    pl.semaphore_wait(barrier, len(peers))
    for copy in halo_copies:
        copy.start()
    patched = turned_patches(normed * sig_n)
    loads[5].wait()
    mixed = dot(ws[...], patched, 1, 0).T[:ROWS]
    y = (x + mixed).astype(BF16).astype(F32)
    sig_y = sigmoid(y)
    slot = lax.broadcasted_iota(jnp.int32, (ROWS, CH), 0) // PIX
    live = slot < count
    u = jnp.where(live, y * sig_y, 0.0).astype(BF16)

    for copy in halo_copies:
        copy.wait()
    prev_edge = jnp.where(tm == 0, 0.0, halo[0].astype(F32))
    next_edge = jnp.where(tm == 7, 0.0, halo[1].astype(F32))
    g_ext = jnp.concatenate(
        [
            prev_edge,
            g_frames[0],
            jnp.where(count == 1, next_edge, g_frames[1]),
            jnp.where(count == 2, next_edge, g_frames[2]),
            next_edge,
        ],
        axis=0,
    )

    g_turned = g_ext.T.astype(BF16)
    g_ext = g_ext.astype(BF16)
    none = jnp.zeros((ROWS, 64), BF16)
    u_low = jnp.concatenate([u, none], axis=1)
    u_high = jnp.concatenate([none, u], axis=1)

    def below(value, frames):
        zero = jnp.zeros((PIX, value.shape[1]), BF16)
        return jnp.concatenate([zero] * frames + [value] + [zero] * (2 - frames), axis=0)

    t0 = dot(g_turned, below(u_low, 2), 1, 0)
    t1 = dot(g_turned, below(u_high, 1), 1, 0)
    t2 = dot(g_turned, below(u_low, 0), 1, 0)
    units = [
        t0[:, 0:128], t0[:, 128:256], t0[:, 256:384] + t1[:, 0:128], t1[:, 128:256], t1[:, 256:384],
        t2[:, 0:128], t2[:, 128:256], t2[:, 256:384],
    ]
    for r in range(4):
        for l in range(UNITS):
            piece = units[l][r * BLOCK : (r + 1) * BLOCK]
            part[r * UNITS + l] = piece
            part16[r * UNITS + l] = piece.astype(BF16)

    groups = plane + [chip]
    core_copies = [
        remote(
            part16.at[pl.ds((1 - core) * 16 + p * 4, 4)], from_core.at[pl.ds(p * 4, 4)],
            core_send.at[j], core_recv.at[j], partner,
        )
        for j, p in enumerate(groups)
    ]
    for copy in core_copies:
        copy.start()

    loads[6].wait()
    du = jnp.zeros((ROWS, CH), F32)
    for k in range(3):
        du = du + dot(g_ext[(2 - k) * PIX : (2 - k) * PIX + ROWS], wt[:, k * CH : (k + 1) * CH], 1, 0)
    back_t = (sig_y * (1.0 + y * (1.0 - sig_y)) * du).astype(BF16).astype(F32)
    dy = jnp.where(live, (g + back_t).astype(BF16).astype(F32), 0.0)

    z_order = far + [dp]
    for j, p in enumerate(groups):
        core_copies[j].wait()
        quad = part[pl.ds(core * 16 + p * 4, 4)] + from_core[pl.ds(p * 4, 4)].astype(F32)
        if j == 3:
            own[...] = quad
        else:
            quad16[j] = quad.astype(BF16)
    plane_copies = []
    for k, z in enumerate(z_order):
        for j, p in enumerate(plane):
            i = k * 3 + j
            copy = remote(quad16.at[j, z], from_plane.at[j, k], plane_send.at[i], plane_recv.at[i], at(dp, p, core))
            copy.start()
            plane_copies.append(copy)

    def summed_plane(k, z):
        for j in range(3):
            plane_copies[k * 3 + j].wait()
        return own[z] + from_plane[0, k].astype(F32) + from_plane[1, k].astype(F32) + from_plane[2, k].astype(F32)

    z_copies = []

    def pass_to_z(k):
        own16[k] = summed_plane(k, z_order[k]).astype(BF16)
        copy = remote(own16.at[k], from_z.at[dp], z_send.at[k], z_recv.at[dp], at(z_order[k], chip, core))
        copy.start()
        z_copies.append(copy)

    stage_shifts(dy, line, padded)
    da = jnp.zeros((ROWS, CH), F32)
    for tap in range(9):
        da = da + dot(shifted(padded, 2 - tap % 3, 2 - tap // 3), ws[:, tap * CH : (tap + 1) * CH], 1, 0)
        if tap in (4, 6, 8):
            pass_to_z(tap // 2 - 2)
    total = summed_plane(3, dp)

    dhat = da * (sig_n * (1.0 + normed * (1.0 - sig_n))) * gain
    dhat_frames = [frame_of(dhat, s) for s in range(CAP)]
    xhat_frames = [frame_of(xhat, s) for s in range(CAP)]
    mean_d = group_means([column_sum(v) for v in dhat_frames], members)
    mean_dx = group_means([column_sum(v * w) for v, w in zip(dhat_frames, xhat_frames)], members)
    dx = jnp.concatenate(
        [
            inverse[s : s + 1] * (dhat_frames[s] - mean_d[s : s + 1] - xhat_frames[s] * mean_dx[s : s + 1])
            for s in range(CAP)
        ],
        axis=0,
    )
    out_ref[...] = jnp.where(live, dy + dx, 0.0).astype(BF16)

    first = core * 16 + chip * 4
    mine = first + dp
    for z in near:
        remote(from_z.at[z], from_z.at[z], z_send.at[0], z_recv.at[z], partner).wait_recv()
        total = total + from_z[z].astype(F32)
    full[mine] = total.astype(BF16)

    sent = []

    def pass_on(chunk, device, recv_sem):
        copy = remote(full.at[chunk], full.at[chunk], gather_send.at[len(sent)], recv_sem, device)
        copy.start()
        sent.append(copy)

    def await_chunk(chunk, recv_sem):
        remote(full.at[chunk], full.at[chunk], gather_send.at[0], recv_sem, partner).wait_recv()

    for z in far:
        pass_on(mine, at(z, chip, core), gather_z.at[dp])
    for j, p in enumerate(plane):
        pass_on(mine, at(dp, p, core), gather_plane.at[dp * 3 + j])
    pass_on(mine, partner, gather_core.at[dp * 4 + 3])
    for z in near:
        await_chunk(first + z, gather_z.at[z])
        for j, p in enumerate(plane):
            pass_on(first + z, at(dp, p, core), gather_plane.at[z * 3 + j])
        pass_on(first + z, partner, gather_core.at[z * 4 + 3])
    for z in [dp] + near:
        for j, p in enumerate(plane):
            chunk = core * 16 + p * 4 + z
            await_chunk(chunk, gather_plane.at[z * 3 + j])
            pass_on(chunk, partner, gather_core.at[z * 4 + j])

    scale = 1.0 / math.sqrt(4 * 2 * 8 * PIX)

    def put(half):
        for r in range(2):
            rows = pl.ds(pl.multiple_of(half * 2 * BLOCK + r * BLOCK, 8), BLOCK)
            for l in range(UNITS):
                width = min(LANE, 3 * CH - l * LANE)
                value = full[half * 16 + r * UNITS + l].astype(F32) * scale
                grad_ref[rows, l * LANE : l * LANE + width] = value[:, :width]

    put(core)
    for z in [dp] + near:
        for j, p in enumerate(groups):
            await_chunk((1 - core) * 16 + p * 4 + z, gather_core.at[z * 4 + j])
    put(1 - core)
    for copy in z_copies + sent:
        copy.wait_send()


def fused_shards(frames_in, cotangent, counts, norm_gain, norm_shift, spatial_weight, temporal_weight):
    vmem = pl.BlockSpec(memory_space=pltpu.VMEM)
    hbm = pl.BlockSpec(memory_space=pltpu.HBM)
    dma = pltpu.SemaphoreType.DMA
    out, grad = pl.pallas_call(
        fused_kernel,
        out_shape=(
            pltpu.VMEM((ROWS, CH), BF16),
            pltpu.VMEM((CH, 3 * CH), F32),
        ),
        in_specs=[hbm] * 7,
        out_specs=(vmem, vmem),
        scratch_shapes=[
            pltpu.SMEM((1, 8), jnp.int32),
            pltpu.VMEM((ROWS, CH), BF16),
            pltpu.VMEM((ROWS, CH), BF16),
            pltpu.VMEM((CH,), F32),
            pltpu.VMEM((CH,), F32),
            pltpu.VMEM((CH, 9 * CH), BF16),
            pltpu.VMEM((CH, 3 * CH), BF16),
            pltpu.VMEM((ROWS + 16, CH), F32),
            pltpu.VMEM((3, CAP, SIDE + 2, SIDE, CH), F32),
            pltpu.VMEM((2, PIX, CH), BF16),
            pltpu.VMEM((2, PIX, CH), BF16),
            pltpu.VMEM((CHUNKS, BLOCK, LANE), F32),
            pltpu.VMEM((CHUNKS, BLOCK, LANE), BF16),
            pltpu.VMEM((16, BLOCK, LANE), BF16),
            pltpu.VMEM((3, 4, BLOCK, LANE), BF16),
            pltpu.VMEM((3, 4, BLOCK, LANE), BF16),
            pltpu.VMEM((4, BLOCK, LANE), F32),
            pltpu.VMEM((3, BLOCK, LANE), BF16),
            pltpu.VMEM((4, BLOCK, LANE), BF16),
            pltpu.VMEM((CHUNKS, BLOCK, LANE), BF16),
            dma((7,)), dma((2,)), dma((2,)), dma((4,)), dma((4,)), dma((12,)), dma((12,)), dma((3,)), dma((4,)),
            dma((31,)), dma((4,)), dma((12,)), dma((16,)),
        ],
        compiler_params=pltpu.CompilerParams(
            collective_id=0, has_side_effects=True, vmem_limit_bytes=60 * 1024 * 1024
        ),
    )(
        counts,
        frames_in.reshape(ROWS, CH),
        cotangent.reshape(ROWS, CH),
        norm_gain,
        norm_shift,
        spatial_weight.T,
        temporal_weight.T,
    )
    return out.reshape(frames_in.shape), grad.T


def solution(mesh):
    fused = mesh.shape["dp"] == 4 and mesh.shape["tm"] == 8

    def block(frames_in, *rest):
        if fused and frames_in.shape == (1, CAP, SIDE, SIDE, CH):
            return fused_shards(frames_in, *rest)
        return shards(frames_in, *rest)

    return jax.shard_map(
        block,
        mesh=mesh,
        in_specs=(
            P("dp", "tm", None, None, None),
            P("dp", "tm", None, None, None),
            P("dp", None),
            P(),
            P(),
            P(),
            P(),
        ),
        out_specs=(P("dp", "tm", None, None, None), P()),
        check_vma=False,
    )
```

```python
import math

import jax
import jax.numpy as jnp
from jax import lax
from jax.experimental import pallas as pl
from jax.experimental.pallas import tpu as pltpu
from jax.sharding import PartitionSpec as P

GROUPS = 32


def norm_act(values, gain, shift, groups):
    nframes, height, width, channels = values.shape
    per_group = channels // groups
    entries = height * width * per_group

    def group_mean(totals):
        summed = totals.reshape(nframes, groups, per_group).sum(axis=2) / entries
        return jnp.repeat(summed, per_group, axis=1).reshape(nframes, 1, 1, channels)

    centre = group_mean(values.sum(axis=(1, 2)))
    centred = values - centre
    spread = group_mean((centred * centred).sum(axis=(1, 2)))
    normed = centred * lax.rsqrt(spread + 1e-05) * gain + shift
    return jax.nn.silu(normed)


def patches(field):
    height, width = (field.shape[1], field.shape[2])
    padded = jnp.pad(field, ((0, 0), (1, 1), (1, 1), (0, 0)))
    pieces = [
        padded[:, row_off : row_off + height, col_off : col_off + width, :]
        for row_off in range(3)
        for col_off in range(3)
    ]
    return jnp.concatenate(pieces, axis=3)


def spatial_conv(field, weight):
    stacked = patches(field)
    leading = stacked.shape[:3]
    product = jnp.dot(
        stacked.reshape(-1, stacked.shape[3]), weight, preferred_element_type=jnp.float32
    )
    return product.reshape(leading + (weight.shape[1],))


def spatial_conv_t(field, weight):
    channels = weight.shape[1]
    flipped = (
        weight.reshape(9, -1, channels)[::-1].transpose(0, 2, 1).reshape(-1, weight.shape[0] // 9)
    )
    return spatial_conv(field, flipped)


def silu_grad(values):
    sigma = jax.nn.sigmoid(values)
    return sigma * (1.0 + values * (1.0 - sigma))


def temporal_core(y_ext, g_ext, weight):
    nframes = y_ext.shape[0] - 2
    channels = weight.shape[1]
    units = jax.nn.silu(y_ext.astype(jnp.float32)).astype(jnp.bfloat16)
    g_middle = g_ext[1:-1]
    g_mid = g_middle.reshape(-1, channels)
    grads = []
    back_sum = jnp.zeros((g_mid.shape[0], channels), jnp.float32)
    for tap_k in range(3):
        taken = units[tap_k : tap_k + nframes].reshape(-1, channels)
        grads.append(
            lax.dot_general(
                taken, g_mid, (((0,), (0,)), ((), ())), preferred_element_type=jnp.float32
            )
        )
        tap_weight = weight[tap_k * channels : (tap_k + 1) * channels]
        source = g_ext[2 - tap_k : 2 - tap_k + nframes].reshape(-1, channels)
        back_sum = back_sum + lax.dot_general(
            source, tap_weight, (((1,), (1,)), ((), ())), preferred_element_type=jnp.float32
        )
    middle = y_ext[1:-1]
    back_t = (silu_grad(middle.astype(jnp.float32)) * back_sum.reshape(middle.shape)).astype(
        jnp.bfloat16
    )
    return (back_t, jnp.concatenate(grads, axis=0))


def frame_slots(counts_row, nframes, cap):
    ndevices = counts_row.shape[0]
    ends = jnp.cumsum(counts_row)
    starts = ends - counts_row
    frame_ids = jnp.arange(nframes, dtype=jnp.int32)
    owner = jnp.sum((ends[None, :] <= frame_ids[:, None]).astype(jnp.int32), axis=1)
    device_ids = jnp.arange(ndevices, dtype=jnp.int32)
    first = jnp.sum(jnp.where(device_ids[None, :] == owner[:, None], starts[None, :], 0), axis=1)
    return owner * cap + frame_ids - first


def slot_frames(counts_row, cap):
    ndevices = counts_row.shape[0]
    ends = jnp.cumsum(counts_row)
    starts = ends - counts_row
    slot_ids = jnp.arange(ndevices * cap, dtype=jnp.int32)
    device = slot_ids // cap
    inner = slot_ids % cap
    device_ids = jnp.arange(ndevices, dtype=jnp.int32)
    onehot = device[:, None] == device_ids[None, :]
    held = jnp.sum(jnp.where(onehot, counts_row[None, :], 0), axis=1)
    first = jnp.sum(jnp.where(onehot, starts[None, :], 0), axis=1)
    live = inner < held
    return (jnp.where(live, first + inner, 0), live)


def shards(frames_in, cotangent, counts, norm_gain, norm_shift, spatial_weight, temporal_weight):
    inputs = frames_in[0]
    cotan = cotangent[0]
    counts_row = counts[0]
    cap = inputs.shape[0]
    tm_size = lax.axis_size("tm")
    own_count = jnp.sum(
        jnp.where(jnp.arange(tm_size, dtype=jnp.int32) == lax.axis_index("tm"), counts_row, 0)
    )
    live_slots = (jnp.arange(cap, dtype=jnp.int32) < own_count)[:, None, None, None]

    def activate(values):
        return norm_act(values, norm_gain, norm_shift, GROUPS)

    inputs_f = inputs.astype(jnp.float32)
    act_f, act_back = jax.vjp(activate, inputs_f)
    acts = act_f.astype(jnp.bfloat16)
    mixed = spatial_conv(acts, spatial_weight)
    y_out = (inputs_f + mixed).astype(jnp.bfloat16)
    y_rows, g_rows = (
        lax.all_to_all(y_out, "tm", split_axis=1, concat_axis=0, tiled=True),
        lax.all_to_all(cotan, "tm", split_axis=1, concat_axis=0, tiled=True),
    )
    pick = frame_slots(counts_row, 2 * tm_size, cap)
    pad_spec = ((1, 1), (0, 0), (0, 0), (0, 0))
    y_ext = jnp.pad(jnp.take(y_rows, pick, axis=0), pad_spec)
    g_ext = jnp.pad(jnp.take(g_rows, pick, axis=0), pad_spec)
    back_rows, grad_part = temporal_core(y_ext, g_ext, temporal_weight)
    back_idx, live = slot_frames(counts_row, cap)
    back_slots = jnp.where(
        live[:, None, None, None],
        jnp.take(back_rows, back_idx, axis=0),
        jnp.zeros((), jnp.bfloat16),
    )
    back_t = lax.all_to_all(back_slots, "tm", split_axis=0, concat_axis=1, tiled=True)
    d_out = (cotan.astype(jnp.float32) + back_t.astype(jnp.float32)).astype(jnp.bfloat16)
    d_act = spatial_conv_t(d_out, spatial_weight)
    d_in = d_out.astype(jnp.float32) + act_back(d_act)[0]
    d_in = jnp.where(live_slots, d_in, 0.0).astype(jnp.bfloat16)
    height, width = (inputs.shape[1], inputs.shape[2])
    scale = 1.0 / math.sqrt(lax.axis_size("dp") * 2 * tm_size * height * width)
    summed = lax.psum(grad_part, ("dp", "tm"))
    return (d_in[None], summed * scale)


CAP = 3
SIDE = 8
CH = 320
PIX = SIDE * SIDE
ROWS = CAP * PIX
LANE = 128
UNITS = 8
BLOCK = 80
CHUNKS = 32
F32 = jnp.float32
BF16 = jnp.bfloat16


def dot(a, b, ca, cb):
    return lax.dot_general(a, b, (((ca,), (cb,)), ((), ())), preferred_element_type=F32)


def group_matrix():
    def ids(axis):
        index = lax.broadcasted_iota(jnp.int32, (CH, CH), axis).astype(F32)
        return jnp.floor((index + 0.5) * (GROUPS / CH))

    return (ids(0) == ids(1)).astype(BF16)


def group_means(totals, members):
    rows = jnp.concatenate(totals, axis=0)
    high = rows.astype(BF16)
    rest = rows - high.astype(F32)
    mid = rest.astype(BF16)
    low = (rest - mid.astype(F32)).astype(BF16)
    summed = dot(high, members, 1, 0) + dot(mid, members, 1, 0) + dot(low, members, 1, 0)
    return summed * (1.0 / (PIX * (CH // GROUPS)))


def frame_of(value, frame):
    return value[frame * PIX : (frame + 1) * PIX]


def column_sum(value):
    return jnp.sum(value, axis=0, keepdims=True)


def sigmoid(value):
    return 1.0 / (1.0 + jnp.exp(-value))


def stage_shifts(value, line, padded):
    column = lax.broadcasted_iota(jnp.int32, (ROWS, CH), 0) & (SIDE - 1)
    line[8 : 8 + ROWS, :] = value
    left = jnp.where(column == 0, 0.0, line[7 : 7 + ROWS, :])
    right = jnp.where(column == SIDE - 1, 0.0, line[9 : 9 + ROWS, :])
    for j, moved in enumerate((left, value, right)):
        padded[j, :, 1 : 1 + SIDE] = moved.reshape(CAP, SIDE, SIDE, CH)


def turned_patches(value):
    wide = jnp.concatenate([value, jnp.zeros((64, CH), F32)], axis=0).T
    pixel = lax.broadcasted_iota(jnp.int32, (1, wide.shape[1]), 1)
    row, column = (pixel & (PIX - 1)) >> 3, pixel & (SIDE - 1)
    pieces = []
    for i in (-1, 0, 1):
        for j in (-1, 0, 1):
            move = (-(i * SIDE + j)) % wide.shape[1]
            moved = pltpu.roll(wide, move, 1) if move else wide
            inside = (row + i >= 0) & (row + i < SIDE) & (column + j >= 0) & (column + j < SIDE)
            pieces.append((moved * inside.astype(F32)).astype(BF16))
    return jnp.concatenate(pieces, axis=0)


def shifted(padded, j, i):
    return padded[j, :, i : i + SIDE].reshape(ROWS, CH).astype(BF16)


def fused_kernel(
    counts_hbm, x_hbm, g_hbm, gain_hbm, shift_hbm, ws_hbm, wt_hbm, out_ref, grad_ref,
    counts, x_ref, g_ref, gain_ref, shift_ref, ws, wt, line, padded, edge, halo, turned, part, part16, from_core, quad16, from_plane, own, own16, from_z, full,
    weight_sem, halo_send, halo_recv, core_send, core_recv, plane_send, plane_recv, z_send, z_recv,
    gather_send, gather_z, gather_plane, gather_core,
):
    dp = lax.axis_index("dp")
    tm = lax.axis_index("tm")
    yy, xx, core = tm // 4, (tm // 2) % 2, tm % 2
    chip = tm // 2

    def at(z, chip_id, core_id):
        return (z, chip_id * 2 + core_id)

    plane = [yy * 2 + (1 - xx), (1 - yy) * 2 + xx, (1 - yy) * 2 + (1 - xx)]
    near = [dp + 1 - 2 * (dp % 2), 2 - dp // 2, 3 - 3 * (dp // 2)]
    far = near[::-1]
    before, after = lax.rem(tm + 7, 8), lax.rem(tm + 1, 8)
    partner = at(dp, chip, 1 - core)
    peers = [(dp, before), (dp, after)] + [at(dp, p, core) for p in plane] + [at(z, chip, core) for z in near]

    def remote(src, dst, send_sem, recv_sem, device):
        copy = pltpu.make_async_remote_copy(
            src_ref=src, dst_ref=dst, send_sem=send_sem, recv_sem=recv_sem,
            device_id=device, device_id_type=pl.DeviceIdType.MESH,
        )
        return copy

    barrier = pltpu.get_barrier_semaphore()
    for peer in peers:
        pl.semaphore_signal(barrier, inc=1, device_id=peer, device_id_type=pl.DeviceIdType.MESH)
    places = [
        (g_hbm, g_ref), (counts_hbm, counts), (x_hbm, x_ref), (gain_hbm, gain_ref), (shift_hbm, shift_ref),
        (ws_hbm, ws), (wt_hbm, wt),
    ]
    loads = [pltpu.make_async_copy(src, dst, weight_sem.at[i]) for i, (src, dst) in enumerate(places)]
    for load in loads:
        load.start()
    members = group_matrix()
    for load in loads[:2]:
        load.wait()

    count = counts[0, tm]
    g = g_ref[...].astype(F32)
    g_frames = [frame_of(g, s) for s in range(CAP)]
    last = jnp.where(count == 3, g_frames[2], jnp.where(count == 2, g_frames[1], g_frames[0]))
    edge[0] = g_frames[0].astype(BF16)
    edge[1] = last.astype(BF16)
    halo_copies = [
        remote(edge.at[0], halo.at[1], halo_send.at[0], halo_recv.at[1], (dp, before)),
        remote(edge.at[1], halo.at[0], halo_send.at[1], halo_recv.at[0], (dp, after)),
    ]
    pl.semaphore_wait(barrier, len(peers))
    for copy in halo_copies:
        copy.start()
    for load in loads[2:5]:
        load.wait()

    gain, shift = gain_ref[...].reshape(1, CH), shift_ref[...].reshape(1, CH)
    x = x_ref[...].astype(F32)
    x_frames = [frame_of(x, s) for s in range(CAP)]
    means = group_means([column_sum(v) for v in x_frames], members)
    centred = [v - means[s : s + 1] for s, v in enumerate(x_frames)]
    spread = group_means([column_sum(v * v) for v in centred], members)
    inverse = lax.rsqrt(spread + 1e-05)
    xhat = jnp.concatenate([v * inverse[s : s + 1] for s, v in enumerate(centred)], axis=0)
    normed = xhat * gain + shift
    sig_n = sigmoid(normed)
    padded[...] = jnp.zeros_like(padded)
    patched = turned_patches(normed * sig_n)
    for copy in halo_copies:
        copy.wait()
    prev_edge = jnp.where(tm == 0, 0.0, halo[0].astype(F32))
    next_edge = jnp.where(tm == 7, 0.0, halo[1].astype(F32))
    g_ext = jnp.concatenate(
        [
            prev_edge,
            g_frames[0],
            jnp.where(count == 1, next_edge, g_frames[1]),
            jnp.where(count == 2, next_edge, g_frames[2]),
            next_edge,
        ],
        axis=0,
    )
    turned[...] = g_ext.T.astype(BF16)
    g_ext = g_ext.astype(BF16)

    loads[5].wait()
    mixed = dot(ws[...], patched, 1, 0).T[:ROWS]
    y = (x + mixed).astype(BF16).astype(F32)
    sig_y = sigmoid(y)
    live = lax.broadcasted_iota(jnp.int32, (ROWS, CH), 0) < count * PIX
    u = jnp.where(live, y * sig_y, 0.0).astype(BF16)

    none = jnp.zeros((ROWS, 64), BF16)
    u_low = jnp.concatenate([u, none], axis=1)
    u_high = jnp.concatenate([none, u], axis=1)

    def below(value, frames):
        zero = jnp.zeros((PIX, value.shape[1]), BF16)
        return jnp.concatenate([zero] * frames + [value] + [zero] * (2 - frames), axis=0)

    first_tap, second_tap, third_tap = below(u_low, 2), below(u_high, 1), below(u_low, 0)

    def gradient_half(half):
        rows = turned[pl.ds(pl.multiple_of(half * 2 * BLOCK, 16), 2 * BLOCK), :]
        t0, t1, t2 = dot(rows, first_tap, 1, 0), dot(rows, second_tap, 1, 0), dot(rows, third_tap, 1, 0)
        units = [
            t0[:, 0:128], t0[:, 128:256], t0[:, 256:384] + t1[:, 0:128], t1[:, 128:256], t1[:, 256:384],
            t2[:, 0:128], t2[:, 128:256], t2[:, 256:384],
        ]
        return [(r * UNITS + l, units[l][r * BLOCK : (r + 1) * BLOCK]) for r in range(2) for l in range(UNITS)]

    for i, piece in gradient_half(1 - core):
        part16[i] = piece.astype(BF16)
    groups = plane + [chip]
    core_copies = [
        remote(
            part16.at[pl.ds(p * 4, 4)], from_core.at[pl.ds(p * 4, 4)],
            core_send.at[j], core_recv.at[j], partner,
        )
        for j, p in enumerate(groups)
    ]
    for copy in core_copies:
        copy.start()
    for i, piece in gradient_half(core):
        part[i] = piece

    loads[6].wait()
    du = jnp.zeros((ROWS, CH), F32)
    for k in range(3):
        du = du + dot(g_ext[(2 - k) * PIX : (2 - k) * PIX + ROWS], wt[:, k * CH : (k + 1) * CH], 1, 0)
    back_t = (sig_y * (1.0 + y * (1.0 - sig_y)) * du).astype(BF16).astype(F32)
    dy = jnp.where(live, (g + back_t).astype(BF16).astype(F32), 0.0)

    z_order = far + [dp]
    for j, p in enumerate(groups):
        core_copies[j].wait()
        quad = part[pl.ds(p * 4, 4)] + from_core[pl.ds(p * 4, 4)].astype(F32)
        if j == 3:
            own[...] = quad
        else:
            quad16[j] = quad.astype(BF16)
    plane_copies = []
    for k, z in enumerate(z_order):
        for j, p in enumerate(plane):
            i = k * 3 + j
            copy = remote(quad16.at[j, z], from_plane.at[j, k], plane_send.at[i], plane_recv.at[i], at(dp, p, core))
            copy.start()
            plane_copies.append(copy)

    def summed_plane(k, z):
        for j in range(3):
            plane_copies[k * 3 + j].wait()
        return own[z] + from_plane[0, k].astype(F32) + from_plane[1, k].astype(F32) + from_plane[2, k].astype(F32)

    z_copies = []

    def pass_to_z(k):
        own16[k] = summed_plane(k, z_order[k]).astype(BF16)
        copy = remote(own16.at[k], from_z.at[dp], z_send.at[k], z_recv.at[dp], at(z_order[k], chip, core))
        copy.start()
        z_copies.append(copy)

    stage_shifts(dy, line, padded)
    da = jnp.zeros((ROWS, CH), F32)
    for tap in range(9):
        da = da + dot(shifted(padded, 2 - tap % 3, 2 - tap // 3), ws[:, tap * CH : (tap + 1) * CH], 1, 0)
        if tap in (4, 6, 8):
            pass_to_z(tap // 2 - 2)
    total = summed_plane(3, dp)

    dhat = da * (sig_n * (1.0 + normed * (1.0 - sig_n))) * gain
    dhat_frames = [frame_of(dhat, s) for s in range(CAP)]
    xhat_frames = [frame_of(xhat, s) for s in range(CAP)]
    mean_d = group_means([column_sum(v) for v in dhat_frames], members)
    mean_dx = group_means([column_sum(v * w) for v, w in zip(dhat_frames, xhat_frames)], members)
    dx = jnp.concatenate(
        [
            inverse[s : s + 1] * (dhat_frames[s] - mean_d[s : s + 1] - xhat_frames[s] * mean_dx[s : s + 1])
            for s in range(CAP)
        ],
        axis=0,
    )
    out_ref[...] = jnp.where(live, dy + dx, 0.0).astype(BF16)

    first = core * 16 + chip * 4
    mine = first + dp
    for z in near:
        remote(from_z.at[z], from_z.at[z], z_send.at[0], z_recv.at[z], partner).wait_recv()
        total = total + from_z[z].astype(F32)
    full[mine] = total.astype(BF16)

    sent = []

    def pass_on(chunk, device, recv_sem):
        copy = remote(full.at[chunk], full.at[chunk], gather_send.at[len(sent)], recv_sem, device)
        copy.start()
        sent.append(copy)

    def await_chunk(chunk, recv_sem):
        remote(full.at[chunk], full.at[chunk], gather_send.at[0], recv_sem, partner).wait_recv()

    for z in far:
        pass_on(mine, at(z, chip, core), gather_z.at[dp])
    for j, p in enumerate(plane):
        pass_on(mine, at(dp, p, core), gather_plane.at[dp * 3 + j])
    pass_on(mine, partner, gather_core.at[dp * 4 + 3])
    for z in near:
        await_chunk(first + z, gather_z.at[z])
        for j, p in enumerate(plane):
            pass_on(first + z, at(dp, p, core), gather_plane.at[z * 3 + j])
        pass_on(first + z, partner, gather_core.at[z * 4 + 3])
    for z in [dp] + near:
        for j, p in enumerate(plane):
            chunk = core * 16 + p * 4 + z
            await_chunk(chunk, gather_plane.at[z * 3 + j])
            pass_on(chunk, partner, gather_core.at[z * 4 + j])

    scale = 1.0 / math.sqrt(4 * 2 * 8 * PIX)

    def put(half):
        for r in range(2):
            rows = pl.ds(pl.multiple_of(half * 2 * BLOCK + r * BLOCK, 8), BLOCK)
            for l in range(UNITS):
                width = min(LANE, 3 * CH - l * LANE)
                value = full[half * 16 + r * UNITS + l].astype(F32) * scale
                grad_ref[rows, l * LANE : l * LANE + width] = value[:, :width]

    put(core)
    for z in [dp] + near:
        for j, p in enumerate(groups):
            await_chunk((1 - core) * 16 + p * 4 + z, gather_core.at[z * 4 + j])
    put(1 - core)
    for copy in z_copies + sent:
        copy.wait_send()


def fused_shards(frames_in, cotangent, counts, norm_gain, norm_shift, spatial_weight, temporal_weight):
    vmem = pl.BlockSpec(memory_space=pltpu.VMEM)
    hbm = pl.BlockSpec(memory_space=pltpu.HBM)
    dma = pltpu.SemaphoreType.DMA
    out, grad = pl.pallas_call(
        fused_kernel,
        out_shape=(
            pltpu.VMEM((ROWS, CH), BF16),
            pltpu.VMEM((CH, 3 * CH), F32),
        ),
        in_specs=[hbm] * 7,
        out_specs=(vmem, vmem),
        scratch_shapes=[
            pltpu.SMEM((1, 8), jnp.int32),
            pltpu.VMEM((ROWS, CH), BF16),
            pltpu.VMEM((ROWS, CH), BF16),
            pltpu.VMEM((CH,), F32),
            pltpu.VMEM((CH,), F32),
            pltpu.VMEM((CH, 9 * CH), BF16),
            pltpu.VMEM((CH, 3 * CH), BF16),
            pltpu.VMEM((ROWS + 16, CH), F32),
            pltpu.VMEM((3, CAP, SIDE + 2, SIDE, CH), F32),
            pltpu.VMEM((2, PIX, CH), BF16),
            pltpu.VMEM((2, PIX, CH), BF16),
            pltpu.VMEM((CH, (CAP + 2) * PIX), BF16),
            pltpu.VMEM((16, BLOCK, LANE), F32),
            pltpu.VMEM((16, BLOCK, LANE), BF16),
            pltpu.VMEM((16, BLOCK, LANE), BF16),
            pltpu.VMEM((3, 4, BLOCK, LANE), BF16),
            pltpu.VMEM((3, 4, BLOCK, LANE), BF16),
            pltpu.VMEM((4, BLOCK, LANE), F32),
            pltpu.VMEM((3, BLOCK, LANE), BF16),
            pltpu.VMEM((4, BLOCK, LANE), BF16),
            pltpu.VMEM((CHUNKS, BLOCK, LANE), BF16),
            dma((7,)), dma((2,)), dma((2,)), dma((4,)), dma((4,)), dma((12,)), dma((12,)), dma((3,)), dma((4,)),
            dma((31,)), dma((4,)), dma((12,)), dma((16,)),
        ],
        compiler_params=pltpu.CompilerParams(
            collective_id=0, has_side_effects=True, vmem_limit_bytes=60 * 1024 * 1024
        ),
    )(
        counts,
        frames_in.reshape(ROWS, CH),
        cotangent.reshape(ROWS, CH),
        norm_gain,
        norm_shift,
        spatial_weight.T,
        temporal_weight.T,
    )
    return out.reshape(frames_in.shape), grad.T


def solution(mesh):
    fused = mesh.shape["dp"] == 4 and mesh.shape["tm"] == 8

    def block(frames_in, *rest):
        if fused and frames_in.shape == (1, CAP, SIDE, SIDE, CH):
            return fused_shards(frames_in, *rest)
        return shards(frames_in, *rest)

    return jax.shard_map(
        block,
        mesh=mesh,
        in_specs=(
            P("dp", "tm", None, None, None),
            P("dp", "tm", None, None, None),
            P("dp", None),
            P(),
            P(),
            P(),
            P(),
        ),
        out_specs=(P("dp", "tm", None, None, None), P()),
        check_vma=False,
    )
```

```python
import math

import jax
import jax.numpy as jnp
from jax import lax
from jax.experimental import pallas as pl
from jax.experimental.pallas import tpu as pltpu
from jax.sharding import PartitionSpec as P

GROUPS = 32


def norm_act(values, gain, shift, groups):
    nframes, height, width, channels = values.shape
    per_group = channels // groups
    entries = height * width * per_group

    def group_mean(totals):
        summed = totals.reshape(nframes, groups, per_group).sum(axis=2) / entries
        return jnp.repeat(summed, per_group, axis=1).reshape(nframes, 1, 1, channels)

    centre = group_mean(values.sum(axis=(1, 2)))
    centred = values - centre
    spread = group_mean((centred * centred).sum(axis=(1, 2)))
    normed = centred * lax.rsqrt(spread + 1e-05) * gain + shift
    return jax.nn.silu(normed)


def patches(field):
    height, width = (field.shape[1], field.shape[2])
    padded = jnp.pad(field, ((0, 0), (1, 1), (1, 1), (0, 0)))
    pieces = [
        padded[:, row_off : row_off + height, col_off : col_off + width, :]
        for row_off in range(3)
        for col_off in range(3)
    ]
    return jnp.concatenate(pieces, axis=3)


def spatial_conv(field, weight):
    stacked = patches(field)
    leading = stacked.shape[:3]
    product = jnp.dot(
        stacked.reshape(-1, stacked.shape[3]), weight, preferred_element_type=jnp.float32
    )
    return product.reshape(leading + (weight.shape[1],))


def spatial_conv_t(field, weight):
    channels = weight.shape[1]
    flipped = (
        weight.reshape(9, -1, channels)[::-1].transpose(0, 2, 1).reshape(-1, weight.shape[0] // 9)
    )
    return spatial_conv(field, flipped)


def silu_grad(values):
    sigma = jax.nn.sigmoid(values)
    return sigma * (1.0 + values * (1.0 - sigma))


def temporal_core(y_ext, g_ext, weight):
    nframes = y_ext.shape[0] - 2
    channels = weight.shape[1]
    units = jax.nn.silu(y_ext.astype(jnp.float32)).astype(jnp.bfloat16)
    g_middle = g_ext[1:-1]
    g_mid = g_middle.reshape(-1, channels)
    grads = []
    back_sum = jnp.zeros((g_mid.shape[0], channels), jnp.float32)
    for tap_k in range(3):
        taken = units[tap_k : tap_k + nframes].reshape(-1, channels)
        grads.append(
            lax.dot_general(
                taken, g_mid, (((0,), (0,)), ((), ())), preferred_element_type=jnp.float32
            )
        )
        tap_weight = weight[tap_k * channels : (tap_k + 1) * channels]
        source = g_ext[2 - tap_k : 2 - tap_k + nframes].reshape(-1, channels)
        back_sum = back_sum + lax.dot_general(
            source, tap_weight, (((1,), (1,)), ((), ())), preferred_element_type=jnp.float32
        )
    middle = y_ext[1:-1]
    back_t = (silu_grad(middle.astype(jnp.float32)) * back_sum.reshape(middle.shape)).astype(
        jnp.bfloat16
    )
    return (back_t, jnp.concatenate(grads, axis=0))


def frame_slots(counts_row, nframes, cap):
    ndevices = counts_row.shape[0]
    ends = jnp.cumsum(counts_row)
    starts = ends - counts_row
    frame_ids = jnp.arange(nframes, dtype=jnp.int32)
    owner = jnp.sum((ends[None, :] <= frame_ids[:, None]).astype(jnp.int32), axis=1)
    device_ids = jnp.arange(ndevices, dtype=jnp.int32)
    first = jnp.sum(jnp.where(device_ids[None, :] == owner[:, None], starts[None, :], 0), axis=1)
    return owner * cap + frame_ids - first


def slot_frames(counts_row, cap):
    ndevices = counts_row.shape[0]
    ends = jnp.cumsum(counts_row)
    starts = ends - counts_row
    slot_ids = jnp.arange(ndevices * cap, dtype=jnp.int32)
    device = slot_ids // cap
    inner = slot_ids % cap
    device_ids = jnp.arange(ndevices, dtype=jnp.int32)
    onehot = device[:, None] == device_ids[None, :]
    held = jnp.sum(jnp.where(onehot, counts_row[None, :], 0), axis=1)
    first = jnp.sum(jnp.where(onehot, starts[None, :], 0), axis=1)
    live = inner < held
    return (jnp.where(live, first + inner, 0), live)


def shards(frames_in, cotangent, counts, norm_gain, norm_shift, spatial_weight, temporal_weight):
    inputs = frames_in[0]
    cotan = cotangent[0]
    counts_row = counts[0]
    cap = inputs.shape[0]
    tm_size = lax.axis_size("tm")
    own_count = jnp.sum(
        jnp.where(jnp.arange(tm_size, dtype=jnp.int32) == lax.axis_index("tm"), counts_row, 0)
    )
    live_slots = (jnp.arange(cap, dtype=jnp.int32) < own_count)[:, None, None, None]

    def activate(values):
        return norm_act(values, norm_gain, norm_shift, GROUPS)

    inputs_f = inputs.astype(jnp.float32)
    act_f, act_back = jax.vjp(activate, inputs_f)
    acts = act_f.astype(jnp.bfloat16)
    mixed = spatial_conv(acts, spatial_weight)
    y_out = (inputs_f + mixed).astype(jnp.bfloat16)
    y_rows, g_rows = (
        lax.all_to_all(y_out, "tm", split_axis=1, concat_axis=0, tiled=True),
        lax.all_to_all(cotan, "tm", split_axis=1, concat_axis=0, tiled=True),
    )
    pick = frame_slots(counts_row, 2 * tm_size, cap)
    pad_spec = ((1, 1), (0, 0), (0, 0), (0, 0))
    y_ext = jnp.pad(jnp.take(y_rows, pick, axis=0), pad_spec)
    g_ext = jnp.pad(jnp.take(g_rows, pick, axis=0), pad_spec)
    back_rows, grad_part = temporal_core(y_ext, g_ext, temporal_weight)
    back_idx, live = slot_frames(counts_row, cap)
    back_slots = jnp.where(
        live[:, None, None, None],
        jnp.take(back_rows, back_idx, axis=0),
        jnp.zeros((), jnp.bfloat16),
    )
    back_t = lax.all_to_all(back_slots, "tm", split_axis=0, concat_axis=1, tiled=True)
    d_out = (cotan.astype(jnp.float32) + back_t.astype(jnp.float32)).astype(jnp.bfloat16)
    d_act = spatial_conv_t(d_out, spatial_weight)
    d_in = d_out.astype(jnp.float32) + act_back(d_act)[0]
    d_in = jnp.where(live_slots, d_in, 0.0).astype(jnp.bfloat16)
    height, width = (inputs.shape[1], inputs.shape[2])
    scale = 1.0 / math.sqrt(lax.axis_size("dp") * 2 * tm_size * height * width)
    summed = lax.psum(grad_part, ("dp", "tm"))
    return (d_in[None], summed * scale)


CAP = 3
SIDE = 8
CH = 320
PIX = SIDE * SIDE
ROWS = CAP * PIX
LANE = 128
UNITS = 8
BLOCK = 80
CHUNKS = 32
F32 = jnp.float32
BF16 = jnp.bfloat16


def dot(a, b, ca, cb):
    return lax.dot_general(a, b, (((ca,), (cb,)), ((), ())), preferred_element_type=F32)


def group_matrix():
    def ids(axis):
        index = lax.broadcasted_iota(jnp.int32, (CH, CH), axis).astype(F32)
        return jnp.floor((index + 0.5) * (GROUPS / CH))

    return (ids(0) == ids(1)).astype(BF16)


def group_means(totals, members):
    rows = jnp.concatenate(totals, axis=0)
    high = rows.astype(BF16)
    rest = rows - high.astype(F32)
    mid = rest.astype(BF16)
    low = (rest - mid.astype(F32)).astype(BF16)
    summed = dot(high, members, 1, 0) + dot(mid, members, 1, 0) + dot(low, members, 1, 0)
    return summed * (1.0 / (PIX * (CH // GROUPS)))


def frame_of(value, frame):
    return value[frame * PIX : (frame + 1) * PIX]


def column_sum(value):
    return jnp.sum(value, axis=0, keepdims=True)


def sigmoid(value):
    return 1.0 / (1.0 + jnp.exp(-value))


def stage_shifts(value, line, padded):
    column = lax.broadcasted_iota(jnp.int32, (ROWS, CH), 0) & (SIDE - 1)
    line[8 : 8 + ROWS, :] = value
    left = jnp.where(column == 0, 0.0, line[7 : 7 + ROWS, :])
    right = jnp.where(column == SIDE - 1, 0.0, line[9 : 9 + ROWS, :])
    for j, moved in enumerate((left, value, right)):
        padded[j, :, 1 : 1 + SIDE] = moved.reshape(CAP, SIDE, SIDE, CH)


def turned_patches(value):
    wide = jnp.concatenate([value, jnp.zeros((64, CH), F32)], axis=0).T
    pixel = lax.broadcasted_iota(jnp.int32, (1, wide.shape[1]), 1)
    row, column = (pixel & (PIX - 1)) >> 3, pixel & (SIDE - 1)
    pieces = []
    for i in (-1, 0, 1):
        for j in (-1, 0, 1):
            move = (-(i * SIDE + j)) % wide.shape[1]
            moved = pltpu.roll(wide, move, 1) if move else wide
            inside = (row + i >= 0) & (row + i < SIDE) & (column + j >= 0) & (column + j < SIDE)
            pieces.append((moved * inside.astype(F32)).astype(BF16))
    return jnp.concatenate(pieces, axis=0)


def shifted(padded, j, i):
    return padded[j, :, i : i + SIDE].reshape(ROWS, CH).astype(BF16)


def fused_kernel(
    counts_hbm, x_hbm, g_hbm, gain_hbm, shift_hbm, ws_hbm, wt_hbm, out_ref, grad_ref,
    counts, x_ref, g_ref, gain_ref, shift_ref, ws, wt, line, padded, edge, halo, turned, part, part16, from_core, quad16, from_plane, own16, from_z, full,
    weight_sem, halo_send, halo_recv, core_send, core_recv, plane_send, plane_recv, z_send, z_recv,
    gather_send, gather_z, gather_plane, gather_core,
):
    dp = lax.axis_index("dp")
    tm = lax.axis_index("tm")
    yy, xx, core = tm // 4, (tm // 2) % 2, tm % 2
    chip = tm // 2

    def at(z, chip_id, core_id):
        return (z, chip_id * 2 + core_id)

    plane = [yy * 2 + (1 - xx), (1 - yy) * 2 + xx, (1 - yy) * 2 + (1 - xx)]
    near = [dp + 1 - 2 * (dp % 2), 2 - dp // 2, 3 - 3 * (dp // 2)]
    far = near[::-1]
    before, after = lax.rem(tm + 7, 8), lax.rem(tm + 1, 8)
    partner = at(dp, chip, 1 - core)
    peers = [(dp, before), (dp, after)] + [at(dp, p, core) for p in plane] + [at(z, chip, core) for z in near]

    def remote(src, dst, send_sem, recv_sem, device):
        copy = pltpu.make_async_remote_copy(
            src_ref=src, dst_ref=dst, send_sem=send_sem, recv_sem=recv_sem,
            device_id=device, device_id_type=pl.DeviceIdType.MESH,
        )
        return copy

    barrier = pltpu.get_barrier_semaphore()
    for peer in peers:
        pl.semaphore_signal(barrier, inc=1, device_id=peer, device_id_type=pl.DeviceIdType.MESH)
    places = [
        (g_hbm, g_ref), (counts_hbm, counts), (x_hbm, x_ref), (gain_hbm, gain_ref), (shift_hbm, shift_ref),
        (ws_hbm, ws), (wt_hbm, wt),
    ]
    loads = [pltpu.make_async_copy(src, dst, weight_sem.at[i]) for i, (src, dst) in enumerate(places)]
    for load in loads:
        load.start()
    members = group_matrix()
    for load in loads[:2]:
        load.wait()

    count = counts[0, tm]
    g = g_ref[...].astype(F32)
    g_frames = [frame_of(g, s) for s in range(CAP)]
    last = jnp.where(count == 3, g_frames[2], jnp.where(count == 2, g_frames[1], g_frames[0]))
    edge[0] = g_frames[0].astype(BF16)
    edge[1] = last.astype(BF16)
    halo_copies = [
        remote(edge.at[0], halo.at[1], halo_send.at[0], halo_recv.at[1], (dp, before)),
        remote(edge.at[1], halo.at[0], halo_send.at[1], halo_recv.at[0], (dp, after)),
    ]
    pl.semaphore_wait(barrier, len(peers))
    for copy in halo_copies:
        copy.start()
    for load in loads[2:5]:
        load.wait()

    gain, shift = gain_ref[...].reshape(1, CH), shift_ref[...].reshape(1, CH)
    x = x_ref[...].astype(F32)
    x_frames = [frame_of(x, s) for s in range(CAP)]
    means = group_means([column_sum(v) for v in x_frames], members)
    centred = [v - means[s : s + 1] for s, v in enumerate(x_frames)]
    spread = group_means([column_sum(v * v) for v in centred], members)
    inverse = lax.rsqrt(spread + 1e-05)
    xhat = jnp.concatenate([v * inverse[s : s + 1] for s, v in enumerate(centred)], axis=0)
    normed = xhat * gain + shift
    sig_n = sigmoid(normed)
    padded[...] = jnp.zeros_like(padded)
    patched = turned_patches(normed * sig_n)
    for copy in halo_copies:
        copy.wait()
    prev_edge = jnp.where(tm == 0, 0.0, halo[0].astype(F32))
    next_edge = jnp.where(tm == 7, 0.0, halo[1].astype(F32))
    g_ext = jnp.concatenate(
        [
            prev_edge,
            g_frames[0],
            jnp.where(count == 1, next_edge, g_frames[1]),
            jnp.where(count == 2, next_edge, g_frames[2]),
            next_edge,
        ],
        axis=0,
    )
    turned[...] = g_ext.T.astype(BF16)
    g_ext = g_ext.astype(BF16)

    loads[5].wait()
    mixed = dot(ws[...], patched, 1, 0).T[:ROWS]
    y = (x + mixed).astype(BF16).astype(F32)
    sig_y = sigmoid(y)
    live = lax.broadcasted_iota(jnp.int32, (ROWS, CH), 0) < count * PIX
    u = jnp.where(live, y * sig_y, 0.0).astype(BF16)

    none = jnp.zeros((ROWS, 64), BF16)
    u_low = jnp.concatenate([u, none], axis=1)
    u_high = jnp.concatenate([none, u], axis=1)

    def below(value, frames):
        zero = jnp.zeros((PIX, value.shape[1]), BF16)
        return jnp.concatenate([zero] * frames + [value] + [zero] * (2 - frames), axis=0)

    first_tap, second_tap, third_tap = below(u_low, 2), below(u_high, 1), below(u_low, 0)

    def gradient_half(half):
        rows = turned[pl.ds(pl.multiple_of(half * 2 * BLOCK, 16), 2 * BLOCK), :]
        t0, t1, t2 = dot(rows, first_tap, 1, 0), dot(rows, second_tap, 1, 0), dot(rows, third_tap, 1, 0)
        units = [
            t0[:, 0:128], t0[:, 128:256], t0[:, 256:384] + t1[:, 0:128], t1[:, 128:256], t1[:, 256:384],
            t2[:, 0:128], t2[:, 128:256], t2[:, 256:384],
        ]
        return [(r * UNITS + l, units[l][r * BLOCK : (r + 1) * BLOCK]) for r in range(2) for l in range(UNITS)]

    for i, piece in gradient_half(1 - core):
        part16[i] = piece.astype(BF16)
    z_order = far + [dp]
    core_copies = [
        remote(
            part16.at[pl.ds(z * 4, 4)], from_core.at[pl.ds(z * 4, 4)], core_send.at[k], core_recv.at[k], partner
        )
        for k, z in enumerate(z_order)
    ]
    for copy in core_copies:
        copy.start()
    for i, piece in gradient_half(core):
        part[i] = piece

    plane_copies = []
    for k, z in enumerate(z_order):
        core_copies[k].wait()
        quad = part[pl.ds(z * 4, 4)] + from_core[pl.ds(z * 4, 4)].astype(F32)
        part[pl.ds(z * 4, 4)] = quad
        quad16[k] = quad.astype(BF16)
        for j, p in enumerate(plane):
            i = k * 3 + j
            copy = remote(quad16.at[k, p], from_plane.at[k, j], plane_send.at[i], plane_recv.at[i], at(dp, p, core))
            copy.start()
            plane_copies.append(copy)

    def summed_plane(k, z):
        for j in range(3):
            plane_copies[k * 3 + j].wait()
        sums = from_plane[k].astype(F32)
        return part[z * 4 + chip] + sums[0] + sums[1] + sums[2]

    z_copies = []

    def pass_to_z(k):
        own16[k] = summed_plane(k, z_order[k]).astype(BF16)
        copy = remote(own16.at[k], from_z.at[dp], z_send.at[k], z_recv.at[dp], at(z_order[k], chip, core))
        copy.start()
        z_copies.append(copy)

    loads[6].wait()
    du = jnp.zeros((ROWS, CH), F32)
    for k in range(3):
        du = du + dot(g_ext[(2 - k) * PIX : (2 - k) * PIX + ROWS], wt[:, k * CH : (k + 1) * CH], 1, 0)
    back_t = (sig_y * (1.0 + y * (1.0 - sig_y)) * du).astype(BF16).astype(F32)
    dy = jnp.where(live, (g + back_t).astype(BF16).astype(F32), 0.0)

    stage_shifts(dy, line, padded)

    def taps_of(row):
        total = jnp.zeros((ROWS, CH), F32)
        for tap in range(3 * row, 3 * row + 3):
            total = total + dot(
                shifted(padded, 2 - tap % 3, 2 - tap // 3), ws[:, tap * CH : (tap + 1) * CH], 1, 0
            )
        return total

    pass_to_z(0)
    da = taps_of(0)
    pass_to_z(1)
    da = da + taps_of(1)
    pass_to_z(2)
    total = summed_plane(3, dp)
    da = da + taps_of(2)

    def chunk_of(core_id, z, chip_id):
        return core_id * 16 + z * 4 + chip_id

    mine = chunk_of(core, dp, chip)
    for z in near:
        remote(from_z.at[z], from_z.at[z], z_send.at[0], z_recv.at[z], partner).wait_recv()
        total = total + from_z[z].astype(F32)
    full[mine] = total.astype(BF16)

    sent = []

    def pass_on(chunk, device, recv_sem):
        copy = remote(full.at[chunk], full.at[chunk], gather_send.at[len(sent)], recv_sem, device)
        copy.start()
        sent.append(copy)

    def await_chunk(chunk, recv_sem):
        remote(full.at[chunk], full.at[chunk], gather_send.at[0], recv_sem, partner).wait_recv()

    for z in far:
        pass_on(mine, at(z, chip, core), gather_z.at[dp])
    for j, p in enumerate(plane):
        pass_on(mine, at(dp, p, core), gather_plane.at[dp * 3 + j])

    dhat = da * (sig_n * (1.0 + normed * (1.0 - sig_n))) * gain
    dhat_frames = [frame_of(dhat, s) for s in range(CAP)]
    xhat_frames = [frame_of(xhat, s) for s in range(CAP)]
    mean_d = group_means([column_sum(v) for v in dhat_frames], members)
    mean_dx = group_means([column_sum(v * w) for v, w in zip(dhat_frames, xhat_frames)], members)
    dx = jnp.concatenate(
        [
            inverse[s : s + 1] * (dhat_frames[s] - mean_d[s : s + 1] - xhat_frames[s] * mean_dx[s : s + 1])
            for s in range(CAP)
        ],
        axis=0,
    )
    out_ref[...] = jnp.where(live, dy + dx, 0.0).astype(BF16)

    for z in near:
        chunk = chunk_of(core, z, chip)
        await_chunk(chunk, gather_z.at[z])
        for j, p in enumerate(plane):
            pass_on(chunk, at(dp, p, core), gather_plane.at[z * 3 + j])
    for z in [dp] + near:
        for j, p in enumerate(plane):
            await_chunk(chunk_of(core, z, p), gather_plane.at[z * 3 + j])
        pass_on(pl.ds(chunk_of(core, z, 0), 4), partner, gather_core.at[z])

    scale = 1.0 / math.sqrt(4 * 2 * 8 * PIX)

    def put(half):
        for r in range(2):
            rows = pl.ds(pl.multiple_of(half * 2 * BLOCK + r * BLOCK, 8), BLOCK)
            for l in range(UNITS):
                width = min(LANE, 3 * CH - l * LANE)
                value = full[half * 16 + r * UNITS + l].astype(F32) * scale
                grad_ref[rows, l * LANE : l * LANE + width] = value[:, :width]

    put(core)
    for z in [dp] + near:
        await_chunk(pl.ds(chunk_of(1 - core, z, 0), 4), gather_core.at[z])
    put(1 - core)
    for copy in z_copies + sent:
        copy.wait_send()


def fused_shards(frames_in, cotangent, counts, norm_gain, norm_shift, spatial_weight, temporal_weight):
    vmem = pl.BlockSpec(memory_space=pltpu.VMEM)
    hbm = pl.BlockSpec(memory_space=pltpu.HBM)
    dma = pltpu.SemaphoreType.DMA
    out, grad = pl.pallas_call(
        fused_kernel,
        out_shape=(
            pltpu.VMEM((ROWS, CH), BF16),
            pltpu.VMEM((CH, 3 * CH), F32),
        ),
        in_specs=[hbm] * 7,
        out_specs=(vmem, vmem),
        scratch_shapes=[
            pltpu.SMEM((1, 8), jnp.int32),
            pltpu.VMEM((ROWS, CH), BF16),
            pltpu.VMEM((ROWS, CH), BF16),
            pltpu.VMEM((CH,), F32),
            pltpu.VMEM((CH,), F32),
            pltpu.VMEM((CH, 9 * CH), BF16),
            pltpu.VMEM((CH, 3 * CH), BF16),
            pltpu.VMEM((ROWS + 16, CH), F32),
            pltpu.VMEM((3, CAP, SIDE + 2, SIDE, CH), F32),
            pltpu.VMEM((2, PIX, CH), BF16),
            pltpu.VMEM((2, PIX, CH), BF16),
            pltpu.VMEM((CH, (CAP + 2) * PIX), BF16),
            pltpu.VMEM((16, BLOCK, LANE), F32),
            pltpu.VMEM((16, BLOCK, LANE), BF16),
            pltpu.VMEM((16, BLOCK, LANE), BF16),
            pltpu.VMEM((4, 4, BLOCK, LANE), BF16),
            pltpu.VMEM((4, 3, BLOCK, LANE), BF16),
            pltpu.VMEM((3, BLOCK, LANE), BF16),
            pltpu.VMEM((4, BLOCK, LANE), BF16),
            pltpu.VMEM((CHUNKS, BLOCK, LANE), BF16),
            dma((7,)), dma((2,)), dma((2,)), dma((4,)), dma((4,)), dma((12,)), dma((12,)), dma((3,)), dma((4,)),
            dma((19,)), dma((4,)), dma((12,)), dma((4,)),
        ],
        compiler_params=pltpu.CompilerParams(
            collective_id=0, has_side_effects=True, vmem_limit_bytes=60 * 1024 * 1024
        ),
    )(
        counts,
        frames_in.reshape(ROWS, CH),
        cotangent.reshape(ROWS, CH),
        norm_gain,
        norm_shift,
        spatial_weight.T,
        temporal_weight.T,
    )
    return out.reshape(frames_in.shape), grad.T


def solution(mesh):
    fused = mesh.shape["dp"] == 4 and mesh.shape["tm"] == 8

    def block(frames_in, *rest):
        if fused and frames_in.shape == (1, CAP, SIDE, SIDE, CH):
            return fused_shards(frames_in, *rest)
        return shards(frames_in, *rest)

    return jax.shard_map(
        block,
        mesh=mesh,
        in_specs=(
            P("dp", "tm", None, None, None),
            P("dp", "tm", None, None, None),
            P("dp", None),
            P(),
            P(),
            P(),
            P(),
        ),
        out_specs=(P("dp", "tm", None, None, None), P()),
        check_vma=False,
    )
```

```python
import math

import jax
import jax.numpy as jnp
from jax import lax
from jax.experimental import pallas as pl
from jax.experimental.pallas import tpu as pltpu
from jax.sharding import PartitionSpec as P

GROUPS = 32


def norm_act(values, gain, shift, groups):
    nframes, height, width, channels = values.shape
    per_group = channels // groups
    entries = height * width * per_group

    def group_mean(totals):
        summed = totals.reshape(nframes, groups, per_group).sum(axis=2) / entries
        return jnp.repeat(summed, per_group, axis=1).reshape(nframes, 1, 1, channels)

    centre = group_mean(values.sum(axis=(1, 2)))
    centred = values - centre
    spread = group_mean((centred * centred).sum(axis=(1, 2)))
    normed = centred * lax.rsqrt(spread + 1e-05) * gain + shift
    return jax.nn.silu(normed)


def patches(field):
    height, width = (field.shape[1], field.shape[2])
    padded = jnp.pad(field, ((0, 0), (1, 1), (1, 1), (0, 0)))
    pieces = [
        padded[:, row_off : row_off + height, col_off : col_off + width, :]
        for row_off in range(3)
        for col_off in range(3)
    ]
    return jnp.concatenate(pieces, axis=3)


def spatial_conv(field, weight):
    stacked = patches(field)
    leading = stacked.shape[:3]
    product = jnp.dot(
        stacked.reshape(-1, stacked.shape[3]), weight, preferred_element_type=jnp.float32
    )
    return product.reshape(leading + (weight.shape[1],))


def spatial_conv_t(field, weight):
    channels = weight.shape[1]
    flipped = (
        weight.reshape(9, -1, channels)[::-1].transpose(0, 2, 1).reshape(-1, weight.shape[0] // 9)
    )
    return spatial_conv(field, flipped)


def silu_grad(values):
    sigma = jax.nn.sigmoid(values)
    return sigma * (1.0 + values * (1.0 - sigma))


def temporal_core(y_ext, g_ext, weight):
    nframes = y_ext.shape[0] - 2
    channels = weight.shape[1]
    units = jax.nn.silu(y_ext.astype(jnp.float32)).astype(jnp.bfloat16)
    g_middle = g_ext[1:-1]
    g_mid = g_middle.reshape(-1, channels)
    grads = []
    back_sum = jnp.zeros((g_mid.shape[0], channels), jnp.float32)
    for tap_k in range(3):
        taken = units[tap_k : tap_k + nframes].reshape(-1, channels)
        grads.append(
            lax.dot_general(
                taken, g_mid, (((0,), (0,)), ((), ())), preferred_element_type=jnp.float32
            )
        )
        tap_weight = weight[tap_k * channels : (tap_k + 1) * channels]
        source = g_ext[2 - tap_k : 2 - tap_k + nframes].reshape(-1, channels)
        back_sum = back_sum + lax.dot_general(
            source, tap_weight, (((1,), (1,)), ((), ())), preferred_element_type=jnp.float32
        )
    middle = y_ext[1:-1]
    back_t = (silu_grad(middle.astype(jnp.float32)) * back_sum.reshape(middle.shape)).astype(
        jnp.bfloat16
    )
    return (back_t, jnp.concatenate(grads, axis=0))


def frame_slots(counts_row, nframes, cap):
    ndevices = counts_row.shape[0]
    ends = jnp.cumsum(counts_row)
    starts = ends - counts_row
    frame_ids = jnp.arange(nframes, dtype=jnp.int32)
    owner = jnp.sum((ends[None, :] <= frame_ids[:, None]).astype(jnp.int32), axis=1)
    device_ids = jnp.arange(ndevices, dtype=jnp.int32)
    first = jnp.sum(jnp.where(device_ids[None, :] == owner[:, None], starts[None, :], 0), axis=1)
    return owner * cap + frame_ids - first


def slot_frames(counts_row, cap):
    ndevices = counts_row.shape[0]
    ends = jnp.cumsum(counts_row)
    starts = ends - counts_row
    slot_ids = jnp.arange(ndevices * cap, dtype=jnp.int32)
    device = slot_ids // cap
    inner = slot_ids % cap
    device_ids = jnp.arange(ndevices, dtype=jnp.int32)
    onehot = device[:, None] == device_ids[None, :]
    held = jnp.sum(jnp.where(onehot, counts_row[None, :], 0), axis=1)
    first = jnp.sum(jnp.where(onehot, starts[None, :], 0), axis=1)
    live = inner < held
    return (jnp.where(live, first + inner, 0), live)


def shards(frames_in, cotangent, counts, norm_gain, norm_shift, spatial_weight, temporal_weight):
    inputs = frames_in[0]
    cotan = cotangent[0]
    counts_row = counts[0]
    cap = inputs.shape[0]
    tm_size = lax.axis_size("tm")
    own_count = jnp.sum(
        jnp.where(jnp.arange(tm_size, dtype=jnp.int32) == lax.axis_index("tm"), counts_row, 0)
    )
    live_slots = (jnp.arange(cap, dtype=jnp.int32) < own_count)[:, None, None, None]

    def activate(values):
        return norm_act(values, norm_gain, norm_shift, GROUPS)

    inputs_f = inputs.astype(jnp.float32)
    act_f, act_back = jax.vjp(activate, inputs_f)
    acts = act_f.astype(jnp.bfloat16)
    mixed = spatial_conv(acts, spatial_weight)
    y_out = (inputs_f + mixed).astype(jnp.bfloat16)
    y_rows, g_rows = (
        lax.all_to_all(y_out, "tm", split_axis=1, concat_axis=0, tiled=True),
        lax.all_to_all(cotan, "tm", split_axis=1, concat_axis=0, tiled=True),
    )
    pick = frame_slots(counts_row, 2 * tm_size, cap)
    pad_spec = ((1, 1), (0, 0), (0, 0), (0, 0))
    y_ext = jnp.pad(jnp.take(y_rows, pick, axis=0), pad_spec)
    g_ext = jnp.pad(jnp.take(g_rows, pick, axis=0), pad_spec)
    back_rows, grad_part = temporal_core(y_ext, g_ext, temporal_weight)
    back_idx, live = slot_frames(counts_row, cap)
    back_slots = jnp.where(
        live[:, None, None, None],
        jnp.take(back_rows, back_idx, axis=0),
        jnp.zeros((), jnp.bfloat16),
    )
    back_t = lax.all_to_all(back_slots, "tm", split_axis=0, concat_axis=1, tiled=True)
    d_out = (cotan.astype(jnp.float32) + back_t.astype(jnp.float32)).astype(jnp.bfloat16)
    d_act = spatial_conv_t(d_out, spatial_weight)
    d_in = d_out.astype(jnp.float32) + act_back(d_act)[0]
    d_in = jnp.where(live_slots, d_in, 0.0).astype(jnp.bfloat16)
    height, width = (inputs.shape[1], inputs.shape[2])
    scale = 1.0 / math.sqrt(lax.axis_size("dp") * 2 * tm_size * height * width)
    summed = lax.psum(grad_part, ("dp", "tm"))
    return (d_in[None], summed * scale)


CAP = 3
SIDE = 8
CH = 320
PIX = SIDE * SIDE
ROWS = CAP * PIX
LANE = 128
UNITS = 8
BLOCK = 80
CHUNKS = 32
F32 = jnp.float32
BF16 = jnp.bfloat16


def dot(a, b, ca, cb):
    return lax.dot_general(a, b, (((ca,), (cb,)), ((), ())), preferred_element_type=F32)


def group_matrix():
    def ids(axis):
        index = lax.broadcasted_iota(jnp.int32, (CH, CH), axis).astype(F32)
        return jnp.floor((index + 0.5) * (GROUPS / CH))

    return (ids(0) == ids(1)).astype(BF16)


def group_means(totals, members):
    rows = jnp.concatenate(totals, axis=0)
    high = rows.astype(BF16)
    rest = rows - high.astype(F32)
    mid = rest.astype(BF16)
    low = (rest - mid.astype(F32)).astype(BF16)
    summed = dot(high, members, 1, 0) + dot(mid, members, 1, 0) + dot(low, members, 1, 0)
    return summed * (1.0 / (PIX * (CH // GROUPS)))


def frame_of(value, frame):
    return value[frame * PIX : (frame + 1) * PIX]


def column_sum(value):
    return jnp.sum(value, axis=0, keepdims=True)


def sigmoid(value):
    return 1.0 / (1.0 + jnp.exp(-value))


def stage_shifts(value, line, padded):
    column = lax.broadcasted_iota(jnp.int32, (ROWS, CH), 0) & (SIDE - 1)
    line[8 : 8 + ROWS, :] = value
    left = jnp.where(column == 0, 0.0, line[7 : 7 + ROWS, :])
    right = jnp.where(column == SIDE - 1, 0.0, line[9 : 9 + ROWS, :])
    for j, moved in enumerate((left, value, right)):
        padded[j, :, 1 : 1 + SIDE] = moved.reshape(CAP, SIDE, SIDE, CH)


def turned_patches(value):
    wide = jnp.concatenate([value, jnp.zeros((64, CH), F32)], axis=0).T
    pixel = lax.broadcasted_iota(jnp.int32, (1, wide.shape[1]), 1)
    row, column = (pixel & (PIX - 1)) >> 3, pixel & (SIDE - 1)
    pieces = []
    for i in (-1, 0, 1):
        for j in (-1, 0, 1):
            move = (-(i * SIDE + j)) % wide.shape[1]
            moved = pltpu.roll(wide, move, 1) if move else wide
            inside = (row + i >= 0) & (row + i < SIDE) & (column + j >= 0) & (column + j < SIDE)
            pieces.append((moved * inside.astype(F32)).astype(BF16))
    return jnp.concatenate(pieces, axis=0)


def shifted(padded, j, i):
    return padded[j, :, i : i + SIDE].reshape(ROWS, CH).astype(BF16)


def fused_kernel(
    counts_hbm, x_hbm, g_hbm, gain_hbm, shift_hbm, ws_hbm, wt_hbm, out_ref, grad_ref,
    counts, x_ref, g_ref, gain_ref, shift_ref, ws, wt, line, padded, edge, halo, turned, part, part16, from_core, quad16, from_first, second16, from_second, own16, from_z, full,
    weight_sem, halo_send, halo_recv, core_send, core_recv, plane_send, plane_recv, z_send, z_recv,
    gather_send, gather_z, gather_plane, gather_core,
):
    dp = lax.axis_index("dp")
    tm = lax.axis_index("tm")
    yy, xx, core = tm // 4, (tm // 2) % 2, tm % 2
    chip = tm // 2

    def at(z, chip_id, core_id):
        return (z, chip_id * 2 + core_id)

    plane = [yy * 2 + (1 - xx), (1 - yy) * 2 + xx, (1 - yy) * 2 + (1 - xx)]
    near = [dp + 1 - 2 * (dp % 2), 2 - dp // 2, 3 - 3 * (dp // 2)]
    far = near[::-1]
    before, after = lax.rem(tm + 7, 8), lax.rem(tm + 1, 8)
    partner = at(dp, chip, 1 - core)
    peers = [(dp, before), (dp, after)] + [at(dp, p, core) for p in plane] + [at(z, chip, core) for z in near]

    def remote(src, dst, send_sem, recv_sem, device):
        copy = pltpu.make_async_remote_copy(
            src_ref=src, dst_ref=dst, send_sem=send_sem, recv_sem=recv_sem,
            device_id=device, device_id_type=pl.DeviceIdType.MESH,
        )
        return copy

    barrier = pltpu.get_barrier_semaphore()
    for peer in peers:
        pl.semaphore_signal(barrier, inc=1, device_id=peer, device_id_type=pl.DeviceIdType.MESH)
    places = [
        (g_hbm, g_ref), (counts_hbm, counts), (x_hbm, x_ref), (gain_hbm, gain_ref), (shift_hbm, shift_ref),
        (ws_hbm, ws), (wt_hbm, wt),
    ]
    loads = [pltpu.make_async_copy(src, dst, weight_sem.at[i]) for i, (src, dst) in enumerate(places)]
    for load in loads:
        load.start()
    members = group_matrix()
    for load in loads[:2]:
        load.wait()

    count = counts[0, tm]
    g = g_ref[...].astype(F32)
    g_frames = [frame_of(g, s) for s in range(CAP)]
    last = jnp.where(count == 3, g_frames[2], jnp.where(count == 2, g_frames[1], g_frames[0]))
    edge[0] = g_frames[0].astype(BF16)
    edge[1] = last.astype(BF16)
    halo_copies = [
        remote(edge.at[0], halo.at[1], halo_send.at[0], halo_recv.at[1], (dp, before)),
        remote(edge.at[1], halo.at[0], halo_send.at[1], halo_recv.at[0], (dp, after)),
    ]
    pl.semaphore_wait(barrier, len(peers))
    for copy in halo_copies:
        copy.start()
    for load in loads[2:5]:
        load.wait()

    gain, shift = gain_ref[...].reshape(1, CH), shift_ref[...].reshape(1, CH)
    x = x_ref[...].astype(F32)
    x_frames = [frame_of(x, s) for s in range(CAP)]
    means = group_means([column_sum(v) for v in x_frames], members)
    centred = [v - means[s : s + 1] for s, v in enumerate(x_frames)]
    spread = group_means([column_sum(v * v) for v in centred], members)
    inverse = lax.rsqrt(spread + 1e-05)
    xhat = jnp.concatenate([v * inverse[s : s + 1] for s, v in enumerate(centred)], axis=0)
    normed = xhat * gain + shift
    sig_n = sigmoid(normed)
    padded[...] = jnp.zeros_like(padded)
    patched = turned_patches(normed * sig_n)
    for copy in halo_copies:
        copy.wait()
    prev_edge = jnp.where(tm == 0, 0.0, halo[0].astype(F32))
    next_edge = jnp.where(tm == 7, 0.0, halo[1].astype(F32))
    g_ext = jnp.concatenate(
        [
            prev_edge,
            g_frames[0],
            jnp.where(count == 1, next_edge, g_frames[1]),
            jnp.where(count == 2, next_edge, g_frames[2]),
            next_edge,
        ],
        axis=0,
    )
    turned[...] = g_ext.T.astype(BF16)
    g_ext = g_ext.astype(BF16)

    loads[5].wait()
    mixed = dot(ws[...], patched, 1, 0).T[:ROWS]
    y = (x + mixed).astype(BF16).astype(F32)
    sig_y = sigmoid(y)
    live = lax.broadcasted_iota(jnp.int32, (ROWS, CH), 0) < count * PIX
    u = jnp.where(live, y * sig_y, 0.0).astype(BF16)

    none = jnp.zeros((ROWS, 64), BF16)
    u_low = jnp.concatenate([u, none], axis=1)
    u_high = jnp.concatenate([none, u], axis=1)

    def below(value, frames):
        zero = jnp.zeros((PIX, value.shape[1]), BF16)
        return jnp.concatenate([zero] * frames + [value] + [zero] * (2 - frames), axis=0)

    first_tap, second_tap, third_tap = below(u_low, 2), below(u_high, 1), below(u_low, 0)

    def gradient_half(half):
        rows = turned[pl.ds(pl.multiple_of(half * 2 * BLOCK, 16), 2 * BLOCK), :]
        t0, t1, t2 = dot(rows, first_tap, 1, 0), dot(rows, second_tap, 1, 0), dot(rows, third_tap, 1, 0)
        units = [
            t0[:, 0:128], t0[:, 128:256], t0[:, 256:384] + t1[:, 0:128], t1[:, 128:256], t1[:, 256:384],
            t2[:, 0:128], t2[:, 128:256], t2[:, 256:384],
        ]
        return [(r * UNITS + l, units[l][r * BLOCK : (r + 1) * BLOCK]) for r in range(2) for l in range(UNITS)]

    for i, piece in gradient_half(1 - core):
        part16[i] = piece.astype(BF16)
    z_order = far + [dp]
    core_copies = [
        remote(
            part16.at[pl.ds(z * 4, 4)], from_core.at[pl.ds(z * 4, 4)], core_send.at[k], core_recv.at[k], partner
        )
        for k, z in enumerate(z_order)
    ]
    for copy in core_copies:
        copy.start()
    for i, piece in gradient_half(core):
        part[i] = piece

    routes = [(plane[k % 2], plane[1 - k % 2]) for k in range(4)]
    first_copies, second_copies = [], []
    for k, z in enumerate(z_order):
        core_copies[k].wait()
        part[pl.ds(z * 4, 4)] = part[pl.ds(z * 4, 4)] + from_core[pl.ds(z * 4, 4)].astype(F32)
        quad16[k, 0] = part[z * 4 + routes[k][0]].astype(BF16)
        quad16[k, 1] = part[z * 4 + plane[2]].astype(BF16)
        copy = remote(
            quad16.at[k], from_first.at[k], plane_send.at[k], plane_recv.at[k], at(dp, routes[k][0], core)
        )
        copy.start()
        first_copies.append(copy)

    def second_step(k):
        first_copies[k].wait()
        second16[k] = (part[z_order[k] * 4 + routes[k][1]] + from_first[k, 1].astype(F32)).astype(BF16)
        copy = remote(
            second16.at[k], from_second.at[k], plane_send.at[4 + k], plane_recv.at[4 + k],
            at(dp, routes[k][1], core),
        )
        copy.start()
        second_copies.append(copy)

    def summed_plane(k, z):
        second_copies[k].wait()
        return part[z * 4 + chip] + from_first[k, 0].astype(F32) + from_second[k].astype(F32)

    second_step(0)
    second_step(1)

    z_copies = []

    def pass_to_z(k):
        own16[k] = summed_plane(k, z_order[k]).astype(BF16)
        copy = remote(own16.at[k], from_z.at[dp], z_send.at[k], z_recv.at[dp], at(z_order[k], chip, core))
        copy.start()
        z_copies.append(copy)

    loads[6].wait()
    du = jnp.zeros((ROWS, CH), F32)
    for k in range(3):
        du = du + dot(g_ext[(2 - k) * PIX : (2 - k) * PIX + ROWS], wt[:, k * CH : (k + 1) * CH], 1, 0)
    back_t = (sig_y * (1.0 + y * (1.0 - sig_y)) * du).astype(BF16).astype(F32)
    dy = jnp.where(live, (g + back_t).astype(BF16).astype(F32), 0.0)

    stage_shifts(dy, line, padded)
    second_step(2)
    second_step(3)

    def taps_of(row):
        total = jnp.zeros((ROWS, CH), F32)
        for tap in range(3 * row, 3 * row + 3):
            total = total + dot(
                shifted(padded, 2 - tap % 3, 2 - tap // 3), ws[:, tap * CH : (tap + 1) * CH], 1, 0
            )
        return total

    pass_to_z(0)
    da = taps_of(0)
    pass_to_z(1)
    da = da + taps_of(1)
    pass_to_z(2)
    total = summed_plane(3, dp)
    da = da + taps_of(2)

    def chunk_of(core_id, z, chip_id):
        return core_id * 16 + z * 4 + chip_id

    mine = chunk_of(core, dp, chip)
    for z in near:
        remote(from_z.at[z], from_z.at[z], z_send.at[0], z_recv.at[z], partner).wait_recv()
        total = total + from_z[z].astype(F32)
    full[mine] = total.astype(BF16)

    sent = []

    def pass_on(chunk, device, recv_sem):
        copy = remote(full.at[chunk], full.at[chunk], gather_send.at[len(sent)], recv_sem, device)
        copy.start()
        sent.append(copy)

    def await_chunk(chunk, recv_sem):
        remote(full.at[chunk], full.at[chunk], gather_send.at[0], recv_sem, partner).wait_recv()

    for z in far:
        pass_on(mine, at(z, chip, core), gather_z.at[dp])
    for j, p in enumerate(plane[:2]):
        pass_on(mine, at(dp, p, core), gather_plane.at[dp * 3 + j])

    dhat = da * (sig_n * (1.0 + normed * (1.0 - sig_n))) * gain
    dhat_frames = [frame_of(dhat, s) for s in range(CAP)]
    xhat_frames = [frame_of(xhat, s) for s in range(CAP)]
    mean_d = group_means([column_sum(v) for v in dhat_frames], members)
    mean_dx = group_means([column_sum(v * w) for v, w in zip(dhat_frames, xhat_frames)], members)
    dx = jnp.concatenate(
        [
            inverse[s : s + 1] * (dhat_frames[s] - mean_d[s : s + 1] - xhat_frames[s] * mean_dx[s : s + 1])
            for s in range(CAP)
        ],
        axis=0,
    )
    out_ref[...] = jnp.where(live, dy + dx, 0.0).astype(BF16)

    for z in near:
        chunk = chunk_of(core, z, chip)
        await_chunk(chunk, gather_z.at[z])
        for j, p in enumerate(plane[:2]):
            pass_on(chunk, at(dp, p, core), gather_plane.at[z * 3 + j])
    for k, z in enumerate([dp] + near):
        for j, p in enumerate(plane[:2]):
            await_chunk(chunk_of(core, z, p), gather_plane.at[z * 3 + j])
        pass_on(chunk_of(core, z, plane[k % 2]), at(dp, plane[1 - k % 2], core), gather_plane.at[z * 3 + 2])
    for z in [dp] + near:
        await_chunk(chunk_of(core, z, plane[2]), gather_plane.at[z * 3 + 2])
        pass_on(pl.ds(chunk_of(core, z, 0), 4), partner, gather_core.at[z])

    scale = 1.0 / math.sqrt(4 * 2 * 8 * PIX)

    def put(half):
        for r in range(2):
            rows = pl.ds(pl.multiple_of(half * 2 * BLOCK + r * BLOCK, 8), BLOCK)
            for l in range(UNITS):
                width = min(LANE, 3 * CH - l * LANE)
                value = full[half * 16 + r * UNITS + l].astype(F32) * scale
                grad_ref[rows, l * LANE : l * LANE + width] = value[:, :width]

    put(core)
    for z in [dp] + near:
        await_chunk(pl.ds(chunk_of(1 - core, z, 0), 4), gather_core.at[z])
    put(1 - core)
    for copy in z_copies + sent:
        copy.wait_send()


def fused_shards(frames_in, cotangent, counts, norm_gain, norm_shift, spatial_weight, temporal_weight):
    vmem = pl.BlockSpec(memory_space=pltpu.VMEM)
    hbm = pl.BlockSpec(memory_space=pltpu.HBM)
    dma = pltpu.SemaphoreType.DMA
    out, grad = pl.pallas_call(
        fused_kernel,
        out_shape=(
            pltpu.VMEM((ROWS, CH), BF16),
            pltpu.VMEM((CH, 3 * CH), F32),
        ),
        in_specs=[hbm] * 7,
        out_specs=(vmem, vmem),
        scratch_shapes=[
            pltpu.SMEM((1, 8), jnp.int32),
            pltpu.VMEM((ROWS, CH), BF16),
            pltpu.VMEM((ROWS, CH), BF16),
            pltpu.VMEM((CH,), F32),
            pltpu.VMEM((CH,), F32),
            pltpu.VMEM((CH, 9 * CH), BF16),
            pltpu.VMEM((CH, 3 * CH), BF16),
            pltpu.VMEM((ROWS + 16, CH), F32),
            pltpu.VMEM((3, CAP, SIDE + 2, SIDE, CH), F32),
            pltpu.VMEM((2, PIX, CH), BF16),
            pltpu.VMEM((2, PIX, CH), BF16),
            pltpu.VMEM((CH, (CAP + 2) * PIX), BF16),
            pltpu.VMEM((16, BLOCK, LANE), F32),
            pltpu.VMEM((16, BLOCK, LANE), BF16),
            pltpu.VMEM((16, BLOCK, LANE), BF16),
            pltpu.VMEM((4, 2, BLOCK, LANE), BF16),
            pltpu.VMEM((4, 2, BLOCK, LANE), BF16),
            pltpu.VMEM((4, BLOCK, LANE), BF16),
            pltpu.VMEM((4, BLOCK, LANE), BF16),
            pltpu.VMEM((3, BLOCK, LANE), BF16),
            pltpu.VMEM((4, BLOCK, LANE), BF16),
            pltpu.VMEM((CHUNKS, BLOCK, LANE), BF16),
            dma((7,)), dma((2,)), dma((2,)), dma((4,)), dma((4,)), dma((8,)), dma((8,)), dma((3,)), dma((4,)),
            dma((19,)), dma((4,)), dma((12,)), dma((4,)),
        ],
        compiler_params=pltpu.CompilerParams(
            collective_id=0, has_side_effects=True, vmem_limit_bytes=60 * 1024 * 1024
        ),
    )(
        counts,
        frames_in.reshape(ROWS, CH),
        cotangent.reshape(ROWS, CH),
        norm_gain,
        norm_shift,
        spatial_weight.T,
        temporal_weight.T,
    )
    return out.reshape(frames_in.shape), grad.T


def solution(mesh):
    fused = mesh.shape["dp"] == 4 and mesh.shape["tm"] == 8

    def block(frames_in, *rest):
        if fused and frames_in.shape == (1, CAP, SIDE, SIDE, CH):
            return fused_shards(frames_in, *rest)
        return shards(frames_in, *rest)

    return jax.shard_map(
        block,
        mesh=mesh,
        in_specs=(
            P("dp", "tm", None, None, None),
            P("dp", "tm", None, None, None),
            P("dp", None),
            P(),
            P(),
            P(),
            P(),
        ),
        out_specs=(P("dp", "tm", None, None, None), P()),
        check_vma=False,
    )
```

```python
import math

import jax
import jax.numpy as jnp
from jax import lax
from jax.experimental import pallas as pl
from jax.experimental.pallas import tpu as pltpu
from jax.sharding import PartitionSpec as P

GROUPS = 32


def norm_act(values, gain, shift, groups):
    nframes, height, width, channels = values.shape
    per_group = channels // groups
    entries = height * width * per_group

    def group_mean(totals):
        summed = totals.reshape(nframes, groups, per_group).sum(axis=2) / entries
        return jnp.repeat(summed, per_group, axis=1).reshape(nframes, 1, 1, channels)

    centre = group_mean(values.sum(axis=(1, 2)))
    centred = values - centre
    spread = group_mean((centred * centred).sum(axis=(1, 2)))
    normed = centred * lax.rsqrt(spread + 1e-05) * gain + shift
    return jax.nn.silu(normed)


def patches(field):
    height, width = (field.shape[1], field.shape[2])
    padded = jnp.pad(field, ((0, 0), (1, 1), (1, 1), (0, 0)))
    pieces = [
        padded[:, row_off : row_off + height, col_off : col_off + width, :]
        for row_off in range(3)
        for col_off in range(3)
    ]
    return jnp.concatenate(pieces, axis=3)


def spatial_conv(field, weight):
    stacked = patches(field)
    leading = stacked.shape[:3]
    product = jnp.dot(
        stacked.reshape(-1, stacked.shape[3]), weight, preferred_element_type=jnp.float32
    )
    return product.reshape(leading + (weight.shape[1],))


def spatial_conv_t(field, weight):
    channels = weight.shape[1]
    flipped = (
        weight.reshape(9, -1, channels)[::-1].transpose(0, 2, 1).reshape(-1, weight.shape[0] // 9)
    )
    return spatial_conv(field, flipped)


def silu_grad(values):
    sigma = jax.nn.sigmoid(values)
    return sigma * (1.0 + values * (1.0 - sigma))


def temporal_core(y_ext, g_ext, weight):
    nframes = y_ext.shape[0] - 2
    channels = weight.shape[1]
    units = jax.nn.silu(y_ext.astype(jnp.float32)).astype(jnp.bfloat16)
    g_middle = g_ext[1:-1]
    g_mid = g_middle.reshape(-1, channels)
    grads = []
    back_sum = jnp.zeros((g_mid.shape[0], channels), jnp.float32)
    for tap_k in range(3):
        taken = units[tap_k : tap_k + nframes].reshape(-1, channels)
        grads.append(
            lax.dot_general(
                taken, g_mid, (((0,), (0,)), ((), ())), preferred_element_type=jnp.float32
            )
        )
        tap_weight = weight[tap_k * channels : (tap_k + 1) * channels]
        source = g_ext[2 - tap_k : 2 - tap_k + nframes].reshape(-1, channels)
        back_sum = back_sum + lax.dot_general(
            source, tap_weight, (((1,), (1,)), ((), ())), preferred_element_type=jnp.float32
        )
    middle = y_ext[1:-1]
    back_t = (silu_grad(middle.astype(jnp.float32)) * back_sum.reshape(middle.shape)).astype(
        jnp.bfloat16
    )
    return (back_t, jnp.concatenate(grads, axis=0))


def frame_slots(counts_row, nframes, cap):
    ndevices = counts_row.shape[0]
    ends = jnp.cumsum(counts_row)
    starts = ends - counts_row
    frame_ids = jnp.arange(nframes, dtype=jnp.int32)
    owner = jnp.sum((ends[None, :] <= frame_ids[:, None]).astype(jnp.int32), axis=1)
    device_ids = jnp.arange(ndevices, dtype=jnp.int32)
    first = jnp.sum(jnp.where(device_ids[None, :] == owner[:, None], starts[None, :], 0), axis=1)
    return owner * cap + frame_ids - first


def slot_frames(counts_row, cap):
    ndevices = counts_row.shape[0]
    ends = jnp.cumsum(counts_row)
    starts = ends - counts_row
    slot_ids = jnp.arange(ndevices * cap, dtype=jnp.int32)
    device = slot_ids // cap
    inner = slot_ids % cap
    device_ids = jnp.arange(ndevices, dtype=jnp.int32)
    onehot = device[:, None] == device_ids[None, :]
    held = jnp.sum(jnp.where(onehot, counts_row[None, :], 0), axis=1)
    first = jnp.sum(jnp.where(onehot, starts[None, :], 0), axis=1)
    live = inner < held
    return (jnp.where(live, first + inner, 0), live)


def shards(frames_in, cotangent, counts, norm_gain, norm_shift, spatial_weight, temporal_weight):
    inputs = frames_in[0]
    cotan = cotangent[0]
    counts_row = counts[0]
    cap = inputs.shape[0]
    tm_size = lax.axis_size("tm")
    own_count = jnp.sum(
        jnp.where(jnp.arange(tm_size, dtype=jnp.int32) == lax.axis_index("tm"), counts_row, 0)
    )
    live_slots = (jnp.arange(cap, dtype=jnp.int32) < own_count)[:, None, None, None]

    def activate(values):
        return norm_act(values, norm_gain, norm_shift, GROUPS)

    inputs_f = inputs.astype(jnp.float32)
    act_f, act_back = jax.vjp(activate, inputs_f)
    acts = act_f.astype(jnp.bfloat16)
    mixed = spatial_conv(acts, spatial_weight)
    y_out = (inputs_f + mixed).astype(jnp.bfloat16)
    y_rows, g_rows = (
        lax.all_to_all(y_out, "tm", split_axis=1, concat_axis=0, tiled=True),
        lax.all_to_all(cotan, "tm", split_axis=1, concat_axis=0, tiled=True),
    )
    pick = frame_slots(counts_row, 2 * tm_size, cap)
    pad_spec = ((1, 1), (0, 0), (0, 0), (0, 0))
    y_ext = jnp.pad(jnp.take(y_rows, pick, axis=0), pad_spec)
    g_ext = jnp.pad(jnp.take(g_rows, pick, axis=0), pad_spec)
    back_rows, grad_part = temporal_core(y_ext, g_ext, temporal_weight)
    back_idx, live = slot_frames(counts_row, cap)
    back_slots = jnp.where(
        live[:, None, None, None],
        jnp.take(back_rows, back_idx, axis=0),
        jnp.zeros((), jnp.bfloat16),
    )
    back_t = lax.all_to_all(back_slots, "tm", split_axis=0, concat_axis=1, tiled=True)
    d_out = (cotan.astype(jnp.float32) + back_t.astype(jnp.float32)).astype(jnp.bfloat16)
    d_act = spatial_conv_t(d_out, spatial_weight)
    d_in = d_out.astype(jnp.float32) + act_back(d_act)[0]
    d_in = jnp.where(live_slots, d_in, 0.0).astype(jnp.bfloat16)
    height, width = (inputs.shape[1], inputs.shape[2])
    scale = 1.0 / math.sqrt(lax.axis_size("dp") * 2 * tm_size * height * width)
    summed = lax.psum(grad_part, ("dp", "tm"))
    return (d_in[None], summed * scale)


CAP = 3
SIDE = 8
CH = 320
PIX = SIDE * SIDE
ROWS = CAP * PIX
LANE = 128
UNITS = 8
BLOCK = 80
CHUNKS = 32
F32 = jnp.float32
BF16 = jnp.bfloat16


def dot(a, b, ca, cb):
    return lax.dot_general(a, b, (((ca,), (cb,)), ((), ())), preferred_element_type=F32)


def group_matrix():
    def ids(axis):
        index = lax.broadcasted_iota(jnp.int32, (CH, CH), axis).astype(F32)
        return jnp.floor((index + 0.5) * (GROUPS / CH))

    return (ids(0) == ids(1)).astype(BF16)


def group_means(totals, members):
    rows = jnp.concatenate(totals, axis=0)
    high = rows.astype(BF16)
    rest = rows - high.astype(F32)
    mid = rest.astype(BF16)
    low = (rest - mid.astype(F32)).astype(BF16)
    summed = dot(high, members, 1, 0) + dot(mid, members, 1, 0) + dot(low, members, 1, 0)
    return summed * (1.0 / (PIX * (CH // GROUPS)))


def frame_of(value, frame):
    return value[frame * PIX : (frame + 1) * PIX]


def column_sum(value):
    return jnp.sum(value, axis=0, keepdims=True)


def sigmoid(value):
    return 1.0 / (1.0 + jnp.exp(-value))


def stage_shifts(value, line, padded):
    column = lax.broadcasted_iota(jnp.int32, (ROWS, CH), 0) % SIDE
    line[8 : 8 + ROWS, :] = value
    left = jnp.where(column == 0, 0.0, line[7 : 7 + ROWS, :])
    right = jnp.where(column == SIDE - 1, 0.0, line[9 : 9 + ROWS, :])
    for j, moved in enumerate((left, value, right)):
        padded[j, :, 1 : 1 + SIDE] = moved.reshape(CAP, SIDE, SIDE, CH)


def turned_patches(value):
    wide = jnp.concatenate([value, jnp.zeros((64, CH), F32)], axis=0).T
    pixel = lax.broadcasted_iota(jnp.int32, wide.shape, 1)
    row, column = (pixel // SIDE) % SIDE, pixel % SIDE
    pieces = []
    for i in (-1, 0, 1):
        for j in (-1, 0, 1):
            move = (-(i * SIDE + j)) % wide.shape[1]
            moved = pltpu.roll(wide, move, 1) if move else wide
            inside = (row + i >= 0) & (row + i < SIDE) & (column + j >= 0) & (column + j < SIDE)
            pieces.append(jnp.where(inside, moved, 0.0).astype(BF16))
    return jnp.concatenate(pieces, axis=0)


def shifted(padded, j, i):
    return padded[j, :, i : i + SIDE].reshape(ROWS, CH).astype(BF16)


def fused_kernel(
    counts_hbm, x_hbm, g_hbm, gain_hbm, shift_hbm, ws_hbm, wt_hbm, out_ref, grad_ref,
    counts, x_ref, g_ref, gain_ref, shift_ref, ws, wt, line, padded, edge, halo, part, part16, from_core, quad16, from_plane, own, own16, from_z, full,
    weight_sem, halo_send, halo_recv, core_send, core_recv, plane_send, plane_recv, z_send, z_recv,
    gather_send, gather_z, gather_plane, gather_core,
):
    dp = lax.axis_index("dp")
    tm = lax.axis_index("tm")
    yy, xx, core = tm // 4, (tm // 2) % 2, tm % 2
    chip = tm // 2

    def at(z, chip_id, core_id):
        return (z, chip_id * 2 + core_id)

    plane = [yy * 2 + (1 - xx), (1 - yy) * 2 + xx, (1 - yy) * 2 + (1 - xx)]
    near = [dp + 1 - 2 * (dp % 2), 2 - dp // 2, 3 - 3 * (dp // 2)]
    far = near[::-1]
    before, after = lax.rem(tm + 7, 8), lax.rem(tm + 1, 8)
    partner = at(dp, chip, 1 - core)
    peers = [(dp, before), (dp, after)] + [at(dp, p, core) for p in plane] + [at(z, chip, core) for z in near]

    def remote(src, dst, send_sem, recv_sem, device):
        copy = pltpu.make_async_remote_copy(
            src_ref=src, dst_ref=dst, send_sem=send_sem, recv_sem=recv_sem,
            device_id=device, device_id_type=pl.DeviceIdType.MESH,
        )
        return copy

    barrier = pltpu.get_barrier_semaphore()
    for peer in peers:
        pl.semaphore_signal(barrier, inc=1, device_id=peer, device_id_type=pl.DeviceIdType.MESH)
    places = [
        (g_hbm, g_ref), (counts_hbm, counts), (x_hbm, x_ref), (gain_hbm, gain_ref), (shift_hbm, shift_ref),
        (ws_hbm, ws), (wt_hbm, wt),
    ]
    loads = [pltpu.make_async_copy(src, dst, weight_sem.at[i]) for i, (src, dst) in enumerate(places)]
    for load in loads:
        load.start()
    members = group_matrix()
    for load in loads[:2]:
        load.wait()

    count = counts[0, tm]
    g = g_ref[...].astype(F32)
    g_frames = [frame_of(g, s) for s in range(CAP)]
    last = jnp.where(count == 3, g_frames[2], jnp.where(count == 2, g_frames[1], g_frames[0]))
    edge[0] = g_frames[0].astype(BF16)
    edge[1] = last.astype(BF16)
    halo_copies = [
        remote(edge.at[0], halo.at[1], halo_send.at[0], halo_recv.at[1], (dp, before)),
        remote(edge.at[1], halo.at[0], halo_send.at[1], halo_recv.at[0], (dp, after)),
    ]
    for load in loads[2:5]:
        load.wait()

    gain, shift = gain_ref[...].reshape(1, CH), shift_ref[...].reshape(1, CH)
    x = x_ref[...].astype(F32)
    x_frames = [frame_of(x, s) for s in range(CAP)]
    means = group_means([column_sum(v) for v in x_frames], members)
    centred = [v - means[s : s + 1] for s, v in enumerate(x_frames)]
    spread = group_means([column_sum(v * v) for v in centred], members)
    inverse = lax.rsqrt(spread + 1e-05)
    xhat = jnp.concatenate([v * inverse[s : s + 1] for s, v in enumerate(centred)], axis=0)
    normed = xhat * gain + shift
    sig_n = sigmoid(normed)
    padded[...] = jnp.zeros_like(padded)
    pl.semaphore_wait(barrier, len(peers))
    for copy in halo_copies:
        copy.start()
    patched = turned_patches(normed * sig_n)
    loads[5].wait()
    mixed = dot(ws[...], patched, 1, 0).T[:ROWS]
    y = (x + mixed).astype(BF16).astype(F32)
    sig_y = sigmoid(y)
    slot = lax.broadcasted_iota(jnp.int32, (ROWS, CH), 0) // PIX
    live = slot < count
    u = jnp.where(live, y * sig_y, 0.0).astype(BF16)

    for copy in halo_copies:
        copy.wait()
    prev_edge = jnp.where(tm == 0, 0.0, halo[0].astype(F32))
    next_edge = jnp.where(tm == 7, 0.0, halo[1].astype(F32))
    g_ext = jnp.concatenate(
        [
            prev_edge,
            g_frames[0],
            jnp.where(count == 1, next_edge, g_frames[1]),
            jnp.where(count == 2, next_edge, g_frames[2]),
            next_edge,
        ],
        axis=0,
    )

    g_turned = g_ext.T.astype(BF16)
    g_ext = g_ext.astype(BF16)
    none = jnp.zeros((ROWS, 64), BF16)
    u_low = jnp.concatenate([u, none], axis=1)
    u_high = jnp.concatenate([none, u], axis=1)

    def below(value, frames):
        zero = jnp.zeros((PIX, value.shape[1]), BF16)
        return jnp.concatenate([zero] * frames + [value] + [zero] * (2 - frames), axis=0)

    t0 = dot(g_turned, below(u_low, 2), 1, 0)
    t1 = dot(g_turned, below(u_high, 1), 1, 0)
    t2 = dot(g_turned, below(u_low, 0), 1, 0)
    units = [
        t0[:, 0:128], t0[:, 128:256], t0[:, 256:384] + t1[:, 0:128], t1[:, 128:256], t1[:, 256:384],
        t2[:, 0:128], t2[:, 128:256], t2[:, 256:384],
    ]
    for r in range(4):
        for l in range(UNITS):
            piece = units[l][r * BLOCK : (r + 1) * BLOCK]
            part[r * UNITS + l] = piece
            part16[r * UNITS + l] = piece.astype(BF16)

    groups = plane + [chip]
    core_copies = [
        remote(
            part16.at[pl.ds((1 - core) * 16 + p * 4, 4)], from_core.at[pl.ds(p * 4, 4)],
            core_send.at[j], core_recv.at[j], partner,
        )
        for j, p in enumerate(groups)
    ]
    for copy in core_copies:
        copy.start()

    loads[6].wait()
    du = jnp.zeros((ROWS, CH), F32)
    for k in range(3):
        du = du + dot(g_ext[(2 - k) * PIX : (2 - k) * PIX + ROWS], wt[:, k * CH : (k + 1) * CH], 1, 0)
    back_t = (sig_y * (1.0 + y * (1.0 - sig_y)) * du).astype(BF16).astype(F32)
    dy = jnp.where(live, (g + back_t).astype(BF16).astype(F32), 0.0)

    z_order = far + [dp]
    for j, p in enumerate(groups):
        core_copies[j].wait()
        quad = part[pl.ds(core * 16 + p * 4, 4)] + from_core[pl.ds(p * 4, 4)].astype(F32)
        if j == 3:
            own[...] = quad
        else:
            quad16[j] = quad.astype(BF16)
    plane_copies = []
    for k, z in enumerate(z_order):
        for j, p in enumerate(plane):
            i = k * 3 + j
            copy = remote(quad16.at[j, z], from_plane.at[j, k], plane_send.at[i], plane_recv.at[i], at(dp, p, core))
            copy.start()
            plane_copies.append(copy)

    def summed_plane(k, z):
        for j in range(3):
            plane_copies[k * 3 + j].wait()
        return own[z] + from_plane[0, k].astype(F32) + from_plane[1, k].astype(F32) + from_plane[2, k].astype(F32)

    z_copies = []

    def pass_to_z(k):
        own16[k] = summed_plane(k, z_order[k]).astype(BF16)
        copy = remote(own16.at[k], from_z.at[dp], z_send.at[k], z_recv.at[dp], at(z_order[k], chip, core))
        copy.start()
        z_copies.append(copy)

    stage_shifts(dy, line, padded)
    da = jnp.zeros((ROWS, CH), F32)
    for tap in range(9):
        da = da + dot(shifted(padded, 2 - tap % 3, 2 - tap // 3), ws[:, tap * CH : (tap + 1) * CH], 1, 0)
        if tap in (4, 6, 8):
            pass_to_z(tap // 2 - 2)
    total = summed_plane(3, dp)

    dhat = da * (sig_n * (1.0 + normed * (1.0 - sig_n))) * gain
    dhat_frames = [frame_of(dhat, s) for s in range(CAP)]
    xhat_frames = [frame_of(xhat, s) for s in range(CAP)]
    mean_d = group_means([column_sum(v) for v in dhat_frames], members)
    mean_dx = group_means([column_sum(v * w) for v, w in zip(dhat_frames, xhat_frames)], members)
    dx = jnp.concatenate(
        [
            inverse[s : s + 1] * (dhat_frames[s] - mean_d[s : s + 1] - xhat_frames[s] * mean_dx[s : s + 1])
            for s in range(CAP)
        ],
        axis=0,
    )
    out_ref[...] = jnp.where(live, dy + dx, 0.0).astype(BF16)

    first = core * 16 + chip * 4
    mine = first + dp
    for z in near:
        remote(from_z.at[z], from_z.at[z], z_send.at[0], z_recv.at[z], partner).wait_recv()
        total = total + from_z[z].astype(F32)
    full[mine] = total.astype(BF16)

    sent = []

    def pass_on(chunk, device, recv_sem):
        copy = remote(full.at[chunk], full.at[chunk], gather_send.at[len(sent)], recv_sem, device)
        copy.start()
        sent.append(copy)

    def await_chunk(chunk, recv_sem):
        remote(full.at[chunk], full.at[chunk], gather_send.at[0], recv_sem, partner).wait_recv()

    for z in far:
        pass_on(mine, at(z, chip, core), gather_z.at[dp])
    for j, p in enumerate(plane):
        pass_on(mine, at(dp, p, core), gather_plane.at[dp * 3 + j])
    pass_on(mine, partner, gather_core.at[dp * 4 + 3])
    for z in near:
        await_chunk(first + z, gather_z.at[z])
        for j, p in enumerate(plane):
            pass_on(first + z, at(dp, p, core), gather_plane.at[z * 3 + j])
        pass_on(first + z, partner, gather_core.at[z * 4 + 3])
    for z in [dp] + near:
        for j, p in enumerate(plane):
            chunk = core * 16 + p * 4 + z
            await_chunk(chunk, gather_plane.at[z * 3 + j])
            pass_on(chunk, partner, gather_core.at[z * 4 + j])

    scale = 1.0 / math.sqrt(4 * 2 * 8 * PIX)

    def put(half):
        for r in range(2):
            rows = pl.ds(pl.multiple_of(half * 2 * BLOCK + r * BLOCK, 8), BLOCK)
            for l in range(UNITS):
                width = min(LANE, 3 * CH - l * LANE)
                value = full[half * 16 + r * UNITS + l].astype(F32) * scale
                grad_ref[rows, l * LANE : l * LANE + width] = value[:, :width]

    put(core)
    for z in [dp] + near:
        for j, p in enumerate(groups):
            await_chunk((1 - core) * 16 + p * 4 + z, gather_core.at[z * 4 + j])
    put(1 - core)
    for copy in z_copies + sent:
        copy.wait_send()


def place_kernel(out_from, grad_from, out_to, grad_to, sems):
    copies = [
        pltpu.make_async_copy(grad_from, grad_to, sems.at[0]),
        pltpu.make_async_copy(out_from, out_to, sems.at[1]),
    ]
    for copy in copies:
        copy.start()
    for copy in copies:
        copy.wait()


def fused_shards(frames_in, cotangent, counts, norm_gain, norm_shift, spatial_weight, temporal_weight):
    vmem = pl.BlockSpec(memory_space=pltpu.VMEM)
    hbm = pl.BlockSpec(memory_space=pltpu.HBM)
    dma = pltpu.SemaphoreType.DMA
    out, grad = pl.pallas_call(
        fused_kernel,
        out_shape=(
            pltpu.VMEM((ROWS, CH), BF16),
            pltpu.VMEM((CH, 3 * CH), F32),
        ),
        in_specs=[hbm] * 7,
        out_specs=(vmem, vmem),
        scratch_shapes=[
            pltpu.SMEM((1, 8), jnp.int32),
            pltpu.VMEM((ROWS, CH), BF16),
            pltpu.VMEM((ROWS, CH), BF16),
            pltpu.VMEM((CH,), F32),
            pltpu.VMEM((CH,), F32),
            pltpu.VMEM((CH, 9 * CH), BF16),
            pltpu.VMEM((CH, 3 * CH), BF16),
            pltpu.VMEM((ROWS + 16, CH), F32),
            pltpu.VMEM((3, CAP, SIDE + 2, SIDE, CH), F32),
            pltpu.VMEM((2, PIX, CH), BF16),
            pltpu.VMEM((2, PIX, CH), BF16),
            pltpu.VMEM((CHUNKS, BLOCK, LANE), F32),
            pltpu.VMEM((CHUNKS, BLOCK, LANE), BF16),
            pltpu.VMEM((16, BLOCK, LANE), BF16),
            pltpu.VMEM((3, 4, BLOCK, LANE), BF16),
            pltpu.VMEM((3, 4, BLOCK, LANE), BF16),
            pltpu.VMEM((4, BLOCK, LANE), F32),
            pltpu.VMEM((3, BLOCK, LANE), BF16),
            pltpu.VMEM((4, BLOCK, LANE), BF16),
            pltpu.VMEM((CHUNKS, BLOCK, LANE), BF16),
            dma((7,)), dma((2,)), dma((2,)), dma((4,)), dma((4,)), dma((12,)), dma((12,)), dma((3,)), dma((4,)),
            dma((31,)), dma((4,)), dma((12,)), dma((16,)),
        ],
        compiler_params=pltpu.CompilerParams(
            collective_id=0, has_side_effects=True, vmem_limit_bytes=60 * 1024 * 1024
        ),
    )(
        counts,
        frames_in.reshape(ROWS, CH),
        cotangent.reshape(ROWS, CH),
        norm_gain,
        norm_shift,
        spatial_weight.T,
        temporal_weight.T,
    )
    anywhere = pl.BlockSpec(memory_space=pl.ANY)
    out, grad = pl.pallas_call(
        place_kernel,
        out_shape=(jax.ShapeDtypeStruct(out.shape, BF16), jax.ShapeDtypeStruct(grad.shape, F32)),
        in_specs=[anywhere, anywhere],
        out_specs=(anywhere, anywhere),
        scratch_shapes=[dma((2,))],
    )(out, grad)
    return out.reshape(frames_in.shape), grad.T


def solution(mesh):
    fused = mesh.shape["dp"] == 4 and mesh.shape["tm"] == 8

    def block(frames_in, *rest):
        if fused and frames_in.shape == (1, CAP, SIDE, SIDE, CH):
            return fused_shards(frames_in, *rest)
        return shards(frames_in, *rest)

    return jax.shard_map(
        block,
        mesh=mesh,
        in_specs=(
            P("dp", "tm", None, None, None),
            P("dp", "tm", None, None, None),
            P("dp", None),
            P(),
            P(),
            P(),
            P(),
        ),
        out_specs=(P("dp", "tm", None, None, None), P()),
        check_vma=False,
    )
```

```python
import math

import jax
import jax.numpy as jnp
from jax import lax
from jax.experimental import pallas as pl
from jax.experimental.pallas import tpu as pltpu
from jax.sharding import PartitionSpec as P

GROUPS = 32


def norm_act(values, gain, shift, groups):
    nframes, height, width, channels = values.shape
    per_group = channels // groups
    entries = height * width * per_group

    def group_mean(totals):
        summed = totals.reshape(nframes, groups, per_group).sum(axis=2) / entries
        return jnp.repeat(summed, per_group, axis=1).reshape(nframes, 1, 1, channels)

    centre = group_mean(values.sum(axis=(1, 2)))
    centred = values - centre
    spread = group_mean((centred * centred).sum(axis=(1, 2)))
    normed = centred * lax.rsqrt(spread + 1e-05) * gain + shift
    return jax.nn.silu(normed)


def patches(field):
    height, width = (field.shape[1], field.shape[2])
    padded = jnp.pad(field, ((0, 0), (1, 1), (1, 1), (0, 0)))
    pieces = [
        padded[:, row_off : row_off + height, col_off : col_off + width, :]
        for row_off in range(3)
        for col_off in range(3)
    ]
    return jnp.concatenate(pieces, axis=3)


def spatial_conv(field, weight):
    stacked = patches(field)
    leading = stacked.shape[:3]
    product = jnp.dot(
        stacked.reshape(-1, stacked.shape[3]), weight, preferred_element_type=jnp.float32
    )
    return product.reshape(leading + (weight.shape[1],))


def spatial_conv_t(field, weight):
    channels = weight.shape[1]
    flipped = (
        weight.reshape(9, -1, channels)[::-1].transpose(0, 2, 1).reshape(-1, weight.shape[0] // 9)
    )
    return spatial_conv(field, flipped)


def silu_grad(values):
    sigma = jax.nn.sigmoid(values)
    return sigma * (1.0 + values * (1.0 - sigma))


def temporal_core(y_ext, g_ext, weight):
    nframes = y_ext.shape[0] - 2
    channels = weight.shape[1]
    units = jax.nn.silu(y_ext.astype(jnp.float32)).astype(jnp.bfloat16)
    g_middle = g_ext[1:-1]
    g_mid = g_middle.reshape(-1, channels)
    grads = []
    back_sum = jnp.zeros((g_mid.shape[0], channels), jnp.float32)
    for tap_k in range(3):
        taken = units[tap_k : tap_k + nframes].reshape(-1, channels)
        grads.append(
            lax.dot_general(
                taken, g_mid, (((0,), (0,)), ((), ())), preferred_element_type=jnp.float32
            )
        )
        tap_weight = weight[tap_k * channels : (tap_k + 1) * channels]
        source = g_ext[2 - tap_k : 2 - tap_k + nframes].reshape(-1, channels)
        back_sum = back_sum + lax.dot_general(
            source, tap_weight, (((1,), (1,)), ((), ())), preferred_element_type=jnp.float32
        )
    middle = y_ext[1:-1]
    back_t = (silu_grad(middle.astype(jnp.float32)) * back_sum.reshape(middle.shape)).astype(
        jnp.bfloat16
    )
    return (back_t, jnp.concatenate(grads, axis=0))


def frame_slots(counts_row, nframes, cap):
    ndevices = counts_row.shape[0]
    ends = jnp.cumsum(counts_row)
    starts = ends - counts_row
    frame_ids = jnp.arange(nframes, dtype=jnp.int32)
    owner = jnp.sum((ends[None, :] <= frame_ids[:, None]).astype(jnp.int32), axis=1)
    device_ids = jnp.arange(ndevices, dtype=jnp.int32)
    first = jnp.sum(jnp.where(device_ids[None, :] == owner[:, None], starts[None, :], 0), axis=1)
    return owner * cap + frame_ids - first


def slot_frames(counts_row, cap):
    ndevices = counts_row.shape[0]
    ends = jnp.cumsum(counts_row)
    starts = ends - counts_row
    slot_ids = jnp.arange(ndevices * cap, dtype=jnp.int32)
    device = slot_ids // cap
    inner = slot_ids % cap
    device_ids = jnp.arange(ndevices, dtype=jnp.int32)
    onehot = device[:, None] == device_ids[None, :]
    held = jnp.sum(jnp.where(onehot, counts_row[None, :], 0), axis=1)
    first = jnp.sum(jnp.where(onehot, starts[None, :], 0), axis=1)
    live = inner < held
    return (jnp.where(live, first + inner, 0), live)


def shards(frames_in, cotangent, counts, norm_gain, norm_shift, spatial_weight, temporal_weight):
    inputs = frames_in[0]
    cotan = cotangent[0]
    counts_row = counts[0]
    cap = inputs.shape[0]
    tm_size = lax.axis_size("tm")
    own_count = jnp.sum(
        jnp.where(jnp.arange(tm_size, dtype=jnp.int32) == lax.axis_index("tm"), counts_row, 0)
    )
    live_slots = (jnp.arange(cap, dtype=jnp.int32) < own_count)[:, None, None, None]

    def activate(values):
        return norm_act(values, norm_gain, norm_shift, GROUPS)

    inputs_f = inputs.astype(jnp.float32)
    act_f, act_back = jax.vjp(activate, inputs_f)
    acts = act_f.astype(jnp.bfloat16)
    mixed = spatial_conv(acts, spatial_weight)
    y_out = (inputs_f + mixed).astype(jnp.bfloat16)
    y_rows, g_rows = (
        lax.all_to_all(y_out, "tm", split_axis=1, concat_axis=0, tiled=True),
        lax.all_to_all(cotan, "tm", split_axis=1, concat_axis=0, tiled=True),
    )
    pick = frame_slots(counts_row, 2 * tm_size, cap)
    pad_spec = ((1, 1), (0, 0), (0, 0), (0, 0))
    y_ext = jnp.pad(jnp.take(y_rows, pick, axis=0), pad_spec)
    g_ext = jnp.pad(jnp.take(g_rows, pick, axis=0), pad_spec)
    back_rows, grad_part = temporal_core(y_ext, g_ext, temporal_weight)
    back_idx, live = slot_frames(counts_row, cap)
    back_slots = jnp.where(
        live[:, None, None, None],
        jnp.take(back_rows, back_idx, axis=0),
        jnp.zeros((), jnp.bfloat16),
    )
    back_t = lax.all_to_all(back_slots, "tm", split_axis=0, concat_axis=1, tiled=True)
    d_out = (cotan.astype(jnp.float32) + back_t.astype(jnp.float32)).astype(jnp.bfloat16)
    d_act = spatial_conv_t(d_out, spatial_weight)
    d_in = d_out.astype(jnp.float32) + act_back(d_act)[0]
    d_in = jnp.where(live_slots, d_in, 0.0).astype(jnp.bfloat16)
    height, width = (inputs.shape[1], inputs.shape[2])
    scale = 1.0 / math.sqrt(lax.axis_size("dp") * 2 * tm_size * height * width)
    summed = lax.psum(grad_part, ("dp", "tm"))
    return (d_in[None], summed * scale)


CAP = 3
SIDE = 8
CH = 320
PIX = SIDE * SIDE
ROWS = CAP * PIX
LANE = 128
UNITS = 8
BLOCK = 80
CHUNKS = 32
F32 = jnp.float32
BF16 = jnp.bfloat16


def dot(a, b, ca, cb):
    return lax.dot_general(a, b, (((ca,), (cb,)), ((), ())), preferred_element_type=F32)


def group_matrix():
    def ids(axis):
        index = lax.broadcasted_iota(jnp.int32, (CH, CH), axis).astype(F32)
        return jnp.floor((index + 0.5) * (GROUPS / CH))

    return (ids(0) == ids(1)).astype(BF16)


def group_means(totals, members):
    rows = jnp.concatenate(totals, axis=0)
    high = rows.astype(BF16)
    rest = rows - high.astype(F32)
    mid = rest.astype(BF16)
    low = (rest - mid.astype(F32)).astype(BF16)
    summed = dot(high, members, 1, 0) + dot(mid, members, 1, 0) + dot(low, members, 1, 0)
    return summed * (1.0 / (PIX * (CH // GROUPS)))


def frame_of(value, frame):
    return value[frame * PIX : (frame + 1) * PIX]


def column_sum(value):
    return jnp.sum(value, axis=0, keepdims=True)


def sigmoid(value):
    return 1.0 / (1.0 + jnp.exp(-value))


def stage_shifts(value, line, padded):
    column = lax.broadcasted_iota(jnp.int32, (ROWS, CH), 0) % SIDE
    line[8 : 8 + ROWS, :] = value
    left = jnp.where(column == 0, 0.0, line[7 : 7 + ROWS, :])
    right = jnp.where(column == SIDE - 1, 0.0, line[9 : 9 + ROWS, :])
    for j, moved in enumerate((left, value, right)):
        padded[j, :, 1 : 1 + SIDE] = moved.reshape(CAP, SIDE, SIDE, CH)


def turned_patches(value):
    wide = jnp.concatenate([value, jnp.zeros((64, CH), F32)], axis=0).T
    pixel = lax.broadcasted_iota(jnp.int32, wide.shape, 1)
    row, column = (pixel // SIDE) % SIDE, pixel % SIDE
    pieces = []
    for i in (-1, 0, 1):
        for j in (-1, 0, 1):
            move = (-(i * SIDE + j)) % wide.shape[1]
            moved = pltpu.roll(wide, move, 1) if move else wide
            inside = (row + i >= 0) & (row + i < SIDE) & (column + j >= 0) & (column + j < SIDE)
            pieces.append(jnp.where(inside, moved, 0.0).astype(BF16))
    return jnp.concatenate(pieces, axis=0)


def shifted(padded, j, i):
    return padded[j, :, i : i + SIDE].reshape(ROWS, CH).astype(BF16)


def fused_kernel(
    counts_hbm, x_hbm, g_hbm, gain_hbm, shift_hbm, ws_hbm, wt_hbm, out_ref, grad_ref,
    counts, x_ref, g_ref, gain_ref, shift_ref, ws, wt, line, padded, edge, halo, part, part16, from_core, quad16, from_plane, own, own16, from_z, full,
    weight_sem, halo_send, halo_recv, core_send, core_recv, plane_send, plane_recv, z_send, z_recv,
    gather_send, gather_z, gather_plane, gather_core,
):
    dp = lax.axis_index("dp")
    tm = lax.axis_index("tm")
    yy, xx, core = tm // 4, (tm // 2) % 2, tm % 2
    chip = tm // 2

    def at(z, chip_id, core_id):
        return (z, chip_id * 2 + core_id)

    plane = [yy * 2 + (1 - xx), (1 - yy) * 2 + xx, (1 - yy) * 2 + (1 - xx)]
    near = [dp + 1 - 2 * (dp % 2), 2 - dp // 2, 3 - 3 * (dp // 2)]
    far = near[::-1]
    before, after = lax.rem(tm + 7, 8), lax.rem(tm + 1, 8)
    partner = at(dp, chip, 1 - core)
    peers = [(dp, before), (dp, after)] + [at(dp, p, core) for p in plane] + [at(z, chip, core) for z in near]

    def remote(src, dst, send_sem, recv_sem, device):
        copy = pltpu.make_async_remote_copy(
            src_ref=src, dst_ref=dst, send_sem=send_sem, recv_sem=recv_sem,
            device_id=device, device_id_type=pl.DeviceIdType.MESH,
        )
        return copy

    barrier = pltpu.get_barrier_semaphore()
    for peer in peers:
        pl.semaphore_signal(barrier, inc=1, device_id=peer, device_id_type=pl.DeviceIdType.MESH)
    places = [
        (g_hbm, g_ref), (counts_hbm, counts), (x_hbm, x_ref), (gain_hbm, gain_ref), (shift_hbm, shift_ref),
        (ws_hbm, ws), (wt_hbm, wt),
    ]
    loads = [pltpu.make_async_copy(src, dst, weight_sem.at[i]) for i, (src, dst) in enumerate(places)]
    for load in loads:
        load.start()
    members = group_matrix()
    for load in loads[:2]:
        load.wait()

    count = counts[0, tm]
    g = g_ref[...].astype(F32)
    g_frames = [frame_of(g, s) for s in range(CAP)]
    last = jnp.where(count == 3, g_frames[2], jnp.where(count == 2, g_frames[1], g_frames[0]))
    edge[0] = g_frames[0].astype(BF16)
    edge[1] = last.astype(BF16)
    halo_copies = [
        remote(edge.at[0], halo.at[1], halo_send.at[0], halo_recv.at[1], (dp, before)),
        remote(edge.at[1], halo.at[0], halo_send.at[1], halo_recv.at[0], (dp, after)),
    ]
    for load in loads[2:5]:
        load.wait()

    gain, shift = gain_ref[...].reshape(1, CH), shift_ref[...].reshape(1, CH)
    x = x_ref[...].astype(F32)
    x_frames = [frame_of(x, s) for s in range(CAP)]
    means = group_means([column_sum(v) for v in x_frames], members)
    centred = [v - means[s : s + 1] for s, v in enumerate(x_frames)]
    spread = group_means([column_sum(v * v) for v in centred], members)
    inverse = lax.rsqrt(spread + 1e-05)
    xhat = jnp.concatenate([v * inverse[s : s + 1] for s, v in enumerate(centred)], axis=0)
    normed = xhat * gain + shift
    sig_n = sigmoid(normed)
    padded[...] = jnp.zeros_like(padded)
    pl.semaphore_wait(barrier, len(peers))
    for copy in halo_copies:
        copy.start()
    patched = turned_patches(normed * sig_n)
    loads[5].wait()
    mixed = dot(ws[...], patched, 1, 0).T[:ROWS]
    y = (x + mixed).astype(BF16).astype(F32)
    sig_y = sigmoid(y)
    slot = lax.broadcasted_iota(jnp.int32, (ROWS, CH), 0) // PIX
    live = slot < count
    u = jnp.where(live, y * sig_y, 0.0).astype(BF16)

    for copy in halo_copies:
        copy.wait()
    prev_edge = jnp.where(tm == 0, 0.0, halo[0].astype(F32))
    next_edge = jnp.where(tm == 7, 0.0, halo[1].astype(F32))
    g_ext = jnp.concatenate(
        [
            prev_edge,
            g_frames[0],
            jnp.where(count == 1, next_edge, g_frames[1]),
            jnp.where(count == 2, next_edge, g_frames[2]),
            next_edge,
        ],
        axis=0,
    )

    g_turned = g_ext.T.astype(BF16)
    g_ext = g_ext.astype(BF16)
    none = jnp.zeros((ROWS, 64), BF16)
    u_low = jnp.concatenate([u, none], axis=1)
    u_high = jnp.concatenate([none, u], axis=1)

    def below(value, frames):
        zero = jnp.zeros((PIX, value.shape[1]), BF16)
        return jnp.concatenate([zero] * frames + [value] + [zero] * (2 - frames), axis=0)

    t0 = dot(g_turned, below(u_low, 2), 1, 0)
    t1 = dot(g_turned, below(u_high, 1), 1, 0)
    t2 = dot(g_turned, below(u_low, 0), 1, 0)
    units = [
        t0[:, 0:128], t0[:, 128:256], t0[:, 256:384] + t1[:, 0:128], t1[:, 128:256], t1[:, 256:384],
        t2[:, 0:128], t2[:, 128:256], t2[:, 256:384],
    ]
    for r in range(4):
        for l in range(UNITS):
            piece = units[l][r * BLOCK : (r + 1) * BLOCK]
            part[r * UNITS + l] = piece
            part16[r * UNITS + l] = piece.astype(BF16)

    groups = plane + [chip]
    core_copies = [
        remote(
            part16.at[pl.ds((1 - core) * 16 + p * 4, 4)], from_core.at[pl.ds(p * 4, 4)],
            core_send.at[j], core_recv.at[j], partner,
        )
        for j, p in enumerate(groups)
    ]
    for copy in core_copies:
        copy.start()

    loads[6].wait()
    du = jnp.zeros((ROWS, CH), F32)
    for k in range(3):
        du = du + dot(g_ext[(2 - k) * PIX : (2 - k) * PIX + ROWS], wt[:, k * CH : (k + 1) * CH], 1, 0)
    back_t = (sig_y * (1.0 + y * (1.0 - sig_y)) * du).astype(BF16).astype(F32)
    dy = jnp.where(live, (g + back_t).astype(BF16).astype(F32), 0.0)

    z_order = far + [dp]
    for j, p in enumerate(groups):
        core_copies[j].wait()
        quad = part[pl.ds(core * 16 + p * 4, 4)] + from_core[pl.ds(p * 4, 4)].astype(F32)
        if j == 3:
            own[...] = quad
        else:
            quad16[j] = quad.astype(BF16)
    plane_copies = []
    for k, z in enumerate(z_order):
        for j, p in enumerate(plane):
            i = k * 3 + j
            copy = remote(quad16.at[j, z], from_plane.at[j, k], plane_send.at[i], plane_recv.at[i], at(dp, p, core))
            copy.start()
            plane_copies.append(copy)

    def summed_plane(k, z):
        for j in range(3):
            plane_copies[k * 3 + j].wait()
        return own[z] + from_plane[0, k].astype(F32) + from_plane[1, k].astype(F32) + from_plane[2, k].astype(F32)

    z_copies = []

    def pass_to_z(k):
        own16[k] = summed_plane(k, z_order[k]).astype(BF16)
        copy = remote(own16.at[k], from_z.at[dp], z_send.at[k], z_recv.at[dp], at(z_order[k], chip, core))
        copy.start()
        z_copies.append(copy)

    stage_shifts(dy, line, padded)
    da = jnp.zeros((ROWS, CH), F32)
    for tap in range(9):
        da = da + dot(shifted(padded, 2 - tap % 3, 2 - tap // 3), ws[:, tap * CH : (tap + 1) * CH], 1, 0)
        if tap in (4, 6, 8):
            pass_to_z(tap // 2 - 2)
    total = summed_plane(3, dp)

    dhat = da * (sig_n * (1.0 + normed * (1.0 - sig_n))) * gain
    dhat_frames = [frame_of(dhat, s) for s in range(CAP)]
    xhat_frames = [frame_of(xhat, s) for s in range(CAP)]
    mean_d = group_means([column_sum(v) for v in dhat_frames], members)
    mean_dx = group_means([column_sum(v * w) for v, w in zip(dhat_frames, xhat_frames)], members)
    dx = jnp.concatenate(
        [
            inverse[s : s + 1] * (dhat_frames[s] - mean_d[s : s + 1] - xhat_frames[s] * mean_dx[s : s + 1])
            for s in range(CAP)
        ],
        axis=0,
    )
    out_ref[...] = jnp.where(live, dy + dx, 0.0).astype(BF16)

    first = core * 16 + chip * 4
    mine = first + dp
    for z in near:
        remote(from_z.at[z], from_z.at[z], z_send.at[0], z_recv.at[z], partner).wait_recv()
        total = total + from_z[z].astype(F32)
    full[mine] = total.astype(BF16)

    sent = []

    def pass_on(chunk, device, recv_sem):
        copy = remote(full.at[chunk], full.at[chunk], gather_send.at[len(sent)], recv_sem, device)
        copy.start()
        sent.append(copy)

    def await_chunk(chunk, recv_sem):
        remote(full.at[chunk], full.at[chunk], gather_send.at[0], recv_sem, partner).wait_recv()

    for z in far:
        pass_on(mine, at(z, chip, core), gather_z.at[dp])
    for j, p in enumerate(plane):
        pass_on(mine, at(dp, p, core), gather_plane.at[dp * 3 + j])
    pass_on(mine, partner, gather_core.at[dp * 4 + 3])
    for z in near:
        await_chunk(first + z, gather_z.at[z])
        for j, p in enumerate(plane):
            pass_on(first + z, at(dp, p, core), gather_plane.at[z * 3 + j])
        pass_on(first + z, partner, gather_core.at[z * 4 + 3])
    for z in [dp] + near:
        for j, p in enumerate(plane):
            chunk = core * 16 + p * 4 + z
            await_chunk(chunk, gather_plane.at[z * 3 + j])
            pass_on(chunk, partner, gather_core.at[z * 4 + j])

    scale = 1.0 / math.sqrt(4 * 2 * 8 * PIX)

    def put(half):
        for r in range(2):
            rows = pl.ds(pl.multiple_of(half * 2 * BLOCK + r * BLOCK, 8), BLOCK)
            for l in range(UNITS):
                width = min(LANE, 3 * CH - l * LANE)
                value = full[half * 16 + r * UNITS + l].astype(F32) * scale
                grad_ref[rows, l * LANE : l * LANE + width] = value[:, :width]

    put(core)
    for z in [dp] + near:
        for j, p in enumerate(groups):
            await_chunk((1 - core) * 16 + p * 4 + z, gather_core.at[z * 4 + j])
    put(1 - core)
    for copy in z_copies + sent:
        copy.wait_send()


def place_kernel(out_from, grad_from, out_to, grad_to, sems):
    copies = [
        pltpu.make_async_copy(grad_from, grad_to, sems.at[0]),
        pltpu.make_async_copy(out_from, out_to, sems.at[1]),
    ]
    for copy in copies:
        copy.start()
    for copy in copies:
        copy.wait()


def fused_shards(frames_in, cotangent, counts, norm_gain, norm_shift, spatial_weight, temporal_weight):
    vmem = pl.BlockSpec(memory_space=pltpu.VMEM)
    hbm = pl.BlockSpec(memory_space=pltpu.HBM)
    dma = pltpu.SemaphoreType.DMA
    out, grad = pl.pallas_call(
        fused_kernel,
        out_shape=(
            pltpu.VMEM((ROWS, CH), BF16),
            pltpu.VMEM((CH, 3 * CH), F32),
        ),
        in_specs=[hbm] * 7,
        out_specs=(vmem, vmem),
        scratch_shapes=[
            pltpu.SMEM((1, 8), jnp.int32),
            pltpu.VMEM((ROWS, CH), BF16),
            pltpu.VMEM((ROWS, CH), BF16),
            pltpu.VMEM((CH,), F32),
            pltpu.VMEM((CH,), F32),
            pltpu.VMEM((CH, 9 * CH), BF16),
            pltpu.VMEM((CH, 3 * CH), BF16),
            pltpu.VMEM((ROWS + 16, CH), F32),
            pltpu.VMEM((3, CAP, SIDE + 2, SIDE, CH), F32),
            pltpu.VMEM((2, PIX, CH), BF16),
            pltpu.VMEM((2, PIX, CH), BF16),
            pltpu.VMEM((CHUNKS, BLOCK, LANE), F32),
            pltpu.VMEM((CHUNKS, BLOCK, LANE), BF16),
            pltpu.VMEM((16, BLOCK, LANE), BF16),
            pltpu.VMEM((3, 4, BLOCK, LANE), BF16),
            pltpu.VMEM((3, 4, BLOCK, LANE), BF16),
            pltpu.VMEM((4, BLOCK, LANE), F32),
            pltpu.VMEM((3, BLOCK, LANE), BF16),
            pltpu.VMEM((4, BLOCK, LANE), BF16),
            pltpu.VMEM((CHUNKS, BLOCK, LANE), BF16),
            dma((7,)), dma((2,)), dma((2,)), dma((4,)), dma((4,)), dma((12,)), dma((12,)), dma((3,)), dma((4,)),
            dma((31,)), dma((4,)), dma((12,)), dma((16,)),
        ],
        compiler_params=pltpu.CompilerParams(
            collective_id=0, has_side_effects=True, vmem_limit_bytes=60 * 1024 * 1024
        ),
    )(
        counts,
        frames_in.reshape(ROWS, CH),
        cotangent.reshape(ROWS, CH),
        norm_gain,
        norm_shift,
        spatial_weight.T,
        temporal_weight.T,
    )
    anywhere = pl.BlockSpec(memory_space=pl.ANY)
    out, grad = pl.pallas_call(
        place_kernel,
        out_shape=(jax.ShapeDtypeStruct(out.shape, BF16), jax.ShapeDtypeStruct(grad.shape, F32)),
        in_specs=[vmem, vmem],
        out_specs=(anywhere, anywhere),
        scratch_shapes=[dma((2,))],
        compiler_params=pltpu.CompilerParams(vmem_limit_bytes=4 * 1024 * 1024),
    )(out, grad)
    return out.reshape(frames_in.shape), grad.T


def solution(mesh):
    fused = mesh.shape["dp"] == 4 and mesh.shape["tm"] == 8

    def block(frames_in, *rest):
        if fused and frames_in.shape == (1, CAP, SIDE, SIDE, CH):
            return fused_shards(frames_in, *rest)
        return shards(frames_in, *rest)

    return jax.shard_map(
        block,
        mesh=mesh,
        in_specs=(
            P("dp", "tm", None, None, None),
            P("dp", "tm", None, None, None),
            P("dp", None),
            P(),
            P(),
            P(),
            P(),
        ),
        out_specs=(P("dp", "tm", None, None, None), P()),
        check_vma=False,
    )
```
